128 devices in a mesh: dp: 8 (over z, core), cent: 16 (over y, x).
Axes of the slice: x: 4, y: 4, z: 4, core: 2. Of those that a mesh axis runs over, the one named last changes fastest.
Arguments:
- vectors: bfloat16 [131072, 768], P(('dp', 'cent')), may hold values from -110 to 110
- centroids: bfloat16 [32768, 768], P('cent'), may hold values from -0.29882812 to 0.29882812
- candidates: int32 [131072, 4], P(('dp', 'cent')), may hold values from 0 to 63, all different within a row; in each aligned block of 1024 rows (0 to 1023, 1024 to 2047, ...) at most 96 rows name the same one
Outputs:
- updated: bfloat16 [32768, 768], P('cent')
The draws below stay inside these ranges and needn't reach their ends.
Inputs may be any that keep to these rules, and one draw needn't show every extreme that they name: `candidates`: each row names four different blocks; among the 1024 rows of one device no block is named more than 96 times, and some block exactly 96 times.
All inputs are finite; a program needn't handle non-finite values.
Results may differ from the reference program's by a relative error of at most 0.02.
Values may be sent and summed in bfloat16 or wider, within the bound.
No kernel may reach another device: no remote copies, remote signals or barrier semaphores. Data moves between devices by JAX's collectives and lax.ppermute only.
A program may use at most 128 MiB of HBM per device.

```python
import math
import jax
import jax.numpy as jnp
import numpy as np
from jax import lax

D = 768
BS = 512
TOK = 1024
NB = 64
MOST = 96
K = 32768
VECTORS = 131072
N_DP = 8
N_CENT = 16
DEVICES = 128


def draw_vectors(key, part):
    key = jax.random.fold_in(key, 11)
    return jnp.clip(jax.random.normal(key, (VECTORS, D), jnp.float32), -4.0, 4.0).astype(jnp.bfloat16)


def level_of(stream_key, shape, shards, least, top_value):
    level = 1.0
    for dim, blocks in shards:
        draws = jax.random.uniform(jax.random.fold_in(jax.random.fold_in(stream_key, 6), dim), (blocks,), jnp.float32, least / len(shards), top_value / len(shards))
        level = level * jnp.repeat(jnp.exp(draws), shape[dim] // blocks).reshape((-1,) + (1,) * (len(shape) - 1 - dim))
    return level


def shared_out(stream_key, own, number, rows, number_of, top, bound, slope):
    ranking = jax.random.permutation(stream_key, number_of)
    crowded, common = load_shares(number_of, rows * top, bound, slope, True), load_shares(number_of, rows * top, bound, slope, False)
    places = jnp.arange(number_of)

    def named(tallies, turn):
        used = int((tallies > 0).sum())
        fixed = max(1, used // 4)
        shifted = fixed + (places - fixed + turn * (used - fixed)) % max(1, number_of - fixed)
        return jnp.zeros((number_of,), jnp.int32).at[ranking[jnp.where(places < fixed, places, shifted)]].set(jnp.asarray(tallies, jnp.int32))

    tallies = jnp.where(number % 4 == 0, named(crowded, number // 4), named(common, number - number // 4 - 1))
    mixed = jax.random.permutation(jax.random.fold_in(own, 3), number_of)
    giver, taker = mixed[0:number_of // 2 * 2:2], mixed[1:number_of // 2 * 2:2]
    room = jnp.minimum(tallies[giver] - 1, bound - tallies[taker]) // 2
    room = jnp.where((giver == ranking[0]) | (taker == ranking[0]) | (tallies[taker] == 0), 0, jnp.maximum(room, 0))
    shifted = jax.random.randint(jax.random.fold_in(own, 4), (number_of // 2,), 0, 1 << 20) % (room + 1)
    tallies = tallies.at[giver].add(-shifted).at[taker].add(shifted)
    members = jnp.searchsorted(jnp.cumsum(tallies), jnp.arange(rows * top), side="right").astype(jnp.int32)
    listing = members.reshape(top, rows).T
    listing = listing[jax.random.permutation(jax.random.fold_in(own, 1), rows)]
    turn = jax.random.randint(jax.random.fold_in(own, 2), (rows, 1), 0, top)
    return jnp.take_along_axis(listing, (jnp.arange(top)[None, :] + turn) % top, axis=1)


def load_shares(amount, total, bound, slope, full):
    loads = [(1 << 20) // math.isqrt(rank ** slope) + 1 for rank in range(1, amount + 1)]
    largest = bound if full else min(bound, max(-(-total // amount), total * loads[0] // sum(loads)))
    least = 1 if total - largest >= amount - 1 else 0
    holding, surplus = [largest] + [least] * (amount - 1), total - largest - least * (amount - 1)
    while surplus > 0:
        movable = [i for i in range(1, amount) if holding[i] < largest] or [i for i in range(1, amount) if holding[i] < bound]
        pool, remaining = sum([loads[i] for i in movable]), surplus
        for i in movable:
            extra = min(bound - holding[i], max(1, remaining * loads[i] // pool), surplus)
            holding[i] = holding[i] + extra
            surplus = surplus - extra
    return np.array(holding)


def noise(own_key, dims, width, reach, shards=(), kind=jnp.bfloat16):
    values = width * jax.random.normal(own_key, dims, jnp.float32)
    if shards:
        values = values * level_of(own_key, dims, shards, -0.22, 0.18)
    return jnp.clip(values, -reach, reach).astype(kind)


def setup_inputs(seed: int = 0) -> dict:
    keys = jax.random.split(jax.random.key(seed), 4)
    vectors = draw_vectors(jax.random.fold_in(keys[3], 71), 0)
    centroids = noise(keys[1], (K, D), 0.05, 0.29882812, ((0, 16),))
    candidates_keys = jax.random.split(jax.random.fold_in(keys[2], 1), VECTORS // TOK)
    candidates_turns = jax.random.permutation(jax.random.fold_in(keys[2], 3), VECTORS // TOK)
    candidates = jax.vmap(lambda own, number: shared_out(jax.random.fold_in(keys[2], 2), own, number, TOK, NB, 4, MOST, 2))(candidates_keys, candidates_turns).reshape((VECTORS, 4))
    return {"vectors": vectors, "centroids": centroids, "candidates": candidates}


def pairwise_table(candidates):
    centroid_blocks = candidates.reshape(DEVICES, TOK * 4).astype(jnp.int32)
    onehot = (centroid_blocks[:, :, None] == jnp.arange(NB, dtype=jnp.int32)[None, None, :]).astype(jnp.int32)
    rank = jnp.sum((jnp.cumsum(onehot, axis=1) - onehot) * onehot, axis=2).astype(jnp.int32)
    device = jnp.arange(DEVICES, dtype=jnp.int32)[:, None]
    column_index = (device * MOST + rank).astype(jnp.int32)
    owner = (jnp.arange(VECTORS, dtype=jnp.int32) // 1).reshape(DEVICES, TOK)
    owner = jnp.repeat(owner, 4, axis=1).astype(jnp.int32)
    table = jnp.full((NB, DEVICES * MOST), VECTORS, jnp.int32).at[centroid_blocks, column_index].set(owner)
    return table, centroid_blocks, column_index


def reference(vectors, centroids, candidates):
    table, centroid_blocks, column_index = pairwise_table(candidates)
    padded = jnp.concatenate([vectors, jnp.zeros((1, D), jnp.bfloat16)], axis=0)
    candidate_blocks = centroids.reshape(NB, BS, D)
    squares = jnp.sum(centroids.astype(jnp.float32) ** 2, axis=1).reshape(NB, BS)

    def block_scores(index):
        rows = padded[table[index]]
        return jnp.dot(rows, candidate_blocks[index].T, preferred_element_type=jnp.float32) - 0.5 * squares[index][None, :]

    def block_stats(index):
        scores = block_scores(index)
        peak = jnp.max(scores, axis=1)
        total = jnp.sum(jnp.exp(scores - peak[:, None]), axis=1)
        return peak, total

    peaks, totals = lax.map(block_stats, jnp.arange(NB, dtype=jnp.int32))
    pair_peak = peaks[centroid_blocks, column_index].reshape(VECTORS, 4)
    pair_total = totals[centroid_blocks, column_index].reshape(VECTORS, 4)
    top = jnp.max(pair_peak, axis=1)
    lse = top + jnp.log(jnp.sum(pair_total * jnp.exp(pair_peak - top[:, None]), axis=1))
    lse_pairs = jnp.repeat(lse, 4).reshape(DEVICES, TOK * 4)
    lse_table = jnp.full((NB, DEVICES * MOST), 1e30, jnp.float32).at[centroid_blocks, column_index].set(lse_pairs)

    def block_refresh(index):
        scores = block_scores(index)
        weight = jnp.exp(scores - lse_table[index][:, None])
        block_weight = weight.astype(jnp.bfloat16)
        rows = padded[table[index]]
        grouped_rows = rows.reshape(N_DP, N_CENT * MOST, D).astype(jnp.float32)
        grouped_w = block_weight.reshape(N_DP, N_CENT * MOST, BS).astype(jnp.float32)
        partial_value = jnp.einsum('gsk,gsd->gkd', grouped_w, grouped_rows)
        counted = jnp.sum(weight.reshape(N_DP, N_CENT * MOST, BS), axis=1)
        partial_value = lax.optimization_barrier(partial_value.astype(jnp.bfloat16)).astype(jnp.float32)
        counted = lax.optimization_barrier(counted.astype(jnp.bfloat16)).astype(jnp.float32)
        sums = jnp.sum(partial_value, axis=0)
        counts = jnp.sum(counted, axis=0)
        fresh = (sums + candidate_blocks[index].astype(jnp.float32)) / (counts + 1.0)[:, None]
        return fresh.astype(jnp.bfloat16)

    updated = lax.map(block_refresh, jnp.arange(NB, dtype=jnp.int32))
    return updated.reshape(K, D)
```

```python
import jax
import jax.numpy as jnp
import numpy as np
from jax import lax
from jax.experimental import pallas as pl
from jax.experimental.pallas import tpu as pltpu
from jax.sharding import Mesh, PartitionSpec as P

BS = 512
MOST = 96
TOK = 1024
D = 768
NSRC = 8
NBLK = 8
SLOTS = NSRC * MOST
LOW = -1e30
F32 = jnp.float32
BF16 = jnp.bfloat16
VMEM = 56 * 1024 * 1024

FROM_D = (4, 3, 0, 7, 6, 1, 2, 5)
FROM_E = (2, 5, 6, 1, 0, 7, 4, 3)
FROM_F = (6, 7, 4, 5, 2, 3, 0, 1)


def turn(a, axis, sign):
    axes = ("z", "core") if axis == "z" else ("core", axis)
    at = (lambda core, i: i * 2 + core) if axis == "z" else (lambda core, i: core * 4 + i)
    pairs = []
    for core in range(2):
        for i in range(4):
            pairs.append((at(core, i), at(core, (i + (sign if core == 0 else -sign)) % 4)))
    return lax.ppermute(a, axes, pairs)


def far(a, axis):
    return lax.ppermute(a, axis, [(i, (i + 2) % 4) for i in range(4)])


def swap(a):
    return lax.ppermute(a, "core", [(0, 1), (1, 0)])


def params(**kw):
    return pltpu.CompilerParams(vmem_limit_bytes=VMEM, **kw)


def cost(flops, nbytes, trans=0):
    return pl.CostEstimate(flops=int(flops), bytes_accessed=int(nbytes), transcendentals=int(trans))


def prep_kernel(cand_ref, blk_ref, rank_ref, idx_ref):
    up = lax.broadcasted_iota(jnp.int32, (TOK, TOK), 0) < lax.broadcasted_iota(jnp.int32, (TOK, TOK), 1)
    up = jnp.where(up, 1.0, 0.0).astype(BF16)
    blk = blk_ref[:, 0:1]
    hits = []
    for s in range(NSRC):
        c = cand_ref[s]
        m = c[0:1] == blk
        for pick in range(1, 4):
            m = m | (c[pick : pick + 1] == blk)
        hits.append(jnp.where(m, 1.0, 0.0))
    hits = jnp.concatenate(hits, axis=0)
    before = jnp.dot(hits.astype(BF16), up, preferred_element_type=F32)
    rank = jnp.where(hits > 0, before, -1.0)
    for s in range(NSRC):
        rank_ref[s] = rank[s * NBLK : (s + 1) * NBLK]
    row = lax.broadcasted_iota(jnp.int32, (8, TOK), 0)
    v = lax.broadcasted_iota(jnp.int32, (8, TOK), 1)
    place = jnp.where(row == 0, v >> 3, jnp.where(row == 1, v & 7, jnp.where(row == 2, 1, 0)))
    place = place.astype(F32).astype(BF16)
    lane = lax.broadcasted_iota(jnp.int32, (1, SLOTS), 1)
    base = jnp.zeros((1, SLOTS), F32)
    for s in range(1, NSRC):
        base = base + jnp.where(lane >= s * MOST, float(TOK), 0.0)
    slot = lax.broadcasted_iota(jnp.int32, (MOST, TOK), 0).astype(F32)
    for b in range(NBLK):
        hot = [
            jnp.where(slot == rank[s * NBLK + b : s * NBLK + b + 1], 1.0, 0.0).astype(BF16)
            for s in range(NSRC)
        ]
        hot = jnp.concatenate(hot, axis=0)
        found = lax.dot_general(place, hot, (((1,), (1,)), ((), ())), preferred_element_type=F32)
        where = found[0:1] * 8.0 + found[1:2] + base
        idx_ref[b : b + 1, :] = jnp.where(found[2:3] > 0, where, -1.0).astype(jnp.int32)


def prep(cand, blk):
    return pl.pallas_call(
        prep_kernel,
        out_shape=(
            jax.ShapeDtypeStruct((NSRC, NBLK, TOK), F32),
            jax.ShapeDtypeStruct((NBLK, SLOTS), jnp.int32),
        ),
        compiler_params=params(),
        cost_estimate=cost(8e9, 1e6),
        name="prep",
    )(cand, blk)


def dispatch_kernel(v_ref, rank_ref, *refs):
    out_ref = refs[-1]
    half = pl.program_id(0)
    slot = lax.broadcasted_iota(jnp.int32, (MOST, TOK), 0).astype(F32)
    hot = []
    for k in range(4):
        r = rank_ref[0, pl.ds(half * 4 + k, 1), :]
        hot.append(jnp.where(slot == r, 1.0, 0.0).astype(BF16))
    hot = jnp.concatenate(hot, axis=0)
    rows = jnp.dot(hot, v_ref[...], preferred_element_type=F32).astype(BF16)
    out_ref[...] = rows.reshape(4, 1, MOST, D)


def dispatch(s, v, rank, rows):
    in_specs = [
        pl.BlockSpec((TOK, D), lambda i: (0, 0)),
        pl.BlockSpec((1, NBLK, TOK), lambda i: (s, 0, 0)),
    ]
    args = [v, rank]
    alias = {}
    if rows is not None:
        in_specs.append(pl.BlockSpec(memory_space=pl.ANY))
        args.append(rows)
        alias = {2: 0}
    return pl.pallas_call(
        dispatch_kernel,
        grid=(2,),
        in_specs=in_specs,
        out_specs=pl.BlockSpec((4, 1, MOST, D), lambda i: (i, s, 0, 0)),
        out_shape=jax.ShapeDtypeStruct((NBLK, NSRC, MOST, D), BF16),
        input_output_aliases=alias,
        compiler_params=params(),
        cost_estimate=cost(2 * NBLK * MOST * TOK * D, 3e6),
        name=f"dispatch{s}",
    )(*args)


def score_kernel(rows_ref, c0, c1, c2, c3, rank_ref, e_ref, peak_ref, stat_ref, cbuf, tot_scr):
    b = pl.program_id(0)
    for q, c in enumerate((c0, c1, c2, c3)):
        @pl.when(b // 2 == q)
        def _(c=c):
            cbuf[...] = c[...]

    cent = cbuf[...]
    rows = rows_ref[...].reshape(SLOTS, D)
    raw = lax.dot_general(cent, rows, (((1,), (1,)), ((), ())), preferred_element_type=F32)
    wide = cent.astype(F32)
    score = raw - 0.5 * jnp.sum(wide * wide, axis=1, keepdims=True)
    peak = jnp.max(score, axis=0, keepdims=True)
    e = jnp.exp(score - peak)
    e_ref[0] = e.astype(BF16)
    peak_ref[pl.ds(b, 1), :] = peak
    tot_scr[pl.ds(b, 1), :] = jnp.sum(e, axis=0, keepdims=True)

    @pl.when(b == NBLK - 1)
    def _():
        for s in range(NSRC):
            k0, k1 = s * MOST // 128, (s * MOST + MOST - 1) // 128
            for j in range(TOK // 128):
                r = rank_ref[s, :, j * 128 : (j + 1) * 128].astype(jnp.int32)
                at = r + s * MOST
                low = at & 127
                near = (at >> 7) == k0

                def fetch(ref):
                    first = jnp.take_along_axis(ref[:, k0 * 128 : (k0 + 1) * 128], low, axis=1, mode="promise_in_bounds")
                    if k1 == k0:
                        return first
                    second = jnp.take_along_axis(ref[:, k1 * 128 : (k1 + 1) * 128], low, axis=1, mode="promise_in_bounds")
                    return jnp.where(near, first, second)

                here = r >= 0
                pv = jnp.where(here, fetch(peak_ref), LOW)
                tv = jnp.where(here, fetch(tot_scr), 0.0)
                m = jnp.max(pv, axis=0, keepdims=True)
                t = jnp.sum(tv * jnp.exp(pv - m), axis=0, keepdims=True)
                stat_ref[0, s : s + 1, j * 128 : (j + 1) * 128] = m
                stat_ref[1, s : s + 1, j * 128 : (j + 1) * 128] = t


def score(rows, cents, rank):
    def cspec(q):
        return pl.BlockSpec((BS, D), lambda b: (jnp.clip(b - 2 * q, 0, 1), 0))

    return pl.pallas_call(
        score_kernel,
        grid=(NBLK,),
        in_specs=[pl.BlockSpec((1, NSRC, MOST, D), lambda b: (b, 0, 0, 0))]
        + [cspec(q) for q in range(4)]
        + [pl.BlockSpec((NSRC, NBLK, TOK), lambda b: (0, 0, 0))],
        out_specs=(
            pl.BlockSpec((1, BS, SLOTS), lambda b: (b, 0, 0)),
            pl.BlockSpec((NBLK, SLOTS), lambda b: (0, 0)),
            pl.BlockSpec((2, NSRC, TOK), lambda b: (0, 0, 0)),
        ),
        out_shape=(
            jax.ShapeDtypeStruct((NBLK, BS, SLOTS), BF16),
            jax.ShapeDtypeStruct((NBLK, SLOTS), F32),
            jax.ShapeDtypeStruct((2, NSRC, TOK), F32),
        ),
        scratch_shapes=[pltpu.VMEM((BS, D), BF16), pltpu.VMEM((NBLK, SLOTS), F32)],
        compiler_params=params(),
        cost_estimate=cost(2 * NBLK * BS * SLOTS * D, 23e6, NBLK * BS * SLOTS),
        name="score",
    )(rows, *cents, rank)


def factor_kernel(stat_refs, idx_ref, peak_ref, f_scr):
    own, from_d, from_e, from_f = stat_refs
    tables = []
    for s in range(NSRC):
        ms = [own[0, s : s + 1, :]]
        ts = [own[1, s : s + 1, :]]
        for ref, order in ((from_d, FROM_D), (from_e, FROM_E), (from_f, FROM_F)):
            o = order[s]
            ms.append(ref[0, o : o + 1, :])
            ts.append(ref[1, o : o + 1, :])
        m = jnp.maximum(jnp.maximum(ms[0], ms[1]), jnp.maximum(ms[2], ms[3]))
        t = ts[0] * jnp.exp(ms[0] - m)
        for k in range(1, 4):
            t = t + ts[k] * jnp.exp(ms[k] - m)
        tables.append(m + jnp.log(t))
    for k in range(SLOTS // 128):
        at = idx_ref[:, k * 128 : (k + 1) * 128]
        low = at & 127
        high = at >> 7
        lse = jnp.zeros((NBLK, 128), F32)
        for s in range(k * 128 // MOST, (k * 128 + 127) // MOST + 1):
            for j in range(TOK // 128):
                table = jnp.broadcast_to(tables[s][:, j * 128 : (j + 1) * 128], (NBLK, 128))
                got = jnp.take_along_axis(table, low, axis=1, mode="promise_in_bounds")
                lse = jnp.where(high == s * (TOK // 128) + j, got, lse)
        f = jnp.exp(peak_ref[:, k * 128 : (k + 1) * 128] - lse)
        f_scr[:, k * 128 : (k + 1) * 128] = jnp.where(at >= 0, f, 0.0)


def sums_kernel(part, where_ref, s0, s1, s2, s3, idx_ref, peak_ref, e_ref, rows_ref, o0, o1, o2, o3, cnt_ref, f_scr, acc):
    q = pl.program_id(0)

    @pl.when(q == 0)
    def _():
        factor_kernel((s0, s1, s2, s3), idx_ref, peak_ref, f_scr)

    f = f_scr[pl.ds(2 * q + part, 1), :]
    w = e_ref[0].astype(F32) * f
    count = jnp.sum(w, axis=1, keepdims=True)
    count = jnp.transpose(jnp.broadcast_to(count, (BS, 128)))[0:1]
    cnt_ref[pl.ds(where_ref[q], 1), :] = count
    rows = rows_ref[...].reshape(SLOTS, D)
    total = jnp.dot(w.astype(BF16), rows, preferred_element_type=F32)
    outs = (o0, o1, o2, o3)
    if part == 0:
        for k in range(4):
            @pl.when(q == k)
            def _(k=k):
                outs[k][...] = total.astype(BF16)
    else:
        acc[...] = total
        for k in range(4):
            start = pl.multiple_of(where_ref[4 + k] * 128, 128)
            outs[k][pl.ds(q, 1)] = acc[pl.ds(start, 128), :].astype(BF16)[None]


def sums(part, where, stats, idx, peak, e, rows):
    full = lambda *shape: pl.BlockSpec(shape, lambda q: (0,) * len(shape))
    shape = (BS, D) if part == 0 else (4, 128, D)

    def kern(*refs):
        sums_kernel(part, *refs)

    return pl.pallas_call(
        kern,
        grid=(4,),
        in_specs=[pl.BlockSpec(memory_space=pltpu.SMEM)]
        + [full(2, NSRC, TOK)] * 4
        + [
            full(NBLK, SLOTS),
            full(NBLK, SLOTS),
            pl.BlockSpec((1, BS, SLOTS), lambda q: (2 * q + part, 0, 0)),
            pl.BlockSpec((1, NSRC, MOST, D), lambda q: (2 * q + part, 0, 0, 0)),
        ],
        out_specs=tuple([full(*shape)] * 4 + [full(4, BS)]),
        out_shape=tuple([jax.ShapeDtypeStruct(shape, BF16)] * 4 + [jax.ShapeDtypeStruct((4, BS), F32)]),
        scratch_shapes=[pltpu.VMEM((NBLK, SLOTS), F32), pltpu.VMEM((BS, D), F32)],
        compiler_params=params(),
        cost_estimate=cost(2 * 4 * BS * SLOTS * D, 12e6),
        name=f"sums{part}",
    )(where, *stats, idx, peak, e, rows)


def place_kernel(where_ref, *refs):
    parts, out_ref, sems = refs[:8], refs[8], refs[9]
    copies = []
    for side in range(2):
        for k in range(4):
            for i in range(2):
                block = where_ref[8 + side] * 2 + i
                quarter = where_ref[4 * (side + 1) - 4 + k]
                copies.append(
                    pltpu.make_async_copy(
                        parts[side * 4 + k].at[i], out_ref.at[block, quarter], sems.at[len(copies)]
                    )
                )
    for copy in copies:
        copy.start()
    for copy in copies:
        copy.wait()


def place(where, parts):
    return pl.pallas_call(
        place_kernel,
        in_specs=[pl.BlockSpec(memory_space=pltpu.SMEM)] + [pl.BlockSpec(memory_space=pl.ANY)] * 8,
        out_specs=pl.BlockSpec(memory_space=pl.ANY),
        out_shape=jax.ShapeDtypeStruct((4, 4, 128, D), BF16),
        scratch_shapes=[pltpu.SemaphoreType.DMA((16,))],
        cost_estimate=cost(0, 6e6),
        name="place",
    )(where, *parts)


def add(*terms):
    total = terms[0].astype(F32)
    for t in terms[1:]:
        total = total + t.astype(F32)
    return total


def ring_sum(own, d, e, f, axis):
    r1 = turn(f, axis, 1)
    r2 = turn(d, axis, -1)
    r3 = turn(add(e, r1).astype(BF16), axis, 1)
    return add(own, r2, r3)


def body(vectors, centroids, candidates):
    core, x, y, z = (lax.axis_index(a) for a in ("core", "x", "y", "z"))
    step = 1 - 2 * core

    def around(i):
        return jnp.stack([i, (i - step) % 4, (i + step) % 4, (i + 2) % 4]).astype(jnp.int32)

    xs, zs = around(x), around(z)
    other_zs = jnp.stack([zs[0], zs[2], zs[1], zs[3]])

    cand = candidates.T.astype(F32)
    pair = jnp.stack([cand, swap(cand)])
    cd, ce, cf = turn(pair, "y", 1), turn(pair, "y", -1), far(pair, "y")
    cands = jnp.stack([pair[0], pair[1], cd[0], ce[1], ce[0], cd[1], cf[0], cf[1]])

    c0 = lax.dynamic_slice_in_dim(centroids, core * 1024, 1024, 0)
    a, b = turn(vectors, "y", 1), turn(vectors, "y", -1)
    c1, c2 = turn(c0, "x", 1), turn(c0, "x", -1)
    c = turn(a, "y", 1)
    c3 = turn(c1, "x", 1)
    sources = [vectors, swap(vectors), a, swap(a), b, swap(b), c, swap(c)]

    blk = ((y * 4 + xs) * 4 + 2 * core)[:, None] + jnp.arange(2, dtype=jnp.int32)[None, :]
    blk = jnp.broadcast_to(blk.reshape(NBLK, 1), (NBLK, 128)).astype(F32)
    rank, idx = prep(cands, blk)
    rows = None
    for s, v in enumerate(sources):
        rows = dispatch(s, v, rank, rows)
    e, peak, stat = score(rows, (c0, c1, c2, c3), rank)

    theirs = swap(stat)
    theirs = jnp.flip(theirs.reshape(2, 4, 2, TOK), axis=2).reshape(2, NSRC, TOK)
    m = jnp.maximum(stat[0], theirs[0])
    t = stat[1] * jnp.exp(stat[0] - m) + theirs[1] * jnp.exp(theirs[0] - m)
    merged = jnp.stack([m, t])
    stats = (merged, turn(merged, "y", 1), turn(merged, "y", -1), far(merged, "y"))

    where = jnp.concatenate([xs, zs])
    *h, cnt0 = sums(0, where, stats, idx, peak, e, rows)
    *g, cnt1 = sums(1, where, stats, idx, peak, e, rows)
    counts = lax.psum(jnp.stack([cnt0, cnt1]), ("x", "z"))
    counts = lax.dynamic_index_in_dim(counts, x, 1, keepdims=False)
    counts = lax.dynamic_slice_in_dim(counts, z * 128, 128, 1)

    h = ring_sum(*h, "x").astype(BF16)
    h = ring_sum(*(lax.dynamic_slice_in_dim(h, zs[k] * 128, 128, 0) for k in range(4)), "z")
    g = ring_sum(*g, "z").astype(BF16)
    g = ring_sum(*(g[k] for k in range(4)), "x")
    mine = lax.dynamic_slice_in_dim(c0.reshape(2, BS, D), z * 128, 128, 1).astype(F32)
    fresh = ((jnp.stack([h, g]) + mine) / (counts + 1.0)[:, :, None]).astype(BF16)

    fa, fb = turn(fresh, "z", 1), turn(fresh, "z", -1)
    fc = turn(fa, "z", 1)
    parts = [fresh, fa, fb, fc] + [swap(p) for p in (fresh, fa, fb, fc)]
    places = jnp.concatenate([zs, other_zs, jnp.stack([core, 1 - core])]).astype(jnp.int32)
    return place(places, parts).reshape(2048, D)


def solution(mesh):
    fine = Mesh(np.asarray(mesh.devices).reshape(4, 2, 4, 4), ("z", "core", "y", "x"))
    return jax.shard_map(
        body,
        mesh=fine,
        in_specs=(P(("z", "core", "y", "x"), None), P(("y", "x"), None), P(("z", "core", "y", "x"), None)),
        out_specs=P(("y", "x"), None),
        check_vma=False,
    )
```

```python
import jax
import jax.numpy as jnp
import numpy as np
from jax import lax
from jax.experimental import pallas as pl
from jax.experimental.pallas import tpu as pltpu
from jax.sharding import Mesh, PartitionSpec as P

BS = 512
MOST = 96
TOK = 1024
D = 768
NSRC = 8
NBLK = 8
SLOTS = NSRC * MOST
EXTRA = 16
EXT = TOK + EXTRA
LOW = -1e30
F32 = jnp.float32
BF16 = jnp.bfloat16
VMEM = 56 * 1024 * 1024

NAMES = ("v", "v'", "a", "b", "a'", "b'", "c", "c'")


def order(**came):
    return tuple(NAMES.index(came[n.replace("'", "_")]) for n in NAMES)


SWAPPED = order(v="v'", v_="v", a="a'", a_="a", b="b'", b_="b", c="c'", c_="c")
FROM_D = order(a="v", b_="v'", c="a", v_="a'", v="b", c_="b'", b="c", a_="c'")
FROM_E = order(b="v", a_="v'", v="a", c_="a'", c="b", v_="b'", a="c", b_="c'")
FROM_F = order(c="v", c_="v'", b="a", b_="a'", a="b", a_="b'", v="c", v_="c'")


def turn(a, axis, sign):
    axes = ("z", "core") if axis == "z" else ("core", axis)
    at = (lambda core, i: i * 2 + core) if axis == "z" else (lambda core, i: core * 4 + i)
    pairs = []
    for core in range(2):
        for i in range(4):
            pairs.append((at(core, i), at(core, (i + (sign if core == 0 else -sign)) % 4)))
    return lax.ppermute(a, axes, pairs)


def far(a, axis):
    return lax.ppermute(a, axis, [(i, (i + 2) % 4) for i in range(4)])


def swap(a):
    return lax.ppermute(a, "core", [(0, 1), (1, 0)])


def params(**kw):
    return pltpu.CompilerParams(vmem_limit_bytes=VMEM, **kw)


def cost(flops, nbytes, trans=0):
    return pl.CostEstimate(flops=int(flops), bytes_accessed=int(nbytes), transcendentals=int(trans))


def earlier():
    up = lax.broadcasted_iota(jnp.int32, (TOK, TOK), 0) < lax.broadcasted_iota(jnp.int32, (TOK, TOK), 1)
    return jnp.where(up, 1.0, 0.0).astype(BF16)


def ranks(tail, blk, up):
    tail = tail.astype(F32)
    hit = None
    for pick in range(4):
        named = jnp.concatenate([tail[2 * pick : 2 * pick + 1, 0:512], tail[2 * pick + 1 : 2 * pick + 2, 0:512]], axis=1)
        m = named == blk
        hit = m if hit is None else hit | m
    hit = jnp.where(hit, 1.0, 0.0)
    hits = jnp.concatenate([hit, jnp.zeros((8, TOK), F32)], axis=0).astype(BF16)
    before = jnp.dot(hits, up, preferred_element_type=F32)[0:NBLK]
    return jnp.where(hit > 0, before, -1.0)


def gathered(rank, vectors):
    slot = lax.broadcasted_iota(jnp.int32, (MOST, TOK), 0).astype(F32)
    hot = [jnp.where(slot == rank[b : b + 1, :], 1.0, 0.0).astype(BF16) for b in range(NBLK)]
    hot = jnp.concatenate(hot, axis=0)
    rows = jnp.dot(hot, vectors, preferred_element_type=F32).astype(BF16)
    return rows.reshape(NBLK, MOST, D)


def index_kernel(*refs):
    rank_refs, idx_ref = refs[:-1], refs[-1]
    sources = [(ref, k) for ref in rank_refs for k in range(ref.shape[0])]
    row = lax.broadcasted_iota(jnp.int32, (8, TOK), 0)
    v = lax.broadcasted_iota(jnp.int32, (8, TOK), 1)
    place = jnp.where(row == 0, v >> 3, jnp.where(row == 1, v & 7, jnp.where(row == 2, 1, 0)))
    place = place.astype(F32).astype(BF16)
    lane = lax.broadcasted_iota(jnp.int32, (1, SLOTS), 1)
    base = jnp.zeros((1, SLOTS), F32)
    for s in range(1, NSRC):
        base = base + jnp.where(lane >= s * MOST, float(TOK), 0.0)
    slot = lax.broadcasted_iota(jnp.int32, (MOST, TOK), 0).astype(F32)
    for b in range(NBLK):
        hot = [jnp.where(slot == ref[k, b : b + 1, :], 1.0, 0.0).astype(BF16) for ref, k in sources]
        hot = jnp.concatenate(hot, axis=0)
        found = lax.dot_general(place, hot, (((1,), (1,)), ((), ())), preferred_element_type=F32)
        where = found[0:1] * 8.0 + found[1:2] + base
        idx_ref[b : b + 1, :] = jnp.where(found[2:3] > 0, where, -1.0).astype(jnp.int32)


def indices(*rank):
    return pl.pallas_call(
        index_kernel,
        out_shape=jax.ShapeDtypeStruct((NBLK, SLOTS), jnp.int32),
        compiler_params=params(),
        cost_estimate=cost(4e9, 1e6),
        name="indices",
    )(*rank)


def dispatch_kernel(n, *refs):
    sources, blk_ref, (rank_ref, out_ref, buf, sems, up) = refs[:n], refs[n], refs[-5:]
    i = pl.program_id(0)

    def copy(k):
        return pltpu.make_async_copy(sources[k], buf.at[k % 2], sems.at[k % 2])

    @pl.when(i == 0)
    def _():
        copy(0).start()
        up[...] = earlier()

    for k in range(n):
        @pl.when(i == k)
        def _(k=k):
            if k + 1 < n:
                copy(k + 1).start()
            copy(k).wait()

    rank = ranks(buf[i % 2, TOK:EXT, :], blk_ref[:, 0:1], up[...])
    rank_ref[0] = rank
    out_ref[...] = gathered(rank, buf[i % 2, 0:TOK, :])


def dispatch(first, sources, blk, rows):
    n = len(sources)
    anywhere = pl.BlockSpec(memory_space=pltpu.HBM)
    in_specs = [anywhere] * n + [pl.BlockSpec((NBLK, 128), lambda i: (0, 0))]
    args = [*sources, blk]
    alias = {}
    if rows is not None:
        in_specs.append(anywhere)
        args.append(rows)
        alias = {n + 1: 1}

    def kern(*refs):
        dispatch_kernel(n, *refs)

    return pl.pallas_call(
        kern,
        grid=(n,),
        in_specs=in_specs,
        out_specs=(
            pl.BlockSpec((1, NBLK, TOK), lambda i: (i, 0, 0)),
            pl.BlockSpec((NBLK, MOST, D), lambda i: (0, first + i, 0)),
        ),
        out_shape=(
            jax.ShapeDtypeStruct((n, NBLK, TOK), F32),
            jax.ShapeDtypeStruct((NBLK, SLOTS, D), BF16),
        ),
        scratch_shapes=[
            pltpu.VMEM((2, EXT, D), BF16),
            pltpu.SemaphoreType.DMA((2,)),
            pltpu.VMEM((TOK, TOK), BF16),
        ],
        input_output_aliases=alias,
        compiler_params=params(),
        cost_estimate=cost(2 * n * NBLK * MOST * TOK * D, n * 3e6),
        name=f"dispatch{first}",
    )(*args)


def score_block(b, rows, cent_refs, cbuf):
    for q, c in enumerate(cent_refs):
        @pl.when(b // 2 == q)
        def _(c=c):
            cbuf[...] = c[...]

    cent = cbuf[...]
    raw = lax.dot_general(cent, rows, (((1,), (1,)), ((), ())), preferred_element_type=F32)
    wide = cent.astype(F32)
    score = raw - 0.5 * jnp.sum(wide * wide, axis=1, keepdims=True)
    peak = jnp.max(score, axis=0, keepdims=True)
    e = jnp.exp(score - peak)
    return e, peak, jnp.sum(e, axis=0, keepdims=True)


def early_kernel(rows_ref, c0, c1, c2, *refs):
    e_ref, peak_ref, lse_ref, cbuf = refs[-4:]
    b = pl.program_id(0)
    e, peak, total = score_block(b, rows_ref[0], (c0, c1, c2), cbuf)
    e_ref[0] = e.astype(BF16)
    peak_ref[pl.ds(b, 1), :] = peak
    lse_ref[pl.ds(b, 1), :] = peak + jnp.log(total)


def cent_spec(q, block):
    return pl.BlockSpec((BS, D), lambda i: (jnp.clip(block(i) - 2 * q, 0, 1), 0))


def early_scores(rows, cents, part, width, e):
    in_specs = [pl.BlockSpec((1, width, D), lambda b: (b, part, 0))] + [cent_spec(q, lambda i: i) for q in range(3)]
    args = [rows, *cents]
    alias = {}
    if e is not None:
        in_specs.append(pl.BlockSpec(memory_space=pltpu.HBM))
        args.append(e)
        alias = {4: 0}
    return pl.pallas_call(
        early_kernel,
        grid=(6,),
        in_specs=in_specs,
        out_specs=(
            pl.BlockSpec((1, BS, width), lambda b: (b, 0, part)),
            pl.BlockSpec((NBLK, width), lambda b: (0, 0)),
            pl.BlockSpec((NBLK, width), lambda b: (0, 0)),
        ),
        out_shape=(
            jax.ShapeDtypeStruct((NBLK, BS, SLOTS), BF16),
            jax.ShapeDtypeStruct((NBLK, width), F32),
            jax.ShapeDtypeStruct((NBLK, width), F32),
        ),
        scratch_shapes=[pltpu.VMEM((BS, D), BF16)],
        input_output_aliases=alias,
        compiler_params=params(),
        cost_estimate=cost(2 * 6 * BS * width * D, 12e6, 6 * BS * width),
        name=f"early_scores{part}",
    )(*args)


def late_block(i):
    return jnp.where(i < 6, i, 6 + (i - 6) // 3)


def late_chunk(i):
    return jnp.where(i < 6, 2, (i - 6) % 3)


def late_kernel(
    source_ref, blk_ref, rows_ref, c0, c1, c2, c3, rank0, rank1, rank2, rank3, peak0, lse0, _,
    e_ref, out_ref, rank_ref, peak_ref, stat_ref, cbuf, lse_scr, buf, sem,
):
    i = pl.program_id(0)
    b, chunk = late_block(i), late_chunk(i)
    lanes = pl.ds(pl.multiple_of(chunk * 256, 256), 256)

    @pl.when(i == 0)
    def _():
        copy = pltpu.make_async_copy(source_ref, buf, sem)
        copy.start()
        peak_ref[:, 0:512] = peak0[...]
        lse_scr[:, 0:512] = lse0[...]
        up = earlier()
        copy.wait()
        rank = ranks(buf[TOK:EXT, :], blk_ref[:, 0:1], up)
        rank_ref[0] = rank
        out_ref[...] = gathered(rank, buf[0:TOK, :])

    head = rows_ref[0, 0:160, :]
    last = jnp.where(chunk == 2, out_ref[pl.ds(b, 1)][0], rows_ref[0, 160:256, :])
    e, peak, total = score_block(b, jnp.concatenate([head, last], axis=0), (c0, c1, c2, c3), cbuf)
    e_ref[0] = e.astype(BF16)
    peak_ref[pl.ds(b, 1), lanes] = peak
    lse_scr[pl.ds(b, 1), lanes] = peak + jnp.log(total)

    @pl.when(i == 11)
    def _():
        sources = [(ref, k) for ref in (rank0, rank1, rank2, rank3, rank_ref) for k in range(ref.shape[0])]
        for s, (ref, k) in enumerate(sources):
            k0, k1 = s * MOST // 128, (s * MOST + MOST - 1) // 128
            for j in range(TOK // 128):
                r = ref[k, :, j * 128 : (j + 1) * 128].astype(jnp.int32)
                at = r + s * MOST
                low = at & 127
                got = jnp.take_along_axis(lse_scr[:, k0 * 128 : (k0 + 1) * 128], low, axis=1, mode="promise_in_bounds")
                if k1 > k0:
                    other = jnp.take_along_axis(
                        lse_scr[:, k1 * 128 : (k1 + 1) * 128], low, axis=1, mode="promise_in_bounds"
                    )
                    got = jnp.where((at >> 7) == k0, got, other)
                got = jnp.where(r >= 0, got, LOW)
                m = jnp.max(got, axis=0, keepdims=True)
                t = jnp.sum(jnp.exp(got - m), axis=0, keepdims=True)
                stat_ref[s : s + 1, j * 128 : (j + 1) * 128] = m + jnp.log(t)


def late_scores(source, blk, rows, cents, ranked, before, e):
    full = lambda *shape: pl.BlockSpec(shape, lambda i: (0,) * len(shape))
    hbm = pl.BlockSpec(memory_space=pltpu.HBM)
    return pl.pallas_call(
        late_kernel,
        grid=(12,),
        in_specs=[hbm, full(NBLK, 128), pl.BlockSpec((1, 256, D), lambda i: (late_block(i), late_chunk(i), 0))]
        + [cent_spec(q, late_block) for q in range(4)]
        + [full(*r.shape) for r in ranked]
        + [full(*p.shape) for p in before]
        + [hbm],
        out_specs=(
            pl.BlockSpec((1, BS, 256), lambda i: (late_block(i), 0, late_chunk(i))),
            pl.BlockSpec((NBLK, MOST, D), lambda i: (0, NSRC - 1, 0)),
            full(1, NBLK, TOK),
            full(NBLK, SLOTS),
            full(NSRC, TOK),
        ),
        out_shape=(
            jax.ShapeDtypeStruct((NBLK, BS, SLOTS), BF16),
            jax.ShapeDtypeStruct((NBLK, SLOTS, D), BF16),
            jax.ShapeDtypeStruct((1, NBLK, TOK), F32),
            jax.ShapeDtypeStruct((NBLK, SLOTS), F32),
            jax.ShapeDtypeStruct((NSRC, TOK), F32),
        ),
        scratch_shapes=[
            pltpu.VMEM((BS, D), BF16),
            pltpu.VMEM((NBLK, SLOTS), F32),
            pltpu.VMEM((EXT, D), BF16),
            pltpu.SemaphoreType.DMA,
        ],
        input_output_aliases={13: 0, 2: 1},
        compiler_params=params(),
        cost_estimate=cost(2 * 4 * BS * SLOTS * D, 20e6, 4 * BS * SLOTS),
        name="late_scores",
    )(source, blk, rows, *cents, *ranked, *before, e)


def factor_kernel(stat_refs, idx_ref, peak_ref, f_scr):
    own, from_d, from_e, from_f = stat_refs
    tables = []
    for s in range(NSRC):
        parts = [own[s : s + 1, :]]
        for ref, order in ((from_d, FROM_D), (from_e, FROM_E), (from_f, FROM_F)):
            parts.append(ref[order[s] : order[s] + 1, :])
        m = jnp.maximum(jnp.maximum(parts[0], parts[1]), jnp.maximum(parts[2], parts[3]))
        t = jnp.exp(parts[0] - m)
        for k in range(1, 4):
            t = t + jnp.exp(parts[k] - m)
        tables.append(m + jnp.log(t))
    for k in range(SLOTS // 128):
        at = idx_ref[:, k * 128 : (k + 1) * 128]
        low = at & 127
        high = at >> 7
        lse = jnp.zeros((NBLK, 128), F32)
        for s in range(k * 128 // MOST, (k * 128 + 127) // MOST + 1):
            for j in range(TOK // 128):
                table = jnp.broadcast_to(tables[s][:, j * 128 : (j + 1) * 128], (NBLK, 128))
                got = jnp.take_along_axis(table, low, axis=1, mode="promise_in_bounds")
                lse = jnp.where(high == s * (TOK // 128) + j, got, lse)
        f = jnp.exp(peak_ref[:, k * 128 : (k + 1) * 128] - lse)
        f_scr[:, k * 128 : (k + 1) * 128] = jnp.where(at >= 0, f, 0.0)


def sums_owner(i):
    t = i % 4
    return jnp.where(t == 0, 3, jnp.where(t == 3, 0, t))


def sums_kernel(where_ref, s0, s1, s2, s3, idx_ref, peak_ref, e_ref, rows_ref, *refs):
    outs, (f_scr, acc, hbuf, gbuf, hsem, gsem) = refs[:8], refs[8:]
    i = pl.program_id(0)
    q, slot = sums_owner(i), i % 2

    def send_h(k):
        return pltpu.make_async_copy(hbuf.at[slot], outs[k], hsem.at[slot])

    def send_g(k):
        return pltpu.make_async_copy(gbuf.at[slot, k], outs[4 + k].at[q], gsem.at[slot, k])

    @pl.when(i == 0)
    def _():
        factor_kernel((s0, s1, s2, s3), idx_ref, peak_ref, f_scr)

    f = f_scr[pl.ds(2 * q + i // 4, 1), :]
    w = e_ref[0].astype(F32) * f
    count = jnp.sum(w, axis=1, keepdims=True)
    count = jnp.transpose(jnp.broadcast_to(count, (BS, 128)))[0:EXTRA]
    count = jnp.concatenate([count, jnp.zeros((EXTRA, D - BS), F32)], axis=1).astype(BF16)
    acc[...] = jnp.dot(w.astype(BF16), rows_ref[0], preferred_element_type=F32)

    @pl.when((i == 2) | (i == 3) | (i == 6) | (i == 7))
    def _():
        @pl.when(i < 4)
        def _():
            send_h(0).wait()

        @pl.when(i >= 4)
        def _():
            for k in range(4):
                send_g(k).wait()

    @pl.when(i < 4)
    def _():
        hbuf[slot, 0:BS, :] = acc[...].astype(BF16)
        hbuf[slot, BS : BS + EXTRA, :] = count
        for k in range(4):
            @pl.when(q == k)
            def _(k=k):
                send_h(k).start()

    @pl.when(i >= 4)
    def _():
        for k in range(4):
            start = pl.multiple_of(where_ref[4 + k] * 128, 128)
            gbuf[slot, k, 0:128, :] = acc[pl.ds(start, 128), :].astype(BF16)
            gbuf[slot, k, 128 : 128 + EXTRA, :] = count
            send_g(k).start()

    @pl.when(i == 7)
    def _():
        for other in range(2):
            pltpu.make_async_copy(hbuf.at[other], outs[0], hsem.at[other]).wait()
            for k in range(4):
                pltpu.make_async_copy(gbuf.at[other, k], outs[4 + k].at[0], gsem.at[other, k]).wait()


def sums(where, stats, idx, peak, e, rows):
    full = lambda *shape: pl.BlockSpec(shape, lambda i: (0,) * len(shape))
    h, g = (BS + EXTRA, D), (4, 128 + EXTRA, D)
    out = pl.pallas_call(
        sums_kernel,
        grid=(8,),
        in_specs=[pl.BlockSpec(memory_space=pltpu.SMEM)]
        + [full(NSRC, TOK)] * 4
        + [
            full(NBLK, SLOTS),
            full(NBLK, SLOTS),
            pl.BlockSpec((1, BS, SLOTS), lambda i: (2 * sums_owner(i) + i // 4, 0, 0)),
            pl.BlockSpec((1, SLOTS, D), lambda i: (2 * sums_owner(i) + i // 4, 0, 0)),
        ],
        out_specs=tuple([pl.BlockSpec(memory_space=pltpu.HBM)] * 8),
        out_shape=tuple([jax.ShapeDtypeStruct(h, BF16)] * 4 + [jax.ShapeDtypeStruct(g, BF16)] * 4),
        scratch_shapes=[
            pltpu.VMEM((NBLK, SLOTS), F32),
            pltpu.VMEM((BS, D), F32),
            pltpu.VMEM((2, *h), BF16),
            pltpu.VMEM((2, *g), BF16),
            pltpu.SemaphoreType.DMA((2,)),
            pltpu.SemaphoreType.DMA((2, 4)),
        ],
        compiler_params=params(),
        cost_estimate=cost(2 * 8 * BS * SLOTS * D, 24e6),
        name="sums",
    )(where, *stats, idx, peak, e, rows)
    return out[:4], out[4:]


def parted_kernel(where_ref, h0, h1, h2, g0, g1, g2, *refs):
    outs, acc = refs[:8], refs[8]
    acc[...] = h0[...].astype(F32) + h1[...].astype(F32) + h2[...].astype(F32)
    for k in range(4):
        start = pl.multiple_of(where_ref[4 + k] * 128, 128)
        outs[k][0:128, :] = acc[pl.ds(start, 128), :].astype(BF16)
        outs[k][128:, :] = acc[BS:, :].astype(BF16)
        total = g0[k].astype(F32) + g1[k].astype(F32) + g2[k].astype(F32)
        outs[4 + k][...] = total.astype(BF16)


def parted(where, h, g):
    vmem = pl.BlockSpec(memory_space=pltpu.VMEM)
    out = pl.pallas_call(
        parted_kernel,
        in_specs=[pl.BlockSpec(memory_space=pltpu.SMEM)] + [vmem] * 6,
        out_specs=(vmem,) * 8,
        out_shape=(jax.ShapeDtypeStruct((128 + EXTRA, D), BF16),) * 8,
        scratch_shapes=[pltpu.VMEM((BS + EXTRA, D), F32)],
        compiler_params=params(),
        cost_estimate=cost(1e6, 8e6),
        name="parted",
    )(where, *h, *g)
    return out[:4], out[4:]


def final_kernel(where_ref, h0, h1, h2, h3, g0, g1, g2, g3, mine_ref, out_ref):
    for i, refs in enumerate(((h0, h1, h2, h3), (g0, g1, g2, g3))):
        total = (refs[0][...].astype(F32) + refs[1][...].astype(F32)) + (refs[2][...].astype(F32) + refs[3][...].astype(F32))
        counts = total[128:136, 0:BS]
        picked = jnp.zeros((8, 128), F32)
        for k in range(4):
            picked = jnp.where(where_ref[4] == k, counts[:, k * 128 : (k + 1) * 128], picked)
        column = jnp.transpose(jnp.broadcast_to(picked[0:1], (128, 128)))[:, 0:1]
        fresh = (total[0:128] + mine_ref[i].astype(F32)) / (column + 1.0)
        out_ref[i] = fresh.astype(BF16)


def final(where, h, g, mine):
    return pl.pallas_call(
        final_kernel,
        in_specs=[pl.BlockSpec(memory_space=pltpu.SMEM)] + [pl.BlockSpec(memory_space=pltpu.VMEM)] * 9,
        out_specs=pl.BlockSpec(memory_space=pltpu.VMEM),
        out_shape=jax.ShapeDtypeStruct((2, 128, D), BF16),
        compiler_params=params(),
        cost_estimate=cost(1e6, 2e6),
        name="final",
    )(where, *h, *g, mine)


def place_kernel(where_ref, *refs):
    parts, out_ref = refs[:8], refs[8]
    for side in range(2):
        for k in range(4):
            for i in range(2):
                block = where_ref[8 + side] * 2 + i
                quarter = where_ref[4 * side + k]
                out_ref[pl.ds(block, 1), pl.ds(quarter, 1)] = parts[side * 4 + k][i][None, None]


def place(where, parts):
    return pl.pallas_call(
        place_kernel,
        in_specs=[pl.BlockSpec(memory_space=pltpu.SMEM)] + [pl.BlockSpec(memory_space=pltpu.VMEM)] * 8,
        out_specs=pl.BlockSpec(memory_space=pltpu.VMEM),
        out_shape=jax.ShapeDtypeStruct((4, 4, 128, D), BF16),
        compiler_params=params(),
        cost_estimate=cost(0, 6e6),
        name="place",
    )(where, *parts)


def tie(a, *after):
    return pl.pallas_call(
        lambda *refs: None,
        in_specs=[pl.BlockSpec(memory_space=pltpu.HBM)] * (1 + len(after)),
        out_specs=pl.BlockSpec(memory_space=pltpu.HBM),
        out_shape=jax.ShapeDtypeStruct(a.shape, a.dtype),
        input_output_aliases={0: 0},
        cost_estimate=cost(0, 0),
        name="tie",
    )(a, *after)


def add(*terms):
    total = terms[0].astype(F32)
    for t in terms[1:]:
        total = total + t.astype(F32)
    return total


def ring_terms(own, d, e, f, axis):
    r1 = turn(f, axis, 1)
    r2 = turn(d, axis, -1)
    r3 = turn(add(e, r1).astype(BF16), axis, 1)
    return own, r2, r3


def direct_terms(own, d, e, f, axis):
    return own, turn(d, axis, -1), turn(e, axis, 1), far(f, axis)


def body(vectors, centroids, candidates):
    core, x, y, z = (lax.axis_index(a) for a in ("core", "x", "y", "z"))
    step = 1 - 2 * core

    def around(i):
        return jnp.stack([i, (i - step) % 4, (i + step) % 4, (i + 2) % 4]).astype(jnp.int32)

    xs, zs = around(x), around(z)
    other_zs = jnp.stack([zs[0], zs[2], zs[1], zs[3]])

    where = jnp.concatenate([xs, zs])
    tail = jnp.pad(candidates.T.reshape(8, 512).astype(BF16), ((0, EXTRA - 8), (0, D - 512)))
    v = jnp.concatenate([vectors, tail])
    a, b = turn(v, "y", 1), turn(v, "y", -1)
    c0 = lax.dynamic_slice_in_dim(centroids, core * 1024, 1024, 0)
    c1, c2 = turn(c0, "x", 1), turn(c0, "x", -1)
    mine = lax.dynamic_slice_in_dim(c0.reshape(2, BS, D), z * 128, 128, 1)
    blk = ((y * 4 + xs) * 4 + 2 * core)[:, None] + jnp.arange(2, dtype=jnp.int32)[None, :]
    blk = jnp.broadcast_to(blk.reshape(NBLK, 1), (NBLK, 128)).astype(F32)

    rank0, rows = dispatch(0, (v, swap(v)), blk, None)
    a = tie(a, rows, b, c1, c2)
    c = turn(a, "y", 1)
    c3 = turn(c1, "x", 1)
    rank1, rows = dispatch(2, (a, b), blk, rows)
    rank2, rows = dispatch(4, (swap(a), swap(b)), blk, rows)
    e, peak0, lse0 = early_scores(rows, (c0, c1, c2), 0, 512, None)
    c = tie(c, e, c3)
    rank3, rows = dispatch(6, (c,), blk, rows)
    ranked = (rank0, rank1, rank2, rank3)
    e, rows, rank4, peak, stat = late_scores(swap(c), blk, rows, (c0, c1, c2, c3), ranked, (peak0, lse0), e)
    idx = indices(*ranked, rank4)

    theirs = swap(stat)
    theirs = jnp.concatenate([theirs[s : s + 1] for s in SWAPPED])
    m = jnp.maximum(stat, theirs)
    merged = m + jnp.log(jnp.exp(stat - m) + jnp.exp(theirs - m))
    stats = (merged, turn(merged, "y", 1), turn(merged, "y", -1), far(merged, "y"))

    h, g = sums(where, stats, idx, peak, e, rows)
    h, g = ring_terms(*h, "x"), ring_terms(*g, "z")
    h, g = parted(where, h, g)
    h, g = direct_terms(*h, "z"), direct_terms(*g, "x")
    fresh = final(where, h, g, mine)

    others = [turn(fresh, "z", 1), turn(fresh, "z", -1), far(fresh, "z")]
    parts = [fresh, *others] + [swap(p) for p in (fresh, *others)]
    places = jnp.concatenate([zs, other_zs, jnp.stack([core, 1 - core])]).astype(jnp.int32)
    return place(places, parts).reshape(2048, D)


def solution(mesh):
    fine = Mesh(np.asarray(mesh.devices).reshape(4, 2, 4, 4), ("z", "core", "y", "x"))
    return jax.shard_map(
        body,
        mesh=fine,
        in_specs=(P(("z", "core", "y", "x"), None), P(("y", "x"), None), P(("z", "core", "y", "x"), None)),
        out_specs=P(("y", "x"), None),
        check_vma=False,
    )
```

```python
import jax
import jax.numpy as jnp
import numpy as np
from jax import lax
from jax.experimental import pallas as pl
from jax.experimental.pallas import tpu as pltpu
from jax.sharding import Mesh, PartitionSpec as P

BS = 512
MOST = 96
TOK = 1024
D = 768
NSRC = 8
NBLK = 8
SLOTS = NSRC * MOST
EXTRA = 16
EXT = TOK + EXTRA
ROWS = (28, SLOTS, D)
SCORES = (40, BS, SLOTS)
LOW = -1e30
F32 = jnp.float32
BF16 = jnp.bfloat16

NAMES = ("v", "v'", "a", "b", "a'", "b'", "c", "c'")


def order(**came):
    return tuple(NAMES.index(came[n.replace("'", "_")]) for n in NAMES)


SWAPPED = order(v="v'", v_="v", a="a'", a_="a", b="b'", b_="b", c="c'", c_="c")
FROM_D = order(a="v", b_="v'", c="a", v_="a'", v="b", c_="b'", b="c", a_="c'")
FROM_E = order(b="v", a_="v'", v="a", c_="a'", c="b", v_="b'", a="c", b_="c'")
FROM_F = order(c="v", c_="v'", b="a", b_="a'", a="b", a_="b'", v="c", v_="c'")


def turn(a, axis, sign):
    axes = ("z", "core") if axis == "z" else ("core", axis)
    at = (lambda core, i: i * 2 + core) if axis == "z" else (lambda core, i: core * 4 + i)
    pairs = []
    for core in range(2):
        for i in range(4):
            pairs.append((at(core, i), at(core, (i + (sign if core == 0 else -sign)) % 4)))
    return lax.ppermute(a, axes, pairs)


def far(a, axis):
    return lax.ppermute(a, axis, [(i, (i + 2) % 4) for i in range(4)])


def swap(a):
    return lax.ppermute(a, "core", [(0, 1), (1, 0)])


def params(mib):
    return pltpu.CompilerParams(vmem_limit_bytes=mib * 1024 * 1024)


def cost(flops, nbytes, trans=0):
    return pl.CostEstimate(flops=int(flops), bytes_accessed=int(nbytes), transcendentals=int(trans))


def earlier():
    up = lax.broadcasted_iota(jnp.int32, (TOK, TOK), 0) < lax.broadcasted_iota(jnp.int32, (TOK, TOK), 1)
    return jnp.where(up, 1.0, 0.0).astype(BF16)


def ranks(tail, blk, up):
    tail = tail.astype(F32)
    hit = None
    for pick in range(4):
        named = jnp.concatenate([tail[2 * pick : 2 * pick + 1, 0:512], tail[2 * pick + 1 : 2 * pick + 2, 0:512]], axis=1)
        m = named == blk
        hit = m if hit is None else hit | m
    hit = jnp.where(hit, 1.0, 0.0)
    hits = jnp.concatenate([hit, jnp.zeros((8, TOK), F32)], axis=0).astype(BF16)
    before = jnp.dot(hits, up, preferred_element_type=F32)[0:NBLK]
    return jnp.where(hit > 0, before, -1.0)


def gathered(rank, vectors):
    slot = lax.broadcasted_iota(jnp.int32, (MOST, TOK), 0).astype(F32)
    hot = [jnp.where(slot == rank[b : b + 1, :], 1.0, 0.0).astype(BF16) for b in range(NBLK)]
    hot = jnp.concatenate(hot, axis=0)
    rows = jnp.dot(hot, vectors, preferred_element_type=F32).astype(BF16)
    return rows.reshape(NBLK, MOST, D)


def index_kernel(*refs):
    rank_refs, idx_ref = refs[:-1], refs[-1]
    sources = [(ref, k) for ref in rank_refs for k in range(ref.shape[0])]
    row = lax.broadcasted_iota(jnp.int32, (8, TOK), 0)
    v = lax.broadcasted_iota(jnp.int32, (8, TOK), 1)
    place = jnp.where(row == 0, v >> 3, jnp.where(row == 1, v & 7, jnp.where(row == 2, 1, 0)))
    place = place.astype(F32).astype(BF16)
    lane = lax.broadcasted_iota(jnp.int32, (1, SLOTS), 1)
    base = jnp.zeros((1, SLOTS), F32)
    for s in range(1, NSRC):
        base = base + jnp.where(lane >= s * MOST, float(TOK), 0.0)
    slot = lax.broadcasted_iota(jnp.int32, (MOST, TOK), 0).astype(F32)
    for b in range(NBLK):
        hot = [jnp.where(slot == ref[k, b : b + 1, :], 1.0, 0.0).astype(BF16) for ref, k in sources]
        hot = jnp.concatenate(hot, axis=0)
        found = lax.dot_general(place, hot, (((1,), (1,)), ((), ())), preferred_element_type=F32)
        where = found[0:1] * 8.0 + found[1:2] + base
        idx_ref[b : b + 1, :] = jnp.where(found[2:3] > 0, where, -1.0).astype(jnp.int32)


def indices(*rank):
    return pl.pallas_call(
        index_kernel,
        out_shape=jax.ShapeDtypeStruct((NBLK, SLOTS), jnp.int32),
        compiler_params=params(12),
        cost_estimate=cost(4e9, 1e6),
        name="indices",
    )(*rank)


def dispatch_kernel(n, *refs):
    sources, blk_ref, (rank_ref, out_ref, buf, sems, up) = refs[:n], refs[n], refs[-5:]
    i = pl.program_id(0)

    def copy(k):
        return pltpu.make_async_copy(sources[k], buf.at[k % 2], sems.at[k % 2])

    @pl.when(i == 0)
    def _():
        copy(0).start()
        up[...] = earlier()

    for k in range(n):
        @pl.when(i == k)
        def _(k=k):
            if k + 1 < n:
                copy(k + 1).start()
            copy(k).wait()

    rank = ranks(buf[i % 2, TOK:EXT, :], blk_ref[:, 0:1], up[...])
    rank_ref[0] = rank
    out_ref[...] = gathered(rank, buf[i % 2, 0:TOK, :])


def dispatch(first, sources, blk, rows):
    n = len(sources)
    anywhere = pl.BlockSpec(memory_space=pl.ANY)
    in_specs = [anywhere] * n + [pl.BlockSpec((NBLK, 128), lambda i: (0, 0))]
    args = [*sources, blk]
    alias = {}
    if rows is not None:
        in_specs.append(pl.BlockSpec(memory_space=pltpu.HBM))
        args.append(rows)
        alias = {n + 1: 1}

    def kern(*refs):
        dispatch_kernel(n, *refs)

    return pl.pallas_call(
        kern,
        grid=(n,),
        in_specs=in_specs,
        out_specs=(
            pl.BlockSpec((1, NBLK, TOK), lambda i: (i, 0, 0)),
            pl.BlockSpec((NBLK, MOST, D), lambda i: (0, first + i, 0)),
        ),
        out_shape=(
            jax.ShapeDtypeStruct((n, NBLK, TOK), F32),
            jax.ShapeDtypeStruct(ROWS, BF16),
        ),
        scratch_shapes=[
            pltpu.VMEM((2, EXT, D), BF16),
            pltpu.SemaphoreType.DMA((2,)),
            pltpu.VMEM((TOK, TOK), BF16),
        ],
        input_output_aliases=alias,
        compiler_params=params(20),
        cost_estimate=cost(2 * n * NBLK * MOST * TOK * D, n * 3e6),
        name=f"dispatch{first}",
    )(*args)


def half_norm(cent):
    wide = cent.astype(F32)
    return 0.5 * jnp.sum(wide * wide, axis=1, keepdims=True)


def score_chunk(cent, norm, rows):
    raw = lax.dot_general(cent, rows, (((1,), (1,)), ((), ())), preferred_element_type=F32)
    score = raw - norm
    peak = jnp.max(score, axis=0, keepdims=True)
    e = jnp.exp(score - peak)
    return e.astype(BF16), peak, peak + jnp.log(jnp.sum(e, axis=0, keepdims=True))


def middle_kernel(
    s0, s1, blk_ref, c0, c1, c2, rows_in,
    rows_out, rank_ref, e_out, peak_ref, lse_ref,
    vbuf, x03, x45, cb, eb, vsem, csem, xsem, osem, esem,
):
    sources = [pltpu.make_async_copy(s, vbuf.at[k], vsem.at[k]) for k, s in enumerate((s0, s1))]
    cents = [pltpu.make_async_copy(c, cb.at[k], csem.at[k]) for k, c in enumerate((c0, c1, c2))]
    first = pltpu.make_async_copy(rows_in.at[pl.ds(0, 6), pl.ds(0, 384), :], x03, xsem)
    for copy in sources:
        copy.start()
    up = earlier()
    for k in range(2):
        sources[k].wait()
        for copy in (first, cents[0]) if k == 0 else cents[1:]:
            copy.start()
        rank = ranks(vbuf[k, TOK:EXT, :], blk_ref[:, 0:1], up)
        rank_ref[k] = rank
        x45[:, k * MOST : (k + 1) * MOST, :] = gathered(rank, vbuf[k, 0:TOK, :])
    back = pltpu.make_async_copy(x45, rows_out.at[pl.ds(0, NBLK), pl.ds(384, 192), :], osem)
    back.start()
    first.wait()
    for q in range(3):
        cents[q].wait()
        for i in range(2):
            b = 2 * q + i
            cent = cb[q, i * BS : (i + 1) * BS, :]
            norm = half_norm(cent)
            chunks = (x03[b, 0:256, :], jnp.concatenate([x03[b, 256:384, :], x45[b, 0:128, :]], axis=0))
            for k, rows in enumerate(chunks):
                e, peak, lse = score_chunk(cent, norm, rows)
                eb[b, :, k * 256 : (k + 1) * 256] = e
                peak_ref[b : b + 1, k * 256 : (k + 1) * 256] = peak
                lse_ref[b : b + 1, k * 256 : (k + 1) * 256] = lse
            pltpu.make_async_copy(eb.at[b], e_out.at[b, :, pl.ds(0, 512)], esem.at[b]).start()
    back.wait()
    for b in range(6):
        pltpu.make_async_copy(eb.at[b], e_out.at[b, :, pl.ds(0, 512)], esem.at[b]).wait()


def middle(sources, blk, cents, rows):
    anywhere, hbm = pl.BlockSpec(memory_space=pl.ANY), pl.BlockSpec(memory_space=pltpu.HBM)
    vmem = pl.BlockSpec(memory_space=pltpu.VMEM)
    return pl.pallas_call(
        middle_kernel,
        in_specs=[anywhere] * 2 + [vmem] + [anywhere] * 3 + [hbm],
        out_specs=(hbm, vmem, hbm, vmem, vmem),
        out_shape=(
            jax.ShapeDtypeStruct(ROWS, BF16),
            jax.ShapeDtypeStruct((2, NBLK, TOK), F32),
            jax.ShapeDtypeStruct(SCORES, BF16),
            jax.ShapeDtypeStruct((NBLK, 512), F32),
            jax.ShapeDtypeStruct((NBLK, 512), F32),
        ),
        scratch_shapes=[
            pltpu.VMEM((2, EXT, D), BF16),
            pltpu.VMEM((6, 384, D), BF16),
            pltpu.VMEM((NBLK, 192, D), BF16),
            pltpu.VMEM((3, 1024, D), BF16),
            pltpu.VMEM((6, BS, 512), BF16),
            pltpu.SemaphoreType.DMA((2,)),
            pltpu.SemaphoreType.DMA((3,)),
            pltpu.SemaphoreType.DMA,
            pltpu.SemaphoreType.DMA,
            pltpu.SemaphoreType.DMA((6,)),
        ],
        input_output_aliases={6: 0},
        compiler_params=params(32),
        cost_estimate=cost(4 * NBLK * MOST * TOK * D, 20e6, 6 * BS * 512),
        name="middle",
    )(*sources, blk, *cents, rows)


def late_kernel(
    source0, source1, blk_ref, c0, c1, c2, c3, rank0, rank1, rank2, peak0, lse0, rows_in, e_in,
    rows_out, e_out, rank_ref, peak_ref, stat_ref,
    vbuf, xa, xb, x67, cb, ea, eb, lse_scr, vsem, csem, xsem, osem, esem,
):
    load0 = pltpu.make_async_copy(source0, vbuf.at[0], vsem.at[0])
    load1 = pltpu.make_async_copy(source1, vbuf.at[1], vsem.at[1])
    near = pltpu.make_async_copy(rows_in.at[pl.ds(0, 6), pl.ds(512, 64), :], xa, xsem.at[0])
    far_rows = pltpu.make_async_copy(rows_in.at[pl.ds(6, 2), pl.ds(0, 576), :], xb, xsem.at[1])
    cents = [pltpu.make_async_copy(c, cb.at[k], csem.at[k]) for k, c in enumerate((c0, c1, c2, c3))]
    load0.start()
    load1.start()
    peak_ref[:, 0:512] = peak0[...]
    lse_scr[:, 0:512] = lse0[...]
    up = earlier()
    load0.wait()
    for copy in (near, cents[0], cents[1]):
        copy.start()
    rank = ranks(vbuf[0, TOK:EXT, :], blk_ref[:, 0:1], up)
    rank_ref[0] = rank
    x67[:, 0:MOST, :] = gathered(rank, vbuf[0, 0:TOK, :])
    load1.wait()
    for copy in (cents[2], cents[3], far_rows):
        copy.start()
    rank = ranks(vbuf[1, TOK:EXT, :], blk_ref[:, 0:1], up)
    rank_ref[1] = rank
    x67[:, MOST : 2 * MOST, :] = gathered(rank, vbuf[1, 0:TOK, :])
    back = pltpu.make_async_copy(x67, rows_out.at[pl.ds(0, NBLK), pl.ds(576, 2 * MOST), :], osem)
    back.start()
    near.wait()

    @pl.loop(0, 3)
    def _(q):
        pltpu.make_async_copy(c0, cb.at[q], csem.at[q]).wait()
        for i in range(2):
            b = 2 * q + i
            cent = cb[q, i * BS : (i + 1) * BS, :]
            e, peak, lse = score_chunk(cent, half_norm(cent), jnp.concatenate([xa[b], x67[b]], axis=0))
            ea[b] = e
            peak_ref[pl.ds(b, 1), 512:768] = peak
            lse_scr[pl.ds(b, 1), 512:768] = lse
            pltpu.make_async_copy(ea.at[b], e_out.at[b, :, pl.ds(512, 256)], esem.at[b]).start()

    cents[3].wait()
    far_rows.wait()
    for i in range(2):
        b = 6 + i
        cent = cb[3, i * BS : (i + 1) * BS, :]
        norm = half_norm(cent)
        chunks = (xb[i, 0:256, :], xb[i, 256:512, :], jnp.concatenate([xb[i, 512:576, :], x67[b]], axis=0))
        for k, rows in enumerate(chunks):
            e, peak, lse = score_chunk(cent, norm, rows)
            eb[i, :, k * 256 : (k + 1) * 256] = e
            peak_ref[b : b + 1, k * 256 : (k + 1) * 256] = peak
            lse_scr[b : b + 1, k * 256 : (k + 1) * 256] = lse
        pltpu.make_async_copy(eb.at[i], e_out.at[b], esem.at[b]).start()

    sources = [(ref, k) for ref in (rank0, rank1, rank2, rank_ref) for k in range(ref.shape[0])]
    for s, (ref, k) in enumerate(sources):
        k0, k1 = s * MOST // 128, (s * MOST + MOST - 1) // 128
        for j in range(TOK // 128):
            r = ref[k, :, j * 128 : (j + 1) * 128].astype(jnp.int32)
            at = r + s * MOST
            low = at & 127
            got = jnp.take_along_axis(lse_scr[:, k0 * 128 : (k0 + 1) * 128], low, axis=1, mode="promise_in_bounds")
            if k1 > k0:
                other = jnp.take_along_axis(
                    lse_scr[:, k1 * 128 : (k1 + 1) * 128], low, axis=1, mode="promise_in_bounds"
                )
                got = jnp.where((at >> 7) == k0, got, other)
            got = jnp.where(r >= 0, got, LOW)
            m = jnp.max(got, axis=0, keepdims=True)
            t = jnp.sum(jnp.exp(got - m), axis=0, keepdims=True)
            stat_ref[s : s + 1, j * 128 : (j + 1) * 128] = m + jnp.log(t)

    back.wait()
    for b in range(6):
        pltpu.make_async_copy(ea.at[b], e_out.at[b, :, pl.ds(512, 256)], esem.at[b]).wait()
    for i in range(2):
        pltpu.make_async_copy(eb.at[i], e_out.at[6 + i], esem.at[6 + i]).wait()


def late_scores(sources, blk, cents, ranked, peak0, lse0, rows, e):
    anywhere, hbm = pl.BlockSpec(memory_space=pl.ANY), pl.BlockSpec(memory_space=pltpu.HBM)
    vmem = pl.BlockSpec(memory_space=pltpu.VMEM)
    return pl.pallas_call(
        late_kernel,
        in_specs=[anywhere] * 2 + [vmem] + [anywhere] * 4 + [vmem] * 5 + [hbm] * 2,
        out_specs=(hbm, hbm, vmem, vmem, vmem),
        out_shape=(
            jax.ShapeDtypeStruct(ROWS, BF16),
            jax.ShapeDtypeStruct(SCORES, BF16),
            jax.ShapeDtypeStruct((2, NBLK, TOK), F32),
            jax.ShapeDtypeStruct((NBLK, SLOTS), F32),
            jax.ShapeDtypeStruct((NSRC, TOK), F32),
        ),
        scratch_shapes=[
            pltpu.VMEM((2, EXT, D), BF16),
            pltpu.VMEM((6, 64, D), BF16),
            pltpu.VMEM((2, 576, D), BF16),
            pltpu.VMEM((NBLK, 2 * MOST, D), BF16),
            pltpu.VMEM((4, 1024, D), BF16),
            pltpu.VMEM((6, BS, 256), BF16),
            pltpu.VMEM((2, BS, SLOTS), BF16),
            pltpu.VMEM((NBLK, SLOTS), F32),
            pltpu.SemaphoreType.DMA((2,)),
            pltpu.SemaphoreType.DMA((4,)),
            pltpu.SemaphoreType.DMA((2,)),
            pltpu.SemaphoreType.DMA,
            pltpu.SemaphoreType.DMA((8,)),
        ],
        input_output_aliases={12: 0, 13: 1},
        compiler_params=params(34),
        cost_estimate=cost(2 * 6 * BS * SLOTS * D, 20e6, 4 * BS * SLOTS),
        name="late_scores",
    )(*sources, blk, *cents, *ranked, peak0, lse0, rows, e)


def factor_kernel(stat_refs, idx_ref, peak_ref, f_scr):
    own, from_d, from_e, from_f = stat_refs
    tables = []
    for s in range(NSRC):
        parts = [own[s : s + 1, :]]
        for ref, order in ((from_d, FROM_D), (from_e, FROM_E), (from_f, FROM_F)):
            parts.append(ref[order[s] : order[s] + 1, :])
        m = jnp.maximum(jnp.maximum(parts[0], parts[1]), jnp.maximum(parts[2], parts[3]))
        t = jnp.exp(parts[0] - m)
        for k in range(1, 4):
            t = t + jnp.exp(parts[k] - m)
        tables.append(m + jnp.log(t))
    for k in range(SLOTS // 128):
        at = idx_ref[:, k * 128 : (k + 1) * 128]
        low = at & 127
        high = at >> 7
        lse = jnp.zeros((NBLK, 128), F32)
        for s in range(k * 128 // MOST, (k * 128 + 127) // MOST + 1):
            for j in range(TOK // 128):
                table = jnp.broadcast_to(tables[s][:, j * 128 : (j + 1) * 128], (NBLK, 128))
                got = jnp.take_along_axis(table, low, axis=1, mode="promise_in_bounds")
                lse = jnp.where(high == s * (TOK // 128) + j, got, lse)
        f = jnp.exp(peak_ref[:, k * 128 : (k + 1) * 128] - lse)
        f_scr[:, k * 128 : (k + 1) * 128] = jnp.where(at >= 0, f, 0.0)


def sums_owner(i):
    t = i % 4
    return jnp.where(t == 0, 3, jnp.where(t == 3, 0, t))


def sums_kernel(where_ref, s0, s1, s2, s3, idx_any, peak_any, e_any, rows_any, *refs):
    outs, (f_scr, hbuf, gbuf, gcount, gtile, stats, idx_ref, peak_ref, e_buf, rows_buf, hsem, gsem, tsem, ssem, esem, rsem) = refs[:8], refs[8:]
    i = pl.program_id(0)
    q, slot = sums_owner(i), i % 2

    def send_h(k, slot=slot):
        return pltpu.make_async_copy(hbuf.at[slot], outs[k], hsem.at[slot])

    def send_g(k, slot=slot):
        start = pl.multiple_of(q * 128, 128)
        return pltpu.make_async_copy(gbuf.at[slot, k], outs[4 + k].at[pl.ds(start, 128), :], gsem.at[slot, k])

    def send_tile(k):
        return pltpu.make_async_copy(gtile.at[k], outs[4 + k].at[pl.ds(BS, EXTRA), :], tsem.at[k])

    def load_block(k):
        b = 2 * sums_owner(k) + k // 4
        pltpu.make_async_copy(e_any.at[b], e_buf.at[k], esem.at[k]).start()
        pltpu.make_async_copy(rows_any.at[b], rows_buf.at[k], rsem.at[k]).start()

    @pl.when(i == 0)
    def _():
        loads = [pltpu.make_async_copy(s, stats.at[k], ssem.at[k]) for k, s in enumerate((s0, s1, s2, s3))]
        loads.append(pltpu.make_async_copy(idx_any, idx_ref, ssem.at[4]))
        loads.append(pltpu.make_async_copy(peak_any, peak_ref, ssem.at[5]))
        for load in loads:
            load.start()
        for k in range(2):
            load_block(k)
        for load in loads:
            load.wait()
        factor_kernel([stats.at[k] for k in range(4)], idx_ref, peak_ref, f_scr)
        gcount[...] = jnp.zeros_like(gcount)

    @pl.when(i < 6)
    def _():
        load_block(i + 2)

    f = f_scr[pl.ds(2 * q + i // 4, 1), :]
    pltpu.make_async_copy(e_any.at[0], e_buf.at[i], esem.at[i]).wait()
    pltpu.make_async_copy(rows_any.at[0], rows_buf.at[i], rsem.at[i]).wait()
    totals, counts = [], []
    for m in range(4):
        w = e_buf[i, m * 128 : (m + 1) * 128, :].astype(F32) * f
        count = jnp.sum(w, axis=1, keepdims=True)
        counts.append(jnp.transpose(jnp.broadcast_to(count, (128, 128)))[0:EXTRA])
        totals.append(jnp.dot(w.astype(BF16), rows_buf[i], preferred_element_type=F32).astype(BF16))

    @pl.when((i == 2) | (i == 3))
    def _():
        send_h(0).wait()

    @pl.when((i == 6) | (i == 7))
    def _():
        for k in range(4):
            send_g(k).wait()

    @pl.when(i < 4)
    def _():
        for m in range(4):
            hbuf[slot, m * 128 : (m + 1) * 128, :] = totals[m]
        tile = jnp.concatenate([*counts, jnp.zeros((EXTRA, D - BS), F32)], axis=1)
        hbuf[slot, BS : BS + EXTRA, :] = tile.astype(BF16)
        for k in range(4):
            @pl.when(q == k)
            def _(k=k):
                send_h(k).start()

    @pl.when(i >= 4)
    def _():
        for m in range(4):
            at = sum(jnp.where(where_ref[4 + k] == m, k, 0) for k in range(1, 4))
            gbuf[slot, at] = totals[m]
            gcount[at, pl.ds(q, 1), :] = counts[m][0:1]
        for k in range(4):
            send_g(k).start()

    @pl.when(i == 7)
    def _():
        for k in range(4):
            tile = jnp.concatenate([gcount[k], jnp.zeros((8, 128), F32)], axis=0)
            tile = jnp.concatenate([tile, jnp.zeros((EXTRA, D - 128), F32)], axis=1)
            gtile[k] = tile.astype(BF16)
            send_tile(k).start()
        for other in range(2):
            send_h(0, other).wait()
            for k in range(4):
                send_g(k, other).wait()
        for k in range(4):
            send_tile(k).wait()


def sums(where, stats, idx, peak, e, rows):
    shape = (BS + EXTRA, D)
    out = pl.pallas_call(
        sums_kernel,
        grid=(8,),
        in_specs=[pl.BlockSpec(memory_space=pltpu.SMEM)]
        + [pl.BlockSpec(memory_space=pl.ANY)] * 6
        + [pl.BlockSpec(memory_space=pltpu.HBM)] * 2,
        out_specs=tuple([pl.BlockSpec(memory_space=pl.ANY)] * 8),
        out_shape=tuple([jax.ShapeDtypeStruct(shape, BF16)] * 8),
        scratch_shapes=[
            pltpu.VMEM((NBLK, SLOTS), F32),
            pltpu.VMEM((2, *shape), BF16),
            pltpu.VMEM((2, 4, 128, D), BF16),
            pltpu.VMEM((4, 8, 128), F32),
            pltpu.VMEM((4, EXTRA, D), BF16),
            pltpu.VMEM((4, NSRC, TOK), F32),
            pltpu.VMEM((NBLK, SLOTS), jnp.int32),
            pltpu.VMEM((NBLK, SLOTS), F32),
            pltpu.VMEM((NBLK, BS, SLOTS), BF16),
            pltpu.VMEM((NBLK, SLOTS, D), BF16),
            pltpu.SemaphoreType.DMA((2,)),
            pltpu.SemaphoreType.DMA((2, 4)),
            pltpu.SemaphoreType.DMA((4,)),
            pltpu.SemaphoreType.DMA((6,)),
            pltpu.SemaphoreType.DMA((8,)),
            pltpu.SemaphoreType.DMA((8,)),
        ],
        compiler_params=params(54),
        cost_estimate=cost(2 * 8 * BS * SLOTS * D, 24e6),
        name="sums",
    )(where, *stats, idx, peak, e, rows)
    return out[:4], out[4:]


def fetched(refs, buf, sem):
    copies = [pltpu.make_async_copy(ref, buf.at[k], sem.at[k]) for k, ref in enumerate(refs)]
    for copy in copies:
        copy.start()
    for copy in copies:
        copy.wait()
    return [buf.at[k] for k in range(len(refs))]


def parted_kernel(where_ref, *refs):
    outs, (acc, buf, sem) = refs[6:14], refs[14:]
    h0, h1, h2, g0, g1, g2 = fetched(refs[:6], buf, sem)

    def tile(counts):
        counts = jnp.broadcast_to(counts, (EXTRA, 128))
        return jnp.concatenate([counts, jnp.zeros((EXTRA, D - 128), F32)], axis=1).astype(BF16)

    acc[...] = h0[...].astype(F32) + h1[...].astype(F32) + h2[...].astype(F32)
    counts = acc[BS : BS + 8, 0:BS]
    for k in range(4):
        part = where_ref[4 + k]
        outs[k][0:128, :] = acc[pl.ds(pl.multiple_of(part * 128, 128), 128), :].astype(BF16)
        picked = counts[:, 0:128]
        for m in range(1, 4):
            picked = jnp.where(part == m, counts[:, m * 128 : (m + 1) * 128], picked)
        outs[k][128:, :] = tile(picked[0:1])
    counts = g0[BS:, 0:128].astype(F32) + g1[BS:, 0:128].astype(F32) + g2[BS:, 0:128].astype(F32)
    for k in range(4):
        rows = slice(k * 128, (k + 1) * 128)
        total = g0[rows, :].astype(F32) + g1[rows, :].astype(F32) + g2[rows, :].astype(F32)
        outs[4 + k][0:128, :] = total.astype(BF16)
        outs[4 + k][128:, :] = tile(counts[k : k + 1])


def parted(where, h, g):
    vmem = pl.BlockSpec(memory_space=pltpu.VMEM)
    out = pl.pallas_call(
        parted_kernel,
        in_specs=[pl.BlockSpec(memory_space=pltpu.SMEM)] + [pl.BlockSpec(memory_space=pl.ANY)] * 6,
        out_specs=(vmem,) * 8,
        out_shape=(jax.ShapeDtypeStruct((128 + EXTRA, D), BF16),) * 8,
        scratch_shapes=[
            pltpu.VMEM((BS + EXTRA, D), F32),
            pltpu.VMEM((6, BS + EXTRA, D), BF16),
            pltpu.SemaphoreType.DMA((6,)),
        ],
        compiler_params=params(16),
        cost_estimate=cost(1e6, 8e6),
        name="parted",
    )(where, *h, *g)
    return out[:4], out[4:]


def final_kernel(*refs):
    mine_ref, out_ref, buf, sem = refs[8:]
    h0, h1, h2, h3, g0, g1, g2, g3 = fetched(refs[:8], buf, sem)
    for i, refs in enumerate(((h0, h1, h2, h3), (g0, g1, g2, g3))):
        total = (refs[0][...].astype(F32) + refs[1][...].astype(F32)) + (refs[2][...].astype(F32) + refs[3][...].astype(F32))
        column = jnp.transpose(jnp.broadcast_to(total[128:129, 0:128], (128, 128)))[:, 0:1]
        out_ref[i] = ((total[0:128] + mine_ref[i].astype(F32)) / (column + 1.0)).astype(BF16)


def final(h, g, mine):
    return pl.pallas_call(
        final_kernel,
        in_specs=[pl.BlockSpec(memory_space=pl.ANY)] * 8 + [pl.BlockSpec(memory_space=pltpu.VMEM)],
        out_specs=pl.BlockSpec(memory_space=pltpu.VMEM),
        out_shape=jax.ShapeDtypeStruct((2, 128, D), BF16),
        scratch_shapes=[pltpu.VMEM((8, 128 + EXTRA, D), BF16), pltpu.SemaphoreType.DMA((8,))],
        compiler_params=params(8),
        cost_estimate=cost(1e6, 2e6),
        name="final",
    )(*h, *g, mine)


def place_kernel(where_ref, *refs):
    parts, (out_ref, buf, in_sem, out_sem) = refs[:8], refs[8:]
    loads = [pltpu.make_async_copy(part, buf.at[k], in_sem.at[k]) for k, part in enumerate(parts)]
    copies = []
    for side in range(2):
        for k in range(4):
            for i in range(2):
                block = where_ref[8 + side] * 2 + i
                quarter = where_ref[4 * side + k]
                copies.append(
                    pltpu.make_async_copy(
                        buf.at[side * 4 + k, i], out_ref.at[block, quarter], out_sem.at[len(copies)]
                    )
                )
    for load in loads:
        load.start()
    for k, load in enumerate(loads):
        load.wait()
        copies[2 * k].start()
        copies[2 * k + 1].start()
    for copy in copies:
        copy.wait()


def place(where, parts):
    return pl.pallas_call(
        place_kernel,
        in_specs=[pl.BlockSpec(memory_space=pltpu.SMEM)] + [pl.BlockSpec(memory_space=pl.ANY)] * 8,
        out_specs=pl.BlockSpec(memory_space=pl.ANY),
        out_shape=jax.ShapeDtypeStruct((4, 4, 128, D), BF16),
        scratch_shapes=[
            pltpu.VMEM((8, 2, 128, D), BF16),
            pltpu.SemaphoreType.DMA((8,)),
            pltpu.SemaphoreType.DMA((16,)),
        ],
        compiler_params=params(8),
        cost_estimate=cost(0, 6e6),
        name="place",
    )(where, *parts)


def tie(a, *after):
    return pl.pallas_call(
        lambda *refs: None,
        in_specs=[pl.BlockSpec(memory_space=pl.ANY)] * (1 + len(after)),
        out_specs=pl.BlockSpec(memory_space=pl.ANY),
        out_shape=jax.ShapeDtypeStruct(a.shape, a.dtype),
        input_output_aliases={0: 0},
        compiler_params=params(8),
        cost_estimate=cost(0, 0),
        name="tie",
    )(a, *after)


def add(*terms):
    total = terms[0].astype(F32)
    for t in terms[1:]:
        total = total + t.astype(F32)
    return total


def ring_terms(own, d, e, f, axis):
    r1 = turn(f, axis, 1)
    r2 = turn(d, axis, -1)
    r3 = turn(add(e, r1).astype(BF16), axis, 1)
    return own, r2, r3


def direct_terms(own, d, e, f, axis):
    return own, turn(d, axis, -1), turn(e, axis, 1), far(f, axis)


def body(vectors, centroids, candidates):
    core, x, y, z = (lax.axis_index(a) for a in ("core", "x", "y", "z"))
    step = 1 - 2 * core

    def around(i):
        return jnp.stack([i, (i - step) % 4, (i + step) % 4, (i + 2) % 4]).astype(jnp.int32)

    xs, zs = around(x), around(z)
    other_zs = jnp.stack([zs[0], zs[2], zs[1], zs[3]])

    where = jnp.concatenate([xs, zs])
    tail = jnp.pad(candidates.T.reshape(8, 512).astype(BF16), ((0, EXTRA - 8), (0, D - 512)))
    v = jnp.concatenate([vectors, tail])
    a, b = turn(v, "y", 1), turn(v, "y", -1)
    c0 = lax.dynamic_slice_in_dim(centroids, core * 1024, 1024, 0)
    c1, c2 = turn(c0, "x", 1), turn(c0, "x", -1)
    mine = lax.dynamic_slice_in_dim(c0.reshape(2, BS, D), z * 128, 128, 1)
    blk = ((y * 4 + xs) * 4 + 2 * core)[:, None] + jnp.arange(2, dtype=jnp.int32)[None, :]
    blk = jnp.broadcast_to(blk.reshape(NBLK, 1), (NBLK, 128)).astype(F32)

    rank0, rows = dispatch(0, (v, swap(v)), blk, None)
    a = tie(a, rank0, b, c1, c2)
    c = turn(a, "y", 1)
    c3 = turn(c1, "x", 1)
    rank1, rows = dispatch(2, (a, b), blk, rows)
    rows, rank2, e, peak0, lse0 = middle((swap(a), swap(b)), blk, (c0, c1, c2), rows)
    c = tie(c, lse0, c3)
    ranked = (rank0, rank1, rank2)
    rows, e, rank3, peak, stat = late_scores((c, swap(c)), blk, (c0, c1, c2, c3), ranked, peak0, lse0, rows, e)
    idx = indices(*ranked, rank3)

    theirs = swap(stat)
    theirs = jnp.concatenate([theirs[s : s + 1] for s in SWAPPED])
    m = jnp.maximum(stat, theirs)
    merged = m + jnp.log(jnp.exp(stat - m) + jnp.exp(theirs - m))
    stats = (merged, turn(merged, "y", 1), turn(merged, "y", -1), far(merged, "y"))

    h, g = sums(where, stats, idx, peak, e, rows)
    h, g = ring_terms(*h, "x"), ring_terms(*g, "z")
    h, g = parted(where, h, g)
    h, g = direct_terms(*h, "z"), direct_terms(*g, "x")
    fresh = final(h, g, mine)

    others = [turn(fresh, "z", 1), turn(fresh, "z", -1), far(fresh, "z")]
    parts = [fresh, *others] + [swap(p) for p in (fresh, *others)]
    places = jnp.concatenate([zs, other_zs, jnp.stack([core, 1 - core])]).astype(jnp.int32)
    return place(places, parts).reshape(2048, D)


def solution(mesh):
    fine = Mesh(np.asarray(mesh.devices).reshape(4, 2, 4, 4), ("z", "core", "y", "x"))
    return jax.shard_map(
        body,
        mesh=fine,
        in_specs=(P(("z", "core", "y", "x"), None), P(("y", "x"), None), P(("z", "core", "y", "x"), None)),
        out_specs=P(("y", "x"), None),
        check_vma=False,
    )
```

```python
import jax
import jax.numpy as jnp
import numpy as np
from jax import lax
from jax.experimental import pallas as pl
from jax.experimental.pallas import tpu as pltpu
from jax.sharding import Mesh, PartitionSpec as P

BS = 512
MOST = 96
TOK = 1024
D = 768
NSRC = 8
NBLK = 8
SLOTS = NSRC * MOST
EXTRA = 16
EXT = TOK + EXTRA
ROWS = (28, SLOTS, D)
SCORES = (40, BS, SLOTS)
LOW = -1e30
F32 = jnp.float32
BF16 = jnp.bfloat16

NAMES = ("v", "v'", "a", "b", "a'", "b'", "c", "c'")


def order(**came):
    return tuple(NAMES.index(came[n.replace("'", "_")]) for n in NAMES)


SWAPPED = order(v="v'", v_="v", a="a'", a_="a", b="b'", b_="b", c="c'", c_="c")
FROM_D = order(a="v", b_="v'", c="a", v_="a'", v="b", c_="b'", b="c", a_="c'")
FROM_E = order(b="v", a_="v'", v="a", c_="a'", c="b", v_="b'", a="c", b_="c'")
FROM_F = order(c="v", c_="v'", b="a", b_="a'", a="b", a_="b'", v="c", v_="c'")


def turn(a, axis, sign):
    axes = ("z", "core") if axis == "z" else ("core", axis)
    at = (lambda core, i: i * 2 + core) if axis == "z" else (lambda core, i: core * 4 + i)
    pairs = []
    for core in range(2):
        for i in range(4):
            pairs.append((at(core, i), at(core, (i + (sign if core == 0 else -sign)) % 4)))
    return lax.ppermute(a, axes, pairs)


def far(a, axis):
    return lax.ppermute(a, axis, [(i, (i + 2) % 4) for i in range(4)])


def swap(a):
    return lax.ppermute(a, "core", [(0, 1), (1, 0)])


def params(mib):
    return pltpu.CompilerParams(vmem_limit_bytes=mib * 1024 * 1024)


def cost(flops, nbytes, trans=0):
    return pl.CostEstimate(flops=int(flops), bytes_accessed=int(nbytes), transcendentals=int(trans))


def earlier():
    up = lax.broadcasted_iota(jnp.int32, (TOK, TOK), 0) < lax.broadcasted_iota(jnp.int32, (TOK, TOK), 1)
    return jnp.where(up, 1.0, 0.0).astype(BF16)


def pack_kernel(vectors, cand_ref, out, buf, in_sem, out_sem):
    loads, stores = [], []
    for k in range(4):
        rows = pl.ds(k * 256, 256)
        loads.append(pltpu.make_async_copy(vectors.at[rows, :], buf.at[rows, :], in_sem.at[k]))
        stores.append(pltpu.make_async_copy(buf.at[rows, :], out.at[rows, :], out_sem.at[k]))
        loads[k].start()
    cand = cand_ref[...].astype(F32)
    halves = [cand[pick : pick + 1, h * 512 : (h + 1) * 512] for pick in range(4) for h in range(2)]
    tail = jnp.concatenate([*halves, jnp.zeros((EXTRA - 8, 512), F32)], axis=0)
    tail = jnp.concatenate([tail, jnp.zeros((EXTRA, D - 512), F32)], axis=1)
    buf[TOK:EXT, :] = tail.astype(BF16)
    end = pltpu.make_async_copy(buf.at[pl.ds(TOK, EXTRA), :], out.at[pl.ds(TOK, EXTRA), :], out_sem.at[4])
    end.start()
    for load, store in zip(loads, stores):
        load.wait()
        store.start()
    for store in (*stores, end):
        store.wait()


def pack(vectors, cand):
    anywhere = pl.BlockSpec(memory_space=pl.ANY)
    return pl.pallas_call(
        pack_kernel,
        in_specs=[anywhere, pl.BlockSpec(memory_space=pltpu.VMEM)],
        out_specs=anywhere,
        out_shape=jax.ShapeDtypeStruct((EXT, D), BF16),
        scratch_shapes=[
            pltpu.VMEM((EXT, D), BF16),
            pltpu.SemaphoreType.DMA((4,)),
            pltpu.SemaphoreType.DMA((5,)),
        ],
        compiler_params=params(60),
        cost_estimate=cost(0, 3e6),
        name="pack",
    )(vectors, cand)


def ranks(tail, blk, up):
    tail = tail.astype(F32)
    hit = None
    for pick in range(4):
        named = jnp.concatenate([tail[2 * pick : 2 * pick + 1, 0:512], tail[2 * pick + 1 : 2 * pick + 2, 0:512]], axis=1)
        m = named == blk
        hit = m if hit is None else hit | m
    hit = jnp.where(hit, 1.0, 0.0)
    hits = jnp.concatenate([hit, jnp.zeros((8, TOK), F32)], axis=0).astype(BF16)
    before = jnp.dot(hits, up, preferred_element_type=F32)[0:NBLK]
    return jnp.where(hit > 0, before, -1.0)


def gathered(rank, vectors):
    slot = lax.broadcasted_iota(jnp.int32, (MOST, TOK), 0).astype(F32)
    hot = [jnp.where(slot == rank[b : b + 1, :], 1.0, 0.0).astype(BF16) for b in range(NBLK)]
    hot = jnp.concatenate(hot, axis=0)
    rows = jnp.dot(hot, vectors, preferred_element_type=F32).astype(BF16)
    return rows.reshape(NBLK, MOST, D)


def index_kernel(pieces, *refs):
    rank_refs, idx_ref = refs[:-1], refs[-1]
    sources = [(ref, k) for ref in rank_refs for k in range(ref.shape[0])]
    row = lax.broadcasted_iota(jnp.int32, (8, TOK), 0)
    v = lax.broadcasted_iota(jnp.int32, (8, TOK), 1)
    place = jnp.where(row == 0, v >> 3, jnp.where(row == 1, v & 7, jnp.where(row == 2, 1, 0)))
    place = place.astype(F32).astype(BF16)
    lane = lax.broadcasted_iota(jnp.int32, (1, idx_ref.shape[1]), 1)
    base, end = jnp.zeros(lane.shape, F32), 0
    for s, _, lo, hi in pieces:
        base = jnp.where(lane >= end, float(s * TOK), base)
        end += hi - lo
    for b in range(NBLK):
        hot = []
        for _, at, lo, hi in pieces:
            ref, k = sources[at]
            slot = (lax.broadcasted_iota(jnp.int32, (hi - lo, TOK), 0) + lo).astype(F32)
            hot.append(jnp.where(slot == ref[k, b : b + 1, :], 1.0, 0.0).astype(BF16))
        hot = jnp.concatenate(hot, axis=0)
        found = lax.dot_general(place, hot, (((1,), (1,)), ((), ())), preferred_element_type=F32)
        where = found[0:1] * 8.0 + found[1:2] + base
        idx_ref[b : b + 1, :] = jnp.where(found[2:3] > 0, where, -1.0).astype(jnp.int32)


def indices(ranked, pieces):
    def kern(*refs):
        index_kernel(pieces, *refs)

    width = sum(hi - lo for _, _, lo, hi in pieces)
    return pl.pallas_call(
        kern,
        out_shape=jax.ShapeDtypeStruct((NBLK, width), jnp.int32),
        compiler_params=params(12),
        cost_estimate=cost(4e9, 1e6),
        name="indices",
    )(*ranked)


def dispatch_kernel(n, *refs):
    sources, blk_ref, (rank_ref, out_ref, buf, sems, up) = refs[:n], refs[n], refs[-5:]
    i = pl.program_id(0)

    def copy(k):
        return pltpu.make_async_copy(sources[k], buf.at[k % 2], sems.at[k % 2])

    @pl.when(i == 0)
    def _():
        copy(0).start()
        up[...] = earlier()

    for k in range(n):
        @pl.when(i == k)
        def _(k=k):
            if k + 1 < n:
                copy(k + 1).start()
            copy(k).wait()

    rank = ranks(buf[i % 2, TOK:EXT, :], blk_ref[:, 0:1], up[...])
    rank_ref[0] = rank
    out_ref[...] = gathered(rank, buf[i % 2, 0:TOK, :])


def dispatch(first, sources, blk, rows):
    n = len(sources)
    anywhere = pl.BlockSpec(memory_space=pl.ANY)
    in_specs = [anywhere] * n + [pl.BlockSpec((NBLK, 128), lambda i: (0, 0))]
    args = [*sources, blk]
    alias = {}
    if rows is not None:
        in_specs.append(pl.BlockSpec(memory_space=pltpu.HBM))
        args.append(rows)
        alias = {n + 1: 1}

    def kern(*refs):
        dispatch_kernel(n, *refs)

    return pl.pallas_call(
        kern,
        grid=(n,),
        in_specs=in_specs,
        out_specs=(
            pl.BlockSpec((1, NBLK, TOK), lambda i: (i, 0, 0)),
            pl.BlockSpec((NBLK, MOST, D), lambda i: (0, first + i, 0)),
        ),
        out_shape=(
            jax.ShapeDtypeStruct((n, NBLK, TOK), F32),
            jax.ShapeDtypeStruct(ROWS, BF16),
        ),
        scratch_shapes=[
            pltpu.VMEM((2, EXT, D), BF16),
            pltpu.SemaphoreType.DMA((2,)),
            pltpu.VMEM((TOK, TOK), BF16),
        ],
        input_output_aliases=alias,
        compiler_params=params(34),
        cost_estimate=cost(2 * n * NBLK * MOST * TOK * D, n * 3e6),
        name=f"dispatch{first}",
    )(*args)


def half_norm(cent):
    wide = cent.astype(F32)
    return 0.5 * jnp.sum(wide * wide, axis=1, keepdims=True)


def score_chunk(cent, norm, rows):
    raw = lax.dot_general(cent, rows, (((1,), (1,)), ((), ())), preferred_element_type=F32)
    score = raw - norm
    peak = jnp.max(score, axis=0, keepdims=True)
    e = jnp.exp(score - peak)
    return e.astype(BF16), peak, peak + jnp.log(jnp.sum(e, axis=0, keepdims=True))


def middle_kernel(
    s0, s1, blk_ref, c0, c1, c2, rows_in,
    rows_out, rank_ref, e_out, peak_ref, lse_ref,
    vbuf, x03, x45, cb, eb, vsem, csem, xsem, osem, esem,
):
    sources = [pltpu.make_async_copy(s, vbuf.at[k], vsem.at[k]) for k, s in enumerate((s0, s1))]
    cents = [pltpu.make_async_copy(c, cb.at[k], csem.at[k]) for k, c in enumerate((c0, c1, c2))]
    first = pltpu.make_async_copy(rows_in.at[pl.ds(0, 6), pl.ds(0, 384), :], x03, xsem)
    for copy in sources:
        copy.start()
    up = earlier()
    for k in range(2):
        sources[k].wait()
        for copy in (first, cents[0]) if k == 0 else cents[1:]:
            copy.start()
        rank = ranks(vbuf[k, TOK:EXT, :], blk_ref[:, 0:1], up)
        rank_ref[k] = rank
        x45[:, k * MOST : (k + 1) * MOST, :] = gathered(rank, vbuf[k, 0:TOK, :])
    back = pltpu.make_async_copy(x45, rows_out.at[pl.ds(0, NBLK), pl.ds(384, 192), :], osem)
    back.start()
    first.wait()
    for q in range(3):
        cents[q].wait()
        for i in range(2):
            b = 2 * q + i
            cent = cb[q, i * BS : (i + 1) * BS, :]
            norm = half_norm(cent)
            chunks = (x03[b, 0:256, :], jnp.concatenate([x03[b, 256:384, :], x45[b, 0:128, :]], axis=0))
            for k, rows in enumerate(chunks):
                e, peak, lse = score_chunk(cent, norm, rows)
                eb[b, :, k * 256 : (k + 1) * 256] = e
                peak_ref[b : b + 1, k * 256 : (k + 1) * 256] = peak
                lse_ref[b : b + 1, k * 256 : (k + 1) * 256] = lse
            pltpu.make_async_copy(eb.at[b], e_out.at[b, :, pl.ds(0, 512)], esem.at[b]).start()
    back.wait()
    for b in range(6):
        pltpu.make_async_copy(eb.at[b], e_out.at[b, :, pl.ds(0, 512)], esem.at[b]).wait()


def middle(sources, blk, cents, rows):
    anywhere, hbm = pl.BlockSpec(memory_space=pl.ANY), pl.BlockSpec(memory_space=pltpu.HBM)
    vmem = pl.BlockSpec(memory_space=pltpu.VMEM)
    return pl.pallas_call(
        middle_kernel,
        in_specs=[anywhere] * 2 + [vmem] + [anywhere] * 3 + [hbm],
        out_specs=(hbm, vmem, hbm, vmem, vmem),
        out_shape=(
            jax.ShapeDtypeStruct(ROWS, BF16),
            jax.ShapeDtypeStruct((2, NBLK, TOK), F32),
            jax.ShapeDtypeStruct(SCORES, BF16),
            jax.ShapeDtypeStruct((NBLK, 512), F32),
            jax.ShapeDtypeStruct((NBLK, 512), F32),
        ),
        scratch_shapes=[
            pltpu.VMEM((2, EXT, D), BF16),
            pltpu.VMEM((6, 384, D), BF16),
            pltpu.VMEM((NBLK, 192, D), BF16),
            pltpu.VMEM((3, 1024, D), BF16),
            pltpu.VMEM((6, BS, 512), BF16),
            pltpu.SemaphoreType.DMA((2,)),
            pltpu.SemaphoreType.DMA((3,)),
            pltpu.SemaphoreType.DMA,
            pltpu.SemaphoreType.DMA,
            pltpu.SemaphoreType.DMA((6,)),
        ],
        input_output_aliases={6: 0},
        compiler_params=params(34),
        cost_estimate=cost(4 * NBLK * MOST * TOK * D, 20e6, 6 * BS * 512),
        name="middle",
    )(*sources, blk, *cents, rows)


def late_kernel(
    source, blk_ref, c0, c1, c2, c3, rank0, rank1, rank2, rank3, peak0, lse0, rows_in, e_in,
    rows_out, e_out, rank_ref, peak_ref, stat_ref,
    vbuf, xa, xb, x7, cb, ea, eb, lse_scr, vsem, csem, xsem, osem, esem,
):
    load = pltpu.make_async_copy(source, vbuf, vsem)
    near = pltpu.make_async_copy(rows_in.at[pl.ds(0, 6), pl.ds(512, 160), :], xa, xsem.at[0])
    far_rows = pltpu.make_async_copy(rows_in.at[pl.ds(6, 2), pl.ds(0, 672), :], xb, xsem.at[1])
    cents = [pltpu.make_async_copy(c, cb.at[k], csem.at[k]) for k, c in enumerate((c0, c1, c2, c3))]
    load.start()
    peak_ref[:, 0:512] = peak0[...]
    lse_scr[:, 0:512] = lse0[...]
    up = earlier()
    load.wait()
    for copy in (near, *cents, far_rows):
        copy.start()
    rank = ranks(vbuf[TOK:EXT, :], blk_ref[:, 0:1], up)
    rank_ref[0] = rank
    x7[...] = gathered(rank, vbuf[0:TOK, :])
    back = pltpu.make_async_copy(x7, rows_out.at[pl.ds(0, NBLK), pl.ds(672, MOST), :], osem)
    back.start()
    near.wait()

    @pl.loop(0, 3)
    def _(q):
        pltpu.make_async_copy(c0, cb.at[q], csem.at[q]).wait()
        for i in range(2):
            b = 2 * q + i
            cent = cb[q, i * BS : (i + 1) * BS, :]
            e, peak, lse = score_chunk(cent, half_norm(cent), jnp.concatenate([xa[b], x7[b]], axis=0))
            ea[b] = e
            peak_ref[pl.ds(b, 1), 512:768] = peak
            lse_scr[pl.ds(b, 1), 512:768] = lse
            pltpu.make_async_copy(ea.at[b], e_out.at[b, :, pl.ds(512, 256)], esem.at[b]).start()

    cents[3].wait()
    far_rows.wait()
    for i in range(2):
        b = 6 + i
        cent = cb[3, i * BS : (i + 1) * BS, :]
        norm = half_norm(cent)
        chunks = (xb[i, 0:256, :], xb[i, 256:512, :], jnp.concatenate([xb[i, 512:672, :], x7[b]], axis=0))
        for k, rows in enumerate(chunks):
            e, peak, lse = score_chunk(cent, norm, rows)
            eb[i, :, k * 256 : (k + 1) * 256] = e
            peak_ref[b : b + 1, k * 256 : (k + 1) * 256] = peak
            lse_scr[b : b + 1, k * 256 : (k + 1) * 256] = lse
        pltpu.make_async_copy(eb.at[i], e_out.at[b], esem.at[b]).start()

    sources = [(ref, k) for ref in (rank0, rank1, rank2, rank3, rank_ref) for k in range(ref.shape[0])]
    for s, (ref, k) in enumerate(sources):
        k0, k1 = s * MOST // 128, (s * MOST + MOST - 1) // 128
        for j in range(TOK // 128):
            r = ref[k, :, j * 128 : (j + 1) * 128].astype(jnp.int32)
            at = r + s * MOST
            low = at & 127
            got = jnp.take_along_axis(lse_scr[:, k0 * 128 : (k0 + 1) * 128], low, axis=1, mode="promise_in_bounds")
            if k1 > k0:
                other = jnp.take_along_axis(
                    lse_scr[:, k1 * 128 : (k1 + 1) * 128], low, axis=1, mode="promise_in_bounds"
                )
                got = jnp.where((at >> 7) == k0, got, other)
            got = jnp.where(r >= 0, got, LOW)
            m = jnp.max(got, axis=0, keepdims=True)
            t = jnp.sum(jnp.exp(got - m), axis=0, keepdims=True)
            stat_ref[s : s + 1, j * 128 : (j + 1) * 128] = m + jnp.log(t)

    back.wait()
    for b in range(6):
        pltpu.make_async_copy(ea.at[b], e_out.at[b, :, pl.ds(512, 256)], esem.at[b]).wait()
    for i in range(2):
        pltpu.make_async_copy(eb.at[i], e_out.at[6 + i], esem.at[6 + i]).wait()


def late_scores(source, blk, cents, ranked, peak0, lse0, rows, e):
    anywhere, hbm = pl.BlockSpec(memory_space=pl.ANY), pl.BlockSpec(memory_space=pltpu.HBM)
    vmem = pl.BlockSpec(memory_space=pltpu.VMEM)
    return pl.pallas_call(
        late_kernel,
        in_specs=[anywhere, vmem] + [anywhere] * 4 + [vmem] * 6 + [hbm] * 2,
        out_specs=(hbm, hbm, vmem, vmem, vmem),
        out_shape=(
            jax.ShapeDtypeStruct(ROWS, BF16),
            jax.ShapeDtypeStruct(SCORES, BF16),
            jax.ShapeDtypeStruct((1, NBLK, TOK), F32),
            jax.ShapeDtypeStruct((NBLK, SLOTS), F32),
            jax.ShapeDtypeStruct((NSRC, TOK), F32),
        ),
        scratch_shapes=[
            pltpu.VMEM((EXT, D), BF16),
            pltpu.VMEM((6, 160, D), BF16),
            pltpu.VMEM((2, 672, D), BF16),
            pltpu.VMEM((NBLK, MOST, D), BF16),
            pltpu.VMEM((4, 1024, D), BF16),
            pltpu.VMEM((6, BS, 256), BF16),
            pltpu.VMEM((2, BS, SLOTS), BF16),
            pltpu.VMEM((NBLK, SLOTS), F32),
            pltpu.SemaphoreType.DMA,
            pltpu.SemaphoreType.DMA((4,)),
            pltpu.SemaphoreType.DMA((2,)),
            pltpu.SemaphoreType.DMA,
            pltpu.SemaphoreType.DMA((8,)),
        ],
        input_output_aliases={12: 0, 13: 1},
        compiler_params=params(34),
        cost_estimate=cost(2 * 6 * BS * SLOTS * D, 20e6, 4 * BS * SLOTS),
        name="late_scores",
    )(source, blk, *cents, *ranked, peak0, lse0, rows, e)


def factor_kernel(stat_refs, idx_ref, peak_ref, f_scr):
    own, from_d, from_e, from_f = stat_refs
    tables = []
    for s in range(NSRC):
        parts = [own[s : s + 1, :]]
        for ref, order in ((from_d, FROM_D), (from_e, FROM_E), (from_f, FROM_F)):
            parts.append(ref[order[s] : order[s] + 1, :])
        m = jnp.maximum(jnp.maximum(parts[0], parts[1]), jnp.maximum(parts[2], parts[3]))
        t = jnp.exp(parts[0] - m)
        for k in range(1, 4):
            t = t + jnp.exp(parts[k] - m)
        tables.append(m + jnp.log(t))
    for k in range(SLOTS // 128):
        at = idx_ref[:, k * 128 : (k + 1) * 128]
        low = at & 127
        high = at >> 7
        lse = jnp.zeros((NBLK, 128), F32)
        for s in range(k * 128 // MOST, (k * 128 + 127) // MOST + 1):
            for j in range(TOK // 128):
                table = jnp.broadcast_to(tables[s][:, j * 128 : (j + 1) * 128], (NBLK, 128))
                got = jnp.take_along_axis(table, low, axis=1, mode="promise_in_bounds")
                lse = jnp.where(high == s * (TOK // 128) + j, got, lse)
        f = jnp.exp(peak_ref[:, k * 128 : (k + 1) * 128] - lse)
        f_scr[:, k * 128 : (k + 1) * 128] = jnp.where(at >= 0, f, 0.0)


def load_factors(s0, s1, s2, s3, idx0, idx1, peak_any, factor_out, f_scr, stats, idx_ref, peak_ref, sem):
    loads = [pltpu.make_async_copy(s, stats.at[k], sem.at[k]) for k, s in enumerate((s0, s1, s2, s3))]
    loads.append(pltpu.make_async_copy(idx0, idx_ref.at[:, pl.ds(0, 512)], sem.at[4]))
    loads.append(pltpu.make_async_copy(idx1, idx_ref.at[:, pl.ds(512, 256)], sem.at[5]))
    loads.append(pltpu.make_async_copy(peak_any, peak_ref, sem.at[6]))
    for load in loads:
        load.start()
    for load in loads:
        load.wait()
    factor_kernel([stats.at[k] for k in range(4)], idx_ref, peak_ref, f_scr)
    factor_out[...] = f_scr[...]


def sums_kernel(part, owners, n_in, *refs):
    ins, refs = refs[:n_in], refs[n_in:]
    e_any, rows_any = ins[-2:]
    n = len(owners)
    i = pl.program_id(0)
    slot = i % 2

    def owner(k):
        return sum(jnp.where(k == step, q, 0) for step, q in enumerate(owners))

    q = owner(i)
    if part == 1:
        outs, factor_out, f_scr, refs = refs[:4], refs[4], refs[5], refs[6:]
        (e_buf, rows_buf, esem, rsem), refs = refs[:4], refs[4:]
    else:
        outs, refs = refs[:n], refs[n:]
        (f_scr, e_buf, rows_buf, fsem, esem, rsem), refs = refs[:6], refs[6:]

    def load_block(k):
        b = 2 * owner(k) + part
        pltpu.make_async_copy(e_any.at[b], e_buf.at[k], esem.at[k]).start()
        pltpu.make_async_copy(rows_any.at[b], rows_buf.at[k], rsem.at[k]).start()

    @pl.when(i == 0)
    def _():
        for k in range(min(2, n)):
            load_block(k)
        if part == 1:
            load_factors(*ins[1:8], factor_out, f_scr, *refs[:4])
        else:
            load = pltpu.make_async_copy(ins[0], f_scr, fsem)
            load.start()
            load.wait()

    if n > 2:
        @pl.when(i < n - 2)
        def _():
            load_block(i + 2)

    f = f_scr[pl.ds(2 * q + part, 1), :]
    pltpu.make_async_copy(e_any.at[0], e_buf.at[i], esem.at[i]).wait()
    pltpu.make_async_copy(rows_any.at[0], rows_buf.at[i], rsem.at[i]).wait()
    totals, counts = [], []
    for m in range(4):
        w = e_buf[i, m * 128 : (m + 1) * 128, :].astype(F32) * f
        count = jnp.sum(w, axis=1, keepdims=True)
        counts.append(jnp.transpose(jnp.broadcast_to(count, (128, 128)))[0:EXTRA])
        totals.append(jnp.dot(w.astype(BF16), rows_buf[i], preferred_element_type=F32).astype(BF16))
    if part == 0:
        owner_first(i, n, totals, counts, outs, *refs)
    else:
        part_first(i, q, slot, ins[0], totals, counts, outs, *refs[4:])


def owner_first(i, n, totals, counts, outs, buf, sem):
    for m in range(4):
        buf[i, m * 128 : (m + 1) * 128, :] = totals[m]
    tile = jnp.concatenate([*counts, jnp.zeros((EXTRA, D - BS), F32)], axis=1)
    buf[i, BS : BS + EXTRA, :] = tile.astype(BF16)
    for k in range(n):
        @pl.when(i == k)
        def _(k=k):
            pltpu.make_async_copy(buf.at[k], outs[k], sem.at[k]).start()

    @pl.when(i == n - 1)
    def _():
        for k in range(n):
            pltpu.make_async_copy(buf.at[k], outs[k], sem.at[k]).wait()


def part_first(i, q, slot, where_ref, totals, counts, outs, buf, gcount, gtile, sem, tsem):
    def send(k, slot=slot):
        start = pl.multiple_of(q * 128, 128)
        return pltpu.make_async_copy(buf.at[slot, k], outs[k].at[pl.ds(start, 128), :], sem.at[slot, k])

    def send_tile(k):
        return pltpu.make_async_copy(gtile.at[k], outs[k].at[pl.ds(BS, EXTRA), :], tsem.at[k])

    @pl.when(i == 0)
    def _():
        gcount[...] = jnp.zeros_like(gcount)

    @pl.when(i >= 2)
    def _():
        for k in range(4):
            send(k).wait()

    for m in range(4):
        at = sum(jnp.where(where_ref[4 + k] == m, k, 0) for k in range(1, 4))
        buf[slot, at] = totals[m]
        gcount[at, pl.ds(q, 1), :] = counts[m][0:1]
    for k in range(4):
        send(k).start()

    @pl.when(i == 3)
    def _():
        for k in range(4):
            tile = jnp.concatenate([gcount[k], jnp.zeros((8, 128), F32)], axis=0)
            tile = jnp.concatenate([tile, jnp.zeros((EXTRA, D - 128), F32)], axis=1)
            gtile[k] = tile.astype(BF16)
            send_tile(k).start()
        for other in range(2):
            for k in range(4):
                send(k, other).wait()
        for k in range(4):
            send_tile(k).wait()


SUMS_SHAPE = (BS + EXTRA, D)


def sums_call(part, owners, small, big, out_shape, out_specs, own):
    n = len(owners)

    def kern(*refs):
        sums_kernel(part, owners, len(small) + len(big), *refs)

    specs = [pl.BlockSpec(memory_space=pl.ANY)] * len(small)
    if part == 1:
        specs[0] = pl.BlockSpec(memory_space=pltpu.SMEM)
    factor = [pltpu.VMEM((NBLK, SLOTS), F32)]
    return pl.pallas_call(
        kern,
        grid=(n,),
        in_specs=specs + [pl.BlockSpec(memory_space=pltpu.HBM)] * len(big),
        out_specs=out_specs,
        out_shape=out_shape,
        scratch_shapes=factor
        + [pltpu.VMEM((n, BS, SLOTS), BF16), pltpu.VMEM((n, SLOTS, D), BF16)]
        + ([pltpu.SemaphoreType.DMA] if part == 0 else [])
        + [pltpu.SemaphoreType.DMA((n,)), pltpu.SemaphoreType.DMA((n,))]
        + own,
        compiler_params=params(54),
        cost_estimate=cost(2 * n * BS * SLOTS * D, n * 3e6),
        name=f"sums{part}",
    )(*small, *big)


def part_sums(where, stats, idx, peak, e, rows):
    anywhere = pl.BlockSpec(memory_space=pl.ANY)
    own = [
        pltpu.VMEM((4, NSRC, TOK), F32),
        pltpu.VMEM((NBLK, SLOTS), jnp.int32),
        pltpu.VMEM((NBLK, SLOTS), F32),
        pltpu.SemaphoreType.DMA((7,)),
        pltpu.VMEM((2, 4, 128, D), BF16),
        pltpu.VMEM((4, 8, 128), F32),
        pltpu.VMEM((4, EXTRA, D), BF16),
        pltpu.SemaphoreType.DMA((2, 4)),
        pltpu.SemaphoreType.DMA((4,)),
    ]
    *out, factor = sums_call(
        1,
        (3, 1, 2, 0),
        (where, *stats, *idx, peak),
        (e, rows),
        (jax.ShapeDtypeStruct(SUMS_SHAPE, BF16),) * 4 + (jax.ShapeDtypeStruct((NBLK, SLOTS), F32),),
        (anywhere,) * 4 + (pl.BlockSpec((NBLK, SLOTS), lambda i: (0, 0)),),
        own,
    )
    return out, factor


def owner_sums(owners, factor, after, e, rows):
    n = len(owners)
    own = [pltpu.VMEM((n, *SUMS_SHAPE), BF16), pltpu.SemaphoreType.DMA((n,))]
    return sums_call(
        0,
        owners,
        (factor, after),
        (e, rows),
        (jax.ShapeDtypeStruct(SUMS_SHAPE, BF16),) * n,
        (pl.BlockSpec(memory_space=pl.ANY),) * n,
        own,
    )


def fetched(refs, buf, sem):
    copies = [pltpu.make_async_copy(ref, buf.at[k], sem.at[k]) for k, ref in enumerate(refs)]
    for copy in copies:
        copy.start()
    for copy in copies:
        copy.wait()
    return [buf.at[k] for k in range(len(refs))]


def count_tile(counts):
    counts = jnp.broadcast_to(counts, (EXTRA, 128))
    return jnp.concatenate([counts, jnp.zeros((EXTRA, D - 128), F32)], axis=1).astype(BF16)


def owner_parts_kernel(where_ref, *refs):
    outs, (acc, buf, sem) = refs[3:7], refs[7:]
    h0, h1, h2 = fetched(refs[:3], buf, sem)
    acc[...] = h0[...].astype(F32) + h1[...].astype(F32) + h2[...].astype(F32)
    counts = acc[BS : BS + 8, 0:BS]
    for k in range(4):
        part = where_ref[4 + k]
        outs[k][0:128, :] = acc[pl.ds(pl.multiple_of(part * 128, 128), 128), :].astype(BF16)
        picked = counts[:, 0:128]
        for m in range(1, 4):
            picked = jnp.where(part == m, counts[:, m * 128 : (m + 1) * 128], picked)
        outs[k][128:, :] = count_tile(picked[0:1])


def part_owners_kernel(where_ref, *refs):
    outs, (_, buf, sem) = refs[3:7], refs[7:]
    g0, g1, g2 = fetched(refs[:3], buf, sem)
    counts = g0[BS:, 0:128].astype(F32) + g1[BS:, 0:128].astype(F32) + g2[BS:, 0:128].astype(F32)
    for k in range(4):
        rows = slice(k * 128, (k + 1) * 128)
        total = g0[rows, :].astype(F32) + g1[rows, :].astype(F32) + g2[rows, :].astype(F32)
        outs[k][0:128, :] = total.astype(BF16)
        outs[k][128:, :] = count_tile(counts[k : k + 1])


def parted(part, where, terms):
    vmem = pl.BlockSpec(memory_space=pltpu.VMEM)
    return pl.pallas_call(
        owner_parts_kernel if part == 0 else part_owners_kernel,
        in_specs=[pl.BlockSpec(memory_space=pltpu.SMEM)] + [pl.BlockSpec(memory_space=pl.ANY)] * 3,
        out_specs=(vmem,) * 4,
        out_shape=(jax.ShapeDtypeStruct((128 + EXTRA, D), BF16),) * 4,
        scratch_shapes=[
            pltpu.VMEM((BS + EXTRA, D), F32),
            pltpu.VMEM((3, BS + EXTRA, D), BF16),
            pltpu.SemaphoreType.DMA((3,)),
        ],
        compiler_params=params(12),
        cost_estimate=cost(1e6, 4e6),
        name=f"parted{part}",
    )(where, *terms)


def final_kernel(*refs):
    mine_ref, out_ref, buf, sem = refs[8:]
    h0, h1, h2, h3, g0, g1, g2, g3 = fetched(refs[:8], buf, sem)
    for i, refs in enumerate(((h0, h1, h2, h3), (g0, g1, g2, g3))):
        total = (refs[0][...].astype(F32) + refs[1][...].astype(F32)) + (refs[2][...].astype(F32) + refs[3][...].astype(F32))
        column = jnp.transpose(jnp.broadcast_to(total[128:129, 0:128], (128, 128)))[:, 0:1]
        out_ref[i] = ((total[0:128] + mine_ref[i].astype(F32)) / (column + 1.0)).astype(BF16)


def final(h, g, mine):
    return pl.pallas_call(
        final_kernel,
        in_specs=[pl.BlockSpec(memory_space=pl.ANY)] * 8 + [pl.BlockSpec(memory_space=pltpu.VMEM)],
        out_specs=pl.BlockSpec(memory_space=pltpu.VMEM),
        out_shape=jax.ShapeDtypeStruct((2, 128, D), BF16),
        scratch_shapes=[pltpu.VMEM((8, 128 + EXTRA, D), BF16), pltpu.SemaphoreType.DMA((8,))],
        compiler_params=params(8),
        cost_estimate=cost(1e6, 2e6),
        name="final",
    )(*h, *g, mine)


def place_kernel(where_ref, *refs):
    parts, (out_ref, buf, in_sem, out_sem) = refs[:8], refs[8:]
    loads = [pltpu.make_async_copy(part, buf.at[k], in_sem.at[k]) for k, part in enumerate(parts)]
    copies = []
    for side in range(2):
        for k in range(4):
            for i in range(2):
                block = where_ref[8 + side] * 2 + i
                quarter = where_ref[4 * side + k]
                copies.append(
                    pltpu.make_async_copy(
                        buf.at[side * 4 + k, i], out_ref.at[block, quarter], out_sem.at[len(copies)]
                    )
                )
    for load in loads:
        load.start()
    for k, load in enumerate(loads):
        load.wait()
        copies[2 * k].start()
        copies[2 * k + 1].start()
    for copy in copies:
        copy.wait()


def place(where, parts):
    return pl.pallas_call(
        place_kernel,
        in_specs=[pl.BlockSpec(memory_space=pltpu.SMEM)] + [pl.BlockSpec(memory_space=pl.ANY)] * 8,
        out_specs=pl.BlockSpec(memory_space=pl.ANY),
        out_shape=jax.ShapeDtypeStruct((4, 4, 128, D), BF16),
        scratch_shapes=[
            pltpu.VMEM((8, 2, 128, D), BF16),
            pltpu.SemaphoreType.DMA((8,)),
            pltpu.SemaphoreType.DMA((16,)),
        ],
        compiler_params=params(8),
        cost_estimate=cost(0, 6e6),
        name="place",
    )(where, *parts)


def tie(a, *after):
    return pl.pallas_call(
        lambda *refs: None,
        in_specs=[pl.BlockSpec(memory_space=pl.ANY)] * (1 + len(after)),
        out_specs=pl.BlockSpec(memory_space=pl.ANY),
        out_shape=jax.ShapeDtypeStruct(a.shape, a.dtype),
        input_output_aliases={0: 0},
        compiler_params=params(8),
        cost_estimate=cost(0, 0),
        name="tie",
    )(a, *after)


def add(*terms):
    total = terms[0].astype(F32)
    for t in terms[1:]:
        total = total + t.astype(F32)
    return total


def ring_terms(own, d, e, f, axis, after=None):
    r1 = turn(f, axis, 1)
    r2 = turn(d if after is None else tie(d, after), axis, -1)
    e = add(e, r1).astype(BF16)
    r3 = turn(e, axis, 1)
    return (own, r2, r3), e


def direct_terms(own, d, e, f, axis):
    return own, turn(d, axis, -1), turn(e, axis, 1), far(f, axis)


def body(vectors, centroids, candidates):
    core, x, y, z = (lax.axis_index(a) for a in ("core", "x", "y", "z"))
    step = 1 - 2 * core

    def around(i):
        return jnp.stack([i, (i - step) % 4, (i + step) % 4, (i + 2) % 4]).astype(jnp.int32)

    xs, zs = around(x), around(z)
    other_zs = jnp.stack([zs[0], zs[2], zs[1], zs[3]])

    where = jnp.concatenate([xs, zs])
    v = pack(vectors, candidates.T)
    a, b = turn(v, "y", 1), turn(v, "y", -1)
    c0 = lax.dynamic_slice_in_dim(centroids, core * 1024, 1024, 0)
    c1, c2 = turn(c0, "x", 1), turn(c0, "x", -1)
    mine = lax.dynamic_slice_in_dim(c0.reshape(2, BS, D), z * 128, 128, 1)
    blk = ((y * 4 + xs) * 4 + 2 * core)[:, None] + jnp.arange(2, dtype=jnp.int32)[None, :]
    blk = jnp.broadcast_to(blk.reshape(NBLK, 1), (NBLK, 128)).astype(F32)

    rank0, rows = dispatch(0, (v, swap(v)), blk, None)
    a = tie(a, rank0, b, c1, c2)
    c = turn(a, "y", 1)
    c3 = turn(c1, "x", 1)
    rank1, rows = dispatch(2, (a, b), blk, rows)
    rows, rank2, e, peak0, lse0 = middle((swap(a), swap(b)), blk, (c0, c1, c2), rows)
    ranked = (rank0, rank1, rank2)
    idx0 = indices(ranked, [(s, s, 0, MOST) for s in range(5)] + [(5, 5, 0, 32)])
    c = tie(c, idx0, c3)
    rank3, rows = dispatch(6, (c,), blk, rows)
    rows, e, rank4, peak, stat = late_scores(
        swap(c), blk, (c0, c1, c2, c3), (*ranked, rank3), peak0, lse0, rows, e
    )
    idx = (idx0, indices((rank2, rank3, rank4), [(5, 1, 32, MOST), (6, 2, 0, MOST), (7, 3, 0, MOST)]))

    theirs = swap(stat)
    theirs = jnp.concatenate([theirs[s : s + 1] for s in SWAPPED])
    m = jnp.maximum(stat, theirs)
    merged = m + jnp.log(jnp.exp(stat - m) + jnp.exp(theirs - m))
    stats = (merged, turn(merged, "y", 1), turn(merged, "y", -1), far(merged, "y"))

    g, factor = part_sums(where, stats, idx, peak, e, rows)
    (h3,) = owner_sums((3,), factor, factor, e, rows)
    h1, h2, h0 = owner_sums((1, 2, 0), factor, h3, e, rows)
    g, _ = ring_terms(*g, "z", h0)
    h, _ = ring_terms(h0, h1, h2, h3, "x")
    h = direct_terms(*parted(0, where, h), "z")
    g = direct_terms(*parted(1, where, g), "x")
    fresh = final(h, g, mine)

    others = [turn(fresh, "z", 1), turn(fresh, "z", -1), far(fresh, "z")]
    parts = [fresh, *others] + [swap(p) for p in (fresh, *others)]
    places = jnp.concatenate([zs, other_zs, jnp.stack([core, 1 - core])]).astype(jnp.int32)
    return place(places, parts).reshape(2048, D)


def solution(mesh):
    fine = Mesh(np.asarray(mesh.devices).reshape(4, 2, 4, 4), ("z", "core", "y", "x"))
    return jax.shard_map(
        body,
        mesh=fine,
        in_specs=(P(("z", "core", "y", "x"), None), P(("y", "x"), None), P(("z", "core", "y", "x"), None)),
        out_specs=P(("y", "x"), None),
        check_vma=False,
    )
```

```python
import jax
import jax.numpy as jnp
import numpy as np
from jax import lax
from jax.experimental import pallas as pl
from jax.experimental.pallas import tpu as pltpu
from jax.sharding import Mesh, PartitionSpec as P

BS = 512
MOST = 96
TOK = 1024
D = 768
NSRC = 8
NBLK = 8
SLOTS = NSRC * MOST
EXTRA = 16
EXT = TOK + EXTRA
ROWS = (28, SLOTS, D)
SCORES = (40, BS, SLOTS)
LOW = -1e30
F32 = jnp.float32
BF16 = jnp.bfloat16

NAMES = ("v", "v'", "a", "b", "a'", "b'", "c", "c'")


def order(**came):
    return tuple(NAMES.index(came[n.replace("'", "_")]) for n in NAMES)


SWAPPED = order(v="v'", v_="v", a="a'", a_="a", b="b'", b_="b", c="c'", c_="c")
FROM_D = order(a="v", b_="v'", c="a", v_="a'", v="b", c_="b'", b="c", a_="c'")
FROM_E = order(b="v", a_="v'", v="a", c_="a'", c="b", v_="b'", a="c", b_="c'")
FROM_F = order(c="v", c_="v'", b="a", b_="a'", a="b", a_="b'", v="c", v_="c'")


def turn(a, axis, sign):
    axes = ("z", "core") if axis == "z" else ("core", axis)
    at = (lambda core, i: i * 2 + core) if axis == "z" else (lambda core, i: core * 4 + i)
    pairs = []
    for core in range(2):
        for i in range(4):
            pairs.append((at(core, i), at(core, (i + (sign if core == 0 else -sign)) % 4)))
    return lax.ppermute(a, axes, pairs)


def far(a, axis):
    return lax.ppermute(a, axis, [(i, (i + 2) % 4) for i in range(4)])


def swap(a):
    return lax.ppermute(a, "core", [(0, 1), (1, 0)])


def params(mib):
    return pltpu.CompilerParams(vmem_limit_bytes=mib * 1024 * 1024)


def cost(flops, nbytes, trans=0):
    return pl.CostEstimate(flops=int(flops), bytes_accessed=int(nbytes), transcendentals=int(trans))


def earlier():
    up = lax.broadcasted_iota(jnp.int32, (TOK, TOK), 0) < lax.broadcasted_iota(jnp.int32, (TOK, TOK), 1)
    return jnp.where(up, 1.0, 0.0).astype(BF16)


def pack_kernel(vectors, cand_ref, out, buf, in_sem, out_sem):
    loads, stores = [], []
    for k in range(4):
        rows = pl.ds(k * 256, 256)
        loads.append(pltpu.make_async_copy(vectors.at[rows, :], buf.at[rows, :], in_sem.at[k]))
        stores.append(pltpu.make_async_copy(buf.at[rows, :], out.at[rows, :], out_sem.at[k]))
        loads[k].start()
    cand = cand_ref[...].astype(F32)
    halves = [cand[pick : pick + 1, h * 512 : (h + 1) * 512] for pick in range(4) for h in range(2)]
    tail = jnp.concatenate([*halves, jnp.zeros((EXTRA - 8, 512), F32)], axis=0)
    tail = jnp.concatenate([tail, jnp.zeros((EXTRA, D - 512), F32)], axis=1)
    buf[TOK:EXT, :] = tail.astype(BF16)
    end = pltpu.make_async_copy(buf.at[pl.ds(TOK, EXTRA), :], out.at[pl.ds(TOK, EXTRA), :], out_sem.at[4])
    end.start()
    for load, store in zip(loads, stores):
        load.wait()
        store.start()
    for store in (*stores, end):
        store.wait()


def pack(vectors, cand):
    anywhere = pl.BlockSpec(memory_space=pl.ANY)
    return pl.pallas_call(
        pack_kernel,
        in_specs=[anywhere, pl.BlockSpec(memory_space=pltpu.VMEM)],
        out_specs=anywhere,
        out_shape=jax.ShapeDtypeStruct((EXT, D), BF16),
        scratch_shapes=[
            pltpu.VMEM((EXT, D), BF16),
            pltpu.SemaphoreType.DMA((4,)),
            pltpu.SemaphoreType.DMA((5,)),
        ],
        compiler_params=params(60),
        cost_estimate=cost(0, 3e6),
        name="pack",
    )(vectors, cand)


def ranks(tail, blk, up):
    tail = tail.astype(F32)
    hit = None
    for pick in range(4):
        named = jnp.concatenate([tail[2 * pick : 2 * pick + 1, 0:512], tail[2 * pick + 1 : 2 * pick + 2, 0:512]], axis=1)
        m = named == blk
        hit = m if hit is None else hit | m
    hit = jnp.where(hit, 1.0, 0.0)
    hits = jnp.concatenate([hit, jnp.zeros((8, TOK), F32)], axis=0).astype(BF16)
    before = jnp.dot(hits, up, preferred_element_type=F32)[0:NBLK]
    return jnp.where(hit > 0, before, -1.0)


def gathered(rank, vectors):
    slot = lax.broadcasted_iota(jnp.int32, (MOST, TOK), 0).astype(F32)
    hot = [jnp.where(slot == rank[b : b + 1, :], 1.0, 0.0).astype(BF16) for b in range(NBLK)]
    hot = jnp.concatenate(hot, axis=0)
    rows = jnp.dot(hot, vectors, preferred_element_type=F32).astype(BF16)
    return rows.reshape(NBLK, MOST, D)


def index_kernel(pieces, *refs):
    rank_refs, idx_ref = refs[:-1], refs[-1]
    sources = [(ref, k) for ref in rank_refs for k in range(ref.shape[0])]
    row = lax.broadcasted_iota(jnp.int32, (8, TOK), 0)
    v = lax.broadcasted_iota(jnp.int32, (8, TOK), 1)
    place = jnp.where(row == 0, v >> 3, jnp.where(row == 1, v & 7, jnp.where(row == 2, 1, 0)))
    place = place.astype(F32).astype(BF16)
    lane = lax.broadcasted_iota(jnp.int32, (1, idx_ref.shape[1]), 1)
    base, end = jnp.zeros(lane.shape, F32), 0
    for s, _, lo, hi in pieces:
        base = jnp.where(lane >= end, float(s * TOK), base)
        end += hi - lo
    for b in range(NBLK):
        hot = []
        for _, at, lo, hi in pieces:
            ref, k = sources[at]
            slot = (lax.broadcasted_iota(jnp.int32, (hi - lo, TOK), 0) + lo).astype(F32)
            hot.append(jnp.where(slot == ref[k, b : b + 1, :], 1.0, 0.0).astype(BF16))
        hot = jnp.concatenate(hot, axis=0)
        found = lax.dot_general(place, hot, (((1,), (1,)), ((), ())), preferred_element_type=F32)
        where = found[0:1] * 8.0 + found[1:2] + base
        idx_ref[b : b + 1, :] = jnp.where(found[2:3] > 0, where, -1.0).astype(jnp.int32)


def indices(ranked, pieces):
    def kern(*refs):
        index_kernel(pieces, *refs)

    width = sum(hi - lo for _, _, lo, hi in pieces)
    return pl.pallas_call(
        kern,
        out_shape=jax.ShapeDtypeStruct((NBLK, width), jnp.int32),
        compiler_params=params(12),
        cost_estimate=cost(4e9, 1e6),
        name="indices",
    )(*ranked)


def dispatch_kernel(n, *refs):
    sources, blk_ref, (rank_ref, out_ref, buf, sems, up) = refs[:n], refs[n], refs[-5:]
    i = pl.program_id(0)

    def copy(k):
        return pltpu.make_async_copy(sources[k], buf.at[k % 2], sems.at[k % 2])

    @pl.when(i == 0)
    def _():
        copy(0).start()
        up[...] = earlier()

    for k in range(n):
        @pl.when(i == k)
        def _(k=k):
            if k + 1 < n:
                copy(k + 1).start()
            copy(k).wait()

    rank = ranks(buf[i % 2, TOK:EXT, :], blk_ref[:, 0:1], up[...])
    rank_ref[0] = rank
    out_ref[...] = gathered(rank, buf[i % 2, 0:TOK, :])


def dispatch(first, sources, blk, rows):
    n = len(sources)
    anywhere = pl.BlockSpec(memory_space=pl.ANY)
    in_specs = [anywhere] * n + [pl.BlockSpec((NBLK, 128), lambda i: (0, 0))]
    args = [*sources, blk]
    alias = {}
    if rows is not None:
        in_specs.append(pl.BlockSpec(memory_space=pltpu.HBM))
        args.append(rows)
        alias = {n + 1: 1}

    def kern(*refs):
        dispatch_kernel(n, *refs)

    return pl.pallas_call(
        kern,
        grid=(n,),
        in_specs=in_specs,
        out_specs=(
            pl.BlockSpec((1, NBLK, TOK), lambda i: (i, 0, 0)),
            pl.BlockSpec((NBLK, MOST, D), lambda i: (0, first + i, 0)),
        ),
        out_shape=(
            jax.ShapeDtypeStruct((n, NBLK, TOK), F32),
            jax.ShapeDtypeStruct(ROWS, BF16),
        ),
        scratch_shapes=[
            pltpu.VMEM((2, EXT, D), BF16),
            pltpu.SemaphoreType.DMA((2,)),
            pltpu.VMEM((TOK, TOK), BF16),
        ],
        input_output_aliases=alias,
        compiler_params=params(34),
        cost_estimate=cost(2 * n * NBLK * MOST * TOK * D, n * 3e6),
        name=f"dispatch{first}",
    )(*args)


def half_norm(cent):
    wide = cent.astype(F32)
    return 0.5 * jnp.sum(wide * wide, axis=1, keepdims=True)


def score_chunk(cent, norm, rows):
    raw = lax.dot_general(cent, rows, (((1,), (1,)), ((), ())), preferred_element_type=F32)
    score = raw - norm
    peak = jnp.max(score, axis=0, keepdims=True)
    e = jnp.exp(score - peak)
    return e.astype(BF16), peak, peak + jnp.log(jnp.sum(e, axis=0, keepdims=True))


def middle_kernel(
    s0, s1, blk_ref, c0, c1, c2, rows_in,
    rows_out, rank_ref, e_out, peak_ref, lse_ref,
    vbuf, x03, x45, cb, eb, vsem, csem, xsem, osem, esem,
):
    sources = [pltpu.make_async_copy(s, vbuf.at[k], vsem.at[k]) for k, s in enumerate((s0, s1))]
    cents = [pltpu.make_async_copy(c, cb.at[k], csem.at[k]) for k, c in enumerate((c0, c1, c2))]
    first = pltpu.make_async_copy(rows_in.at[pl.ds(0, 6), pl.ds(0, 384), :], x03, xsem)
    for copy in sources:
        copy.start()
    up = earlier()
    for k in range(2):
        sources[k].wait()
        for copy in (first, cents[0]) if k == 0 else cents[1:]:
            copy.start()
        rank = ranks(vbuf[k, TOK:EXT, :], blk_ref[:, 0:1], up)
        rank_ref[k] = rank
        x45[:, k * MOST : (k + 1) * MOST, :] = gathered(rank, vbuf[k, 0:TOK, :])
    back = pltpu.make_async_copy(x45, rows_out.at[pl.ds(0, NBLK), pl.ds(384, 192), :], osem)
    back.start()
    first.wait()
    for q in range(3):
        cents[q].wait()
        for i in range(2):
            b = 2 * q + i
            cent = cb[q, i * BS : (i + 1) * BS, :]
            norm = half_norm(cent)
            chunks = (x03[b, 0:256, :], jnp.concatenate([x03[b, 256:384, :], x45[b, 0:128, :]], axis=0))
            for k, rows in enumerate(chunks):
                e, peak, lse = score_chunk(cent, norm, rows)
                eb[b, :, k * 256 : (k + 1) * 256] = e
                peak_ref[b : b + 1, k * 256 : (k + 1) * 256] = peak
                lse_ref[b : b + 1, k * 256 : (k + 1) * 256] = lse
            pltpu.make_async_copy(eb.at[b], e_out.at[b, :, pl.ds(0, 512)], esem.at[b]).start()
    back.wait()
    for b in range(6):
        pltpu.make_async_copy(eb.at[b], e_out.at[b, :, pl.ds(0, 512)], esem.at[b]).wait()


def middle(sources, blk, cents, rows):
    anywhere, hbm = pl.BlockSpec(memory_space=pl.ANY), pl.BlockSpec(memory_space=pltpu.HBM)
    vmem = pl.BlockSpec(memory_space=pltpu.VMEM)
    return pl.pallas_call(
        middle_kernel,
        in_specs=[anywhere] * 2 + [vmem] + [anywhere] * 3 + [hbm],
        out_specs=(hbm, vmem, hbm, vmem, vmem),
        out_shape=(
            jax.ShapeDtypeStruct(ROWS, BF16),
            jax.ShapeDtypeStruct((2, NBLK, TOK), F32),
            jax.ShapeDtypeStruct(SCORES, BF16),
            jax.ShapeDtypeStruct((NBLK, 512), F32),
            jax.ShapeDtypeStruct((NBLK, 512), F32),
        ),
        scratch_shapes=[
            pltpu.VMEM((2, EXT, D), BF16),
            pltpu.VMEM((6, 384, D), BF16),
            pltpu.VMEM((NBLK, 192, D), BF16),
            pltpu.VMEM((3, 1024, D), BF16),
            pltpu.VMEM((6, BS, 512), BF16),
            pltpu.SemaphoreType.DMA((2,)),
            pltpu.SemaphoreType.DMA((3,)),
            pltpu.SemaphoreType.DMA,
            pltpu.SemaphoreType.DMA,
            pltpu.SemaphoreType.DMA((6,)),
        ],
        input_output_aliases={6: 0},
        compiler_params=params(34),
        cost_estimate=cost(4 * NBLK * MOST * TOK * D, 20e6, 6 * BS * 512),
        name="middle",
    )(*sources, blk, *cents, rows)


def late_kernel(
    source, blk_ref, c0, c1, c2, c3, rank0, rank1, rank2, rank3, peak0, lse0, rows_in, e_in,
    rows_out, e_out, rank_ref, peak_ref, stat_ref,
    vbuf, xa, xb, x7, cb, ea, eb, lse_scr, vsem, csem, xsem, osem, esem,
):
    load = pltpu.make_async_copy(source, vbuf, vsem)
    near = pltpu.make_async_copy(rows_in.at[pl.ds(0, 6), pl.ds(512, 160), :], xa, xsem.at[0])
    far_rows = pltpu.make_async_copy(rows_in.at[pl.ds(6, 2), pl.ds(0, 672), :], xb, xsem.at[1])
    cents = [pltpu.make_async_copy(c, cb.at[k], csem.at[k]) for k, c in enumerate((c0, c1, c2, c3))]
    load.start()
    peak_ref[:, 0:512] = peak0[...]
    lse_scr[:, 0:512] = lse0[...]
    up = earlier()
    load.wait()
    for copy in (near, *cents, far_rows):
        copy.start()
    rank = ranks(vbuf[TOK:EXT, :], blk_ref[:, 0:1], up)
    rank_ref[0] = rank
    x7[...] = gathered(rank, vbuf[0:TOK, :])
    back = pltpu.make_async_copy(x7, rows_out.at[pl.ds(0, NBLK), pl.ds(672, MOST), :], osem)
    back.start()
    near.wait()

    @pl.loop(0, 3)
    def _(q):
        pltpu.make_async_copy(c0, cb.at[q], csem.at[q]).wait()
        for i in range(2):
            b = 2 * q + i
            cent = cb[q, i * BS : (i + 1) * BS, :]
            e, peak, lse = score_chunk(cent, half_norm(cent), jnp.concatenate([xa[b], x7[b]], axis=0))
            ea[b] = e
            peak_ref[pl.ds(b, 1), 512:768] = peak
            lse_scr[pl.ds(b, 1), 512:768] = lse
            pltpu.make_async_copy(ea.at[b], e_out.at[b, :, pl.ds(512, 256)], esem.at[b]).start()

    cents[3].wait()
    far_rows.wait()
    for i in range(2):
        b = 6 + i
        cent = cb[3, i * BS : (i + 1) * BS, :]
        norm = half_norm(cent)
        chunks = (xb[i, 0:256, :], xb[i, 256:512, :], jnp.concatenate([xb[i, 512:672, :], x7[b]], axis=0))
        for k, rows in enumerate(chunks):
            e, peak, lse = score_chunk(cent, norm, rows)
            eb[i, :, k * 256 : (k + 1) * 256] = e
            peak_ref[b : b + 1, k * 256 : (k + 1) * 256] = peak
            lse_scr[b : b + 1, k * 256 : (k + 1) * 256] = lse
        pltpu.make_async_copy(eb.at[i], e_out.at[b], esem.at[b]).start()

    sources = [(ref, k) for ref in (rank0, rank1, rank2, rank3, rank_ref) for k in range(ref.shape[0])]
    for s, (ref, k) in enumerate(sources):
        k0, k1 = s * MOST // 128, (s * MOST + MOST - 1) // 128
        for j in range(TOK // 128):
            r = ref[k, :, j * 128 : (j + 1) * 128].astype(jnp.int32)
            at = r + s * MOST
            low = at & 127
            got = jnp.take_along_axis(lse_scr[:, k0 * 128 : (k0 + 1) * 128], low, axis=1, mode="promise_in_bounds")
            if k1 > k0:
                other = jnp.take_along_axis(
                    lse_scr[:, k1 * 128 : (k1 + 1) * 128], low, axis=1, mode="promise_in_bounds"
                )
                got = jnp.where((at >> 7) == k0, got, other)
            got = jnp.where(r >= 0, got, LOW)
            m = jnp.max(got, axis=0, keepdims=True)
            t = jnp.sum(jnp.exp(got - m), axis=0, keepdims=True)
            stat_ref[s : s + 1, j * 128 : (j + 1) * 128] = m + jnp.log(t)

    back.wait()
    for b in range(6):
        pltpu.make_async_copy(ea.at[b], e_out.at[b, :, pl.ds(512, 256)], esem.at[b]).wait()
    for i in range(2):
        pltpu.make_async_copy(eb.at[i], e_out.at[6 + i], esem.at[6 + i]).wait()


def late_scores(source, blk, cents, ranked, peak0, lse0, rows, e):
    anywhere, hbm = pl.BlockSpec(memory_space=pl.ANY), pl.BlockSpec(memory_space=pltpu.HBM)
    vmem = pl.BlockSpec(memory_space=pltpu.VMEM)
    return pl.pallas_call(
        late_kernel,
        in_specs=[anywhere, vmem] + [anywhere] * 4 + [vmem] * 6 + [hbm] * 2,
        out_specs=(hbm, hbm, vmem, vmem, vmem),
        out_shape=(
            jax.ShapeDtypeStruct(ROWS, BF16),
            jax.ShapeDtypeStruct(SCORES, BF16),
            jax.ShapeDtypeStruct((1, NBLK, TOK), F32),
            jax.ShapeDtypeStruct((NBLK, SLOTS), F32),
            jax.ShapeDtypeStruct((NSRC, TOK), F32),
        ),
        scratch_shapes=[
            pltpu.VMEM((EXT, D), BF16),
            pltpu.VMEM((6, 160, D), BF16),
            pltpu.VMEM((2, 672, D), BF16),
            pltpu.VMEM((NBLK, MOST, D), BF16),
            pltpu.VMEM((4, 1024, D), BF16),
            pltpu.VMEM((6, BS, 256), BF16),
            pltpu.VMEM((2, BS, SLOTS), BF16),
            pltpu.VMEM((NBLK, SLOTS), F32),
            pltpu.SemaphoreType.DMA,
            pltpu.SemaphoreType.DMA((4,)),
            pltpu.SemaphoreType.DMA((2,)),
            pltpu.SemaphoreType.DMA,
            pltpu.SemaphoreType.DMA((8,)),
        ],
        input_output_aliases={12: 0, 13: 1},
        compiler_params=params(34),
        cost_estimate=cost(2 * 6 * BS * SLOTS * D, 20e6, 4 * BS * SLOTS),
        name="late_scores",
    )(source, blk, *cents, *ranked, peak0, lse0, rows, e)


def factor_kernel(stat_refs, idx_ref, peak_ref, f_scr):
    own, from_d, from_e, from_f = stat_refs
    tables = []
    for s in range(NSRC):
        parts = [own[s : s + 1, :]]
        for ref, order in ((from_d, FROM_D), (from_e, FROM_E), (from_f, FROM_F)):
            parts.append(ref[order[s] : order[s] + 1, :])
        m = jnp.maximum(jnp.maximum(parts[0], parts[1]), jnp.maximum(parts[2], parts[3]))
        t = jnp.exp(parts[0] - m)
        for k in range(1, 4):
            t = t + jnp.exp(parts[k] - m)
        tables.append(m + jnp.log(t))
    for k in range(SLOTS // 128):
        at = idx_ref[:, k * 128 : (k + 1) * 128]
        low = at & 127
        high = at >> 7
        lse = jnp.zeros((NBLK, 128), F32)
        for s in range(k * 128 // MOST, (k * 128 + 127) // MOST + 1):
            for j in range(TOK // 128):
                table = jnp.broadcast_to(tables[s][:, j * 128 : (j + 1) * 128], (NBLK, 128))
                got = jnp.take_along_axis(table, low, axis=1, mode="promise_in_bounds")
                lse = jnp.where(high == s * (TOK // 128) + j, got, lse)
        f = jnp.exp(peak_ref[:, k * 128 : (k + 1) * 128] - lse)
        f_scr[:, k * 128 : (k + 1) * 128] = jnp.where(at >= 0, f, 0.0)


def load_factors(s0, s1, s2, s3, idx0, idx1, peak_any, factor_out, f_scr, stats, idx_ref, peak_ref, sem):
    loads = [pltpu.make_async_copy(s, stats.at[k], sem.at[k]) for k, s in enumerate((s0, s1, s2, s3))]
    loads.append(pltpu.make_async_copy(idx0, idx_ref.at[:, pl.ds(0, 512)], sem.at[4]))
    loads.append(pltpu.make_async_copy(idx1, idx_ref.at[:, pl.ds(512, 256)], sem.at[5]))
    loads.append(pltpu.make_async_copy(peak_any, peak_ref, sem.at[6]))
    for load in loads:
        load.start()
    for load in loads:
        load.wait()
    factor_kernel([stats.at[k] for k in range(4)], idx_ref, peak_ref, f_scr)
    factor_out[...] = f_scr[...]


def sums_kernel(steps, n_in, *refs):
    ins, refs = refs[:n_in], refs[n_in:]
    e_any, rows_any = ins[-2:]
    n = len(steps)
    first_call = steps[0][1] == 1
    i = pl.program_id(0)
    slot = i % 2

    def at_step(k, column):
        return sum(jnp.where(k == step, entry[column], 0) for step, entry in enumerate(steps))

    def block(k):
        return 2 * at_step(k, 0) + at_step(k, 1)

    if first_call:
        outs, factor_out, f_scr, refs = refs[:5], refs[5], refs[6], refs[7:]
        (e_buf, rows_buf, esem, rsem), refs = refs[:4], refs[4:]
    else:
        outs, refs = refs[:n], refs[n:]
        (f_scr, e_buf, rows_buf, fsem, esem, rsem), refs = refs[:6], refs[6:]

    def load_block(k):
        b = block(k)
        pltpu.make_async_copy(e_any.at[b], e_buf.at[k], esem.at[k]).start()
        pltpu.make_async_copy(rows_any.at[b], rows_buf.at[k], rsem.at[k]).start()

    @pl.when(i == 0)
    def _():
        for k in range(2):
            load_block(k)
        if first_call:
            load_factors(*ins[1:8], factor_out, f_scr, *refs[:4])
        else:
            load = pltpu.make_async_copy(ins[0], f_scr, fsem)
            load.start()
            load.wait()

    @pl.when(i < n - 2)
    def _():
        load_block(i + 2)

    f = f_scr[pl.ds(block(i), 1), :]
    pltpu.make_async_copy(e_any.at[0], e_buf.at[i], esem.at[i]).wait()
    pltpu.make_async_copy(rows_any.at[0], rows_buf.at[i], rsem.at[i]).wait()
    totals, counts = [], []
    for m in range(4):
        w = e_buf[i, m * 128 : (m + 1) * 128, :].astype(F32) * f
        count = jnp.sum(w, axis=1, keepdims=True)
        counts.append(jnp.transpose(jnp.broadcast_to(count, (128, 128)))[0:EXTRA])
        totals.append(jnp.dot(w.astype(BF16), rows_buf[i], preferred_element_type=F32).astype(BF16))
    if first_call:
        part_first(i, at_step(i, 0), slot, ins[0], totals, counts, outs[:4], *refs[4:9])

        @pl.when(i == 4)
        def _():
            owner_first(0, 1, totals, counts, outs[4:], *refs[9:])
    else:
        owner_first(i, n, totals, counts, outs, *refs)


def owner_first(i, n, totals, counts, outs, buf, sem):
    for m in range(4):
        buf[i, m * 128 : (m + 1) * 128, :] = totals[m]
    tile = jnp.concatenate([*counts, jnp.zeros((EXTRA, D - BS), F32)], axis=1)
    buf[i, BS : BS + EXTRA, :] = tile.astype(BF16)
    for k in range(n):
        @pl.when(i == k)
        def _(k=k):
            pltpu.make_async_copy(buf.at[k], outs[k], sem.at[k]).start()

    @pl.when(i == n - 1)
    def _():
        for k in range(n):
            pltpu.make_async_copy(buf.at[k], outs[k], sem.at[k]).wait()


def part_first(i, q, slot, where_ref, totals, counts, outs, buf, gcount, gtile, sem, tsem):
    def send(k, slot=slot):
        start = pl.multiple_of(q * 128, 128)
        return pltpu.make_async_copy(buf.at[slot, k], outs[k].at[pl.ds(start, 128), :], sem.at[slot, k])

    def send_tile(k):
        return pltpu.make_async_copy(gtile.at[k], outs[k].at[pl.ds(BS, EXTRA), :], tsem.at[k])

    @pl.when(i == 0)
    def _():
        gcount[...] = jnp.zeros_like(gcount)

    @pl.when((i == 2) | (i == 3))
    def _():
        for k in range(4):
            send(k).wait()

    @pl.when(i < 4)
    def _():
        for m in range(4):
            at = sum(jnp.where(where_ref[4 + k] == m, k, 0) for k in range(1, 4))
            buf[slot, at] = totals[m]
            gcount[at, pl.ds(q, 1), :] = counts[m][0:1]
        for k in range(4):
            send(k).start()

    @pl.when(i == 3)
    def _():
        for k in range(4):
            tile = jnp.concatenate([gcount[k], jnp.zeros((8, 128), F32)], axis=0)
            tile = jnp.concatenate([tile, jnp.zeros((EXTRA, D - 128), F32)], axis=1)
            gtile[k] = tile.astype(BF16)
            send_tile(k).start()

    @pl.when(i == 4)
    def _():
        for other in range(2):
            for k in range(4):
                send(k, other).wait()
        for k in range(4):
            send_tile(k).wait()


SUMS_SHAPE = (BS + EXTRA, D)


def sums_call(steps, small, big, out_shape, out_specs, own):
    n = len(steps)
    first_call = steps[0][1] == 1

    def kern(*refs):
        sums_kernel(steps, len(small) + len(big), *refs)

    specs = [pl.BlockSpec(memory_space=pl.ANY)] * len(small)
    if first_call:
        specs[0] = pl.BlockSpec(memory_space=pltpu.SMEM)
    factor = [pltpu.VMEM((NBLK, SLOTS), F32)]
    return pl.pallas_call(
        kern,
        grid=(n,),
        in_specs=specs + [pl.BlockSpec(memory_space=pltpu.HBM)] * len(big),
        out_specs=out_specs,
        out_shape=out_shape,
        scratch_shapes=factor
        + [pltpu.VMEM((n, BS, SLOTS), BF16), pltpu.VMEM((n, SLOTS, D), BF16)]
        + ([] if first_call else [pltpu.SemaphoreType.DMA])
        + [pltpu.SemaphoreType.DMA((n,)), pltpu.SemaphoreType.DMA((n,))]
        + own,
        compiler_params=params(54),
        cost_estimate=cost(2 * n * BS * SLOTS * D, n * 3e6),
        name=f"sums{n}",
    )(*small, *big)


def first_sums(where, stats, idx, peak, e, rows):
    anywhere = pl.BlockSpec(memory_space=pl.ANY)
    own = [
        pltpu.VMEM((4, NSRC, TOK), F32),
        pltpu.VMEM((NBLK, SLOTS), jnp.int32),
        pltpu.VMEM((NBLK, SLOTS), F32),
        pltpu.SemaphoreType.DMA((7,)),
        pltpu.VMEM((2, 4, 128, D), BF16),
        pltpu.VMEM((4, 8, 128), F32),
        pltpu.VMEM((4, EXTRA, D), BF16),
        pltpu.SemaphoreType.DMA((2, 4)),
        pltpu.SemaphoreType.DMA((4,)),
        pltpu.VMEM((1, *SUMS_SHAPE), BF16),
        pltpu.SemaphoreType.DMA((1,)),
    ]
    *out, factor = sums_call(
        ((3, 1), (1, 1), (2, 1), (0, 1), (3, 0)),
        (where, *stats, *idx, peak),
        (e, rows),
        (jax.ShapeDtypeStruct(SUMS_SHAPE, BF16),) * 5 + (jax.ShapeDtypeStruct((NBLK, SLOTS), F32),),
        (anywhere,) * 5 + (pl.BlockSpec((NBLK, SLOTS), lambda i: (0, 0)),),
        own,
    )
    return out[:4], out[4], factor


def owner_sums(owners, factor, e, rows):
    n = len(owners)
    own = [pltpu.VMEM((n, *SUMS_SHAPE), BF16), pltpu.SemaphoreType.DMA((n,))]
    return sums_call(
        tuple((q, 0) for q in owners),
        (factor,),
        (e, rows),
        (jax.ShapeDtypeStruct(SUMS_SHAPE, BF16),) * n,
        (pl.BlockSpec(memory_space=pl.ANY),) * n,
        own,
    )


def fetched(refs, buf, sem):
    copies = [pltpu.make_async_copy(ref, buf.at[k], sem.at[k]) for k, ref in enumerate(refs)]
    for copy in copies:
        copy.start()
    for copy in copies:
        copy.wait()
    return [buf.at[k] for k in range(len(refs))]


def count_tile(counts):
    counts = jnp.broadcast_to(counts, (EXTRA, 128))
    return jnp.concatenate([counts, jnp.zeros((EXTRA, D - 128), F32)], axis=1).astype(BF16)


def owner_parts_kernel(where_ref, *refs):
    outs, (acc, buf, sem) = refs[3:7], refs[7:]
    h0, h1, h2 = fetched(refs[:3], buf, sem)
    acc[...] = h0[...].astype(F32) + h1[...].astype(F32) + h2[...].astype(F32)
    counts = acc[BS : BS + 8, 0:BS]
    for k in range(4):
        part = where_ref[4 + k]
        outs[k][0:128, :] = acc[pl.ds(pl.multiple_of(part * 128, 128), 128), :].astype(BF16)
        picked = counts[:, 0:128]
        for m in range(1, 4):
            picked = jnp.where(part == m, counts[:, m * 128 : (m + 1) * 128], picked)
        outs[k][128:, :] = count_tile(picked[0:1])


def part_owners_kernel(where_ref, *refs):
    outs, (_, buf, sem) = refs[3:7], refs[7:]
    g0, g1, g2 = fetched(refs[:3], buf, sem)
    counts = g0[BS:, 0:128].astype(F32) + g1[BS:, 0:128].astype(F32) + g2[BS:, 0:128].astype(F32)
    for k in range(4):
        rows = slice(k * 128, (k + 1) * 128)
        total = g0[rows, :].astype(F32) + g1[rows, :].astype(F32) + g2[rows, :].astype(F32)
        outs[k][0:128, :] = total.astype(BF16)
        outs[k][128:, :] = count_tile(counts[k : k + 1])


def parted(part, where, terms):
    vmem = pl.BlockSpec(memory_space=pltpu.VMEM)
    return pl.pallas_call(
        owner_parts_kernel if part == 0 else part_owners_kernel,
        in_specs=[pl.BlockSpec(memory_space=pltpu.SMEM)] + [pl.BlockSpec(memory_space=pl.ANY)] * 3,
        out_specs=(vmem,) * 4,
        out_shape=(jax.ShapeDtypeStruct((128 + EXTRA, D), BF16),) * 4,
        scratch_shapes=[
            pltpu.VMEM((BS + EXTRA, D), F32),
            pltpu.VMEM((3, BS + EXTRA, D), BF16),
            pltpu.SemaphoreType.DMA((3,)),
        ],
        compiler_params=params(12),
        cost_estimate=cost(1e6, 4e6),
        name=f"parted{part}",
    )(where, *terms)


def final_kernel(*refs):
    mine_ref, out_ref, buf, sem = refs[8:]
    h0, h1, h2, h3, g0, g1, g2, g3 = fetched(refs[:8], buf, sem)
    for i, refs in enumerate(((h0, h1, h2, h3), (g0, g1, g2, g3))):
        total = (refs[0][...].astype(F32) + refs[1][...].astype(F32)) + (refs[2][...].astype(F32) + refs[3][...].astype(F32))
        column = jnp.transpose(jnp.broadcast_to(total[128:129, 0:128], (128, 128)))[:, 0:1]
        out_ref[i] = ((total[0:128] + mine_ref[i].astype(F32)) / (column + 1.0)).astype(BF16)


def final(h, g, mine):
    return pl.pallas_call(
        final_kernel,
        in_specs=[pl.BlockSpec(memory_space=pl.ANY)] * 8 + [pl.BlockSpec(memory_space=pltpu.VMEM)],
        out_specs=pl.BlockSpec(memory_space=pltpu.VMEM),
        out_shape=jax.ShapeDtypeStruct((2, 128, D), BF16),
        scratch_shapes=[pltpu.VMEM((8, 128 + EXTRA, D), BF16), pltpu.SemaphoreType.DMA((8,))],
        compiler_params=params(8),
        cost_estimate=cost(1e6, 2e6),
        name="final",
    )(*h, *g, mine)


def place_kernel(where_ref, *refs):
    parts, (out_ref, buf, in_sem, out_sem) = refs[:8], refs[8:]
    loads = [pltpu.make_async_copy(part, buf.at[k], in_sem.at[k]) for k, part in enumerate(parts)]
    copies = []
    for side in range(2):
        for k in range(4):
            for i in range(2):
                block = where_ref[8 + side] * 2 + i
                quarter = where_ref[4 * side + k]
                copies.append(
                    pltpu.make_async_copy(
                        buf.at[side * 4 + k, i], out_ref.at[block, quarter], out_sem.at[len(copies)]
                    )
                )
    for load in loads:
        load.start()
    for k, load in enumerate(loads):
        load.wait()
        copies[2 * k].start()
        copies[2 * k + 1].start()
    for copy in copies:
        copy.wait()


def place(where, parts):
    return pl.pallas_call(
        place_kernel,
        in_specs=[pl.BlockSpec(memory_space=pltpu.SMEM)] + [pl.BlockSpec(memory_space=pl.ANY)] * 8,
        out_specs=pl.BlockSpec(memory_space=pl.ANY),
        out_shape=jax.ShapeDtypeStruct((4, 4, 128, D), BF16),
        scratch_shapes=[
            pltpu.VMEM((8, 2, 128, D), BF16),
            pltpu.SemaphoreType.DMA((8,)),
            pltpu.SemaphoreType.DMA((16,)),
        ],
        compiler_params=params(8),
        cost_estimate=cost(0, 6e6),
        name="place",
    )(where, *parts)


def tie(a, *after):
    return pl.pallas_call(
        lambda *refs: None,
        in_specs=[pl.BlockSpec(memory_space=pl.ANY)] * (1 + len(after)),
        out_specs=pl.BlockSpec(memory_space=pl.ANY),
        out_shape=jax.ShapeDtypeStruct(a.shape, a.dtype),
        input_output_aliases={0: 0},
        compiler_params=params(8),
        cost_estimate=cost(0, 0),
        name="tie",
    )(a, *after)


def add(*terms):
    total = terms[0].astype(F32)
    for t in terms[1:]:
        total = total + t.astype(F32)
    return total


def ring_terms(own, d, e, f, axis, after=None):
    r1 = turn(f, axis, 1)
    r2 = turn(d if after is None else tie(d, after), axis, -1)
    e = add(e, r1).astype(BF16)
    r3 = turn(e, axis, 1)
    return (own, r2, r3), e


def direct_terms(own, d, e, f, axis):
    return own, turn(d, axis, -1), turn(e, axis, 1), far(f, axis)


def body(vectors, centroids, candidates):
    core, x, y, z = (lax.axis_index(a) for a in ("core", "x", "y", "z"))
    step = 1 - 2 * core

    def around(i):
        return jnp.stack([i, (i - step) % 4, (i + step) % 4, (i + 2) % 4]).astype(jnp.int32)

    xs, zs = around(x), around(z)
    other_zs = jnp.stack([zs[0], zs[2], zs[1], zs[3]])

    where = jnp.concatenate([xs, zs])
    v = pack(vectors, candidates.T)
    a, b = turn(v, "y", 1), turn(v, "y", -1)
    c0 = lax.dynamic_slice_in_dim(centroids, core * 1024, 1024, 0)
    c1, c2 = turn(c0, "x", 1), turn(c0, "x", -1)
    mine = lax.dynamic_slice_in_dim(c0.reshape(2, BS, D), z * 128, 128, 1)
    blk = ((y * 4 + xs) * 4 + 2 * core)[:, None] + jnp.arange(2, dtype=jnp.int32)[None, :]
    blk = jnp.broadcast_to(blk.reshape(NBLK, 1), (NBLK, 128)).astype(F32)

    rank0, rows = dispatch(0, (v, swap(v)), blk, None)
    a = tie(a, rank0, b, c1, c2)
    c = turn(a, "y", 1)
    c3 = turn(c1, "x", 1)
    rank1, rows = dispatch(2, (a, b), blk, rows)
    rows, rank2, e, peak0, lse0 = middle((swap(a), swap(b)), blk, (c0, c1, c2), rows)
    ranked = (rank0, rank1, rank2)
    idx0 = indices(ranked, [(s, s, 0, MOST) for s in range(5)] + [(5, 5, 0, 32)])
    c = tie(c, idx0, c3)
    rank3, rows = dispatch(6, (c,), blk, rows)
    rows, e, rank4, peak, stat = late_scores(
        swap(c), blk, (c0, c1, c2, c3), (*ranked, rank3), peak0, lse0, rows, e
    )
    idx = (idx0, indices((rank2, rank3, rank4), [(5, 1, 32, MOST), (6, 2, 0, MOST), (7, 3, 0, MOST)]))

    theirs = swap(stat)
    theirs = jnp.concatenate([theirs[s : s + 1] for s in SWAPPED])
    m = jnp.maximum(stat, theirs)
    merged = m + jnp.log(jnp.exp(stat - m) + jnp.exp(theirs - m))
    stats = (merged, turn(merged, "y", 1), turn(merged, "y", -1), far(merged, "y"))

    g, h3, factor = first_sums(where, stats, idx, peak, e, rows)
    h1, h2, h0 = owner_sums((1, 2, 0), factor, e, rows)
    g, _ = ring_terms(*g, "z", h0)
    h, _ = ring_terms(h0, h1, h2, h3, "x")
    h = direct_terms(*parted(0, where, h), "z")
    g = direct_terms(*parted(1, where, g), "x")
    fresh = final(h, g, mine)

    others = [turn(fresh, "z", 1), turn(fresh, "z", -1), far(fresh, "z")]
    parts = [fresh, *others] + [swap(p) for p in (fresh, *others)]
    places = jnp.concatenate([zs, other_zs, jnp.stack([core, 1 - core])]).astype(jnp.int32)
    return place(places, parts).reshape(2048, D)


def solution(mesh):
    fine = Mesh(np.asarray(mesh.devices).reshape(4, 2, 4, 4), ("z", "core", "y", "x"))
    return jax.shard_map(
        body,
        mesh=fine,
        in_specs=(P(("z", "core", "y", "x"), None), P(("y", "x"), None), P(("z", "core", "y", "x"), None)),
        out_specs=P(("y", "x"), None),
        check_vma=False,
    )
```

```python
import jax
import jax.numpy as jnp
import numpy as np
from jax import lax
from jax.experimental import pallas as pl
from jax.experimental.pallas import tpu as pltpu
from jax.sharding import Mesh, PartitionSpec as P

BS = 512
MOST = 96
TOK = 1024
D = 768
NSRC = 8
NBLK = 8
SLOTS = NSRC * MOST
EXTRA = 16
EXT = TOK + EXTRA
ROWS = (28, SLOTS, D)
SCORES = (40, BS, SLOTS)
LOW = -1e30
F32 = jnp.float32
BF16 = jnp.bfloat16

NAMES = ("v", "v'", "a", "b", "a'", "b'", "c", "c'")


def order(**came):
    return tuple(NAMES.index(came[n.replace("'", "_")]) for n in NAMES)


SWAPPED = order(v="v'", v_="v", a="a'", a_="a", b="b'", b_="b", c="c'", c_="c")
FROM_D = order(a="v", b_="v'", c="a", v_="a'", v="b", c_="b'", b="c", a_="c'")
FROM_E = order(b="v", a_="v'", v="a", c_="a'", c="b", v_="b'", a="c", b_="c'")
FROM_F = order(c="v", c_="v'", b="a", b_="a'", a="b", a_="b'", v="c", v_="c'")


def turn(a, axis, sign):
    axes = ("z", "core") if axis == "z" else ("core", axis)
    at = (lambda core, i: i * 2 + core) if axis == "z" else (lambda core, i: core * 4 + i)
    pairs = []
    for core in range(2):
        for i in range(4):
            pairs.append((at(core, i), at(core, (i + (sign if core == 0 else -sign)) % 4)))
    return lax.ppermute(a, axes, pairs)


def far(a, axis):
    return lax.ppermute(a, axis, [(i, (i + 2) % 4) for i in range(4)])


def swap(a):
    return lax.ppermute(a, "core", [(0, 1), (1, 0)])


def params(mib):
    return pltpu.CompilerParams(vmem_limit_bytes=mib * 1024 * 1024)


def cost(flops, nbytes, trans=0):
    return pl.CostEstimate(flops=int(flops), bytes_accessed=int(nbytes), transcendentals=int(trans))


def earlier():
    up = lax.broadcasted_iota(jnp.int32, (TOK, TOK), 0) < lax.broadcasted_iota(jnp.int32, (TOK, TOK), 1)
    return jnp.where(up, 1.0, 0.0).astype(BF16)


def pack_kernel(vectors, cand_ref, out, buf, in_sem, out_sem):
    loads, stores = [], []
    for k in range(2):
        rows = pl.ds(k * 512, 512)
        loads.append(pltpu.make_async_copy(vectors.at[rows, :], buf.at[rows, :], in_sem.at[k]))
        stores.append(pltpu.make_async_copy(buf.at[rows, :], out.at[rows, :], out_sem.at[k]))
        loads[k].start()
    cand = cand_ref[...].astype(F32)
    halves = [cand[pick : pick + 1, h * 512 : (h + 1) * 512] for pick in range(4) for h in range(2)]
    tail = jnp.concatenate([*halves, jnp.zeros((EXTRA - 8, 512), F32)], axis=0)
    tail = jnp.concatenate([tail, jnp.zeros((EXTRA, D - 512), F32)], axis=1)
    buf[TOK:EXT, :] = tail.astype(BF16)
    end = pltpu.make_async_copy(buf.at[pl.ds(TOK, EXTRA), :], out.at[pl.ds(TOK, EXTRA), :], out_sem.at[4])
    end.start()
    for load, store in zip(loads, stores):
        load.wait()
        store.start()
    for store in (*stores, end):
        store.wait()


def pack(vectors, cand):
    anywhere = pl.BlockSpec(memory_space=pl.ANY)
    return pl.pallas_call(
        pack_kernel,
        in_specs=[anywhere, pl.BlockSpec(memory_space=pltpu.VMEM)],
        out_specs=anywhere,
        out_shape=jax.ShapeDtypeStruct((EXT, D), BF16),
        scratch_shapes=[
            pltpu.VMEM((EXT, D), BF16),
            pltpu.SemaphoreType.DMA((4,)),
            pltpu.SemaphoreType.DMA((5,)),
        ],
        compiler_params=params(60),
        cost_estimate=cost(0, 3e6),
        name="pack",
    )(vectors, cand)


def ranks(tail, blk, up):
    tail = tail.astype(F32)
    hit = None
    for pick in range(4):
        named = jnp.concatenate([tail[2 * pick : 2 * pick + 1, 0:512], tail[2 * pick + 1 : 2 * pick + 2, 0:512]], axis=1)
        m = named == blk
        hit = m if hit is None else hit | m
    hit = jnp.where(hit, 1.0, 0.0)
    hits = jnp.concatenate([hit, jnp.zeros((8, TOK), F32)], axis=0).astype(BF16)
    before = jnp.dot(hits, up, preferred_element_type=F32)[0:NBLK]
    return jnp.where(hit > 0, before, -1.0)


def gathered(rank, vectors):
    slot = lax.broadcasted_iota(jnp.int32, (MOST, TOK), 0).astype(F32)
    hot = [jnp.where(slot == rank[b : b + 1, :], 1.0, 0.0).astype(BF16) for b in range(NBLK)]
    hot = jnp.concatenate(hot, axis=0)
    rows = jnp.dot(hot, vectors, preferred_element_type=F32).astype(BF16)
    return rows.reshape(NBLK, MOST, D)


def index_kernel(pieces, *refs):
    rank_refs, idx_ref = refs[:-1], refs[-1]
    sources = [(ref, k) for ref in rank_refs for k in range(ref.shape[0])]
    row = lax.broadcasted_iota(jnp.int32, (8, TOK), 0)
    v = lax.broadcasted_iota(jnp.int32, (8, TOK), 1)
    place = jnp.where(row == 0, v >> 3, jnp.where(row == 1, v & 7, jnp.where(row == 2, 1, 0)))
    place = place.astype(F32).astype(BF16)
    lane = lax.broadcasted_iota(jnp.int32, (1, idx_ref.shape[1]), 1)
    base, end = jnp.zeros(lane.shape, F32), 0
    for s, _, lo, hi in pieces:
        base = jnp.where(lane >= end, float(s * TOK), base)
        end += hi - lo
    for b in range(NBLK):
        hot = []
        for _, at, lo, hi in pieces:
            ref, k = sources[at]
            slot = (lax.broadcasted_iota(jnp.int32, (hi - lo, TOK), 0) + lo).astype(F32)
            hot.append(jnp.where(slot == ref[k, b : b + 1, :], 1.0, 0.0).astype(BF16))
        hot = jnp.concatenate(hot, axis=0)
        found = lax.dot_general(place, hot, (((1,), (1,)), ((), ())), preferred_element_type=F32)
        where = found[0:1] * 8.0 + found[1:2] + base
        idx_ref[b : b + 1, :] = jnp.where(found[2:3] > 0, where, -1.0).astype(jnp.int32)


def indices(ranked, pieces):
    def kern(*refs):
        index_kernel(pieces, *refs)

    width = sum(hi - lo for _, _, lo, hi in pieces)
    return pl.pallas_call(
        kern,
        out_shape=jax.ShapeDtypeStruct((NBLK, width), jnp.int32),
        compiler_params=params(12),
        cost_estimate=cost(4e9, 1e6),
        name="indices",
    )(*ranked)


def dispatch_kernel(n, *refs):
    sources, blk_ref, (rank_ref, out_ref, buf, sems, up) = refs[:n], refs[n], refs[-5:]
    i = pl.program_id(0)

    def copy(k):
        return pltpu.make_async_copy(sources[k], buf.at[k % 2], sems.at[k % 2])

    @pl.when(i == 0)
    def _():
        copy(0).start()
        up[...] = earlier()

    for k in range(n):
        @pl.when(i == k)
        def _(k=k):
            if k + 1 < n:
                copy(k + 1).start()
            copy(k).wait()

    rank = ranks(buf[i % 2, TOK:EXT, :], blk_ref[:, 0:1], up[...])
    rank_ref[0] = rank
    out_ref[...] = gathered(rank, buf[i % 2, 0:TOK, :])


def dispatch(first, sources, blk, rows):
    n = len(sources)
    anywhere = pl.BlockSpec(memory_space=pl.ANY)
    in_specs = [anywhere] * n + [pl.BlockSpec((NBLK, 128), lambda i: (0, 0))]
    args = [*sources, blk]
    alias = {}
    if rows is not None:
        in_specs.append(pl.BlockSpec(memory_space=pltpu.HBM))
        args.append(rows)
        alias = {n + 1: 1}

    def kern(*refs):
        dispatch_kernel(n, *refs)

    return pl.pallas_call(
        kern,
        grid=(n,),
        in_specs=in_specs,
        out_specs=(
            pl.BlockSpec((1, NBLK, TOK), lambda i: (i, 0, 0)),
            pl.BlockSpec((NBLK, MOST, D), lambda i: (0, first + i, 0)),
        ),
        out_shape=(
            jax.ShapeDtypeStruct((n, NBLK, TOK), F32),
            jax.ShapeDtypeStruct(ROWS, BF16),
        ),
        scratch_shapes=[
            pltpu.VMEM((2, EXT, D), BF16),
            pltpu.SemaphoreType.DMA((2,)),
            pltpu.VMEM((TOK, TOK), BF16),
        ],
        input_output_aliases=alias,
        compiler_params=params(34),
        cost_estimate=cost(2 * n * NBLK * MOST * TOK * D, n * 3e6),
        name=f"dispatch{first}",
    )(*args)


def half_norm(cent):
    wide = cent.astype(F32)
    return 0.5 * jnp.sum(wide * wide, axis=1, keepdims=True)


def score_chunk(cent, norm, rows):
    raw = lax.dot_general(cent, rows, (((1,), (1,)), ((), ())), preferred_element_type=F32)
    score = raw - norm
    peak = jnp.max(score, axis=0, keepdims=True)
    e = jnp.exp(score - peak)
    return e.astype(BF16), peak, peak + jnp.log(jnp.sum(e, axis=0, keepdims=True))


def middle_kernel(
    s0, s1, blk_ref, c0, c1, c2, rows_in,
    rows_out, rank_ref, e_out, peak_ref, lse_ref,
    vbuf, x03, x45, cb, eb, vsem, csem, xsem, osem, esem,
):
    sources = [pltpu.make_async_copy(s, vbuf.at[k], vsem.at[k]) for k, s in enumerate((s0, s1))]
    cents = [pltpu.make_async_copy(c, cb.at[k], csem.at[k]) for k, c in enumerate((c0, c1, c2))]
    first = pltpu.make_async_copy(rows_in.at[pl.ds(0, 6), pl.ds(0, 384), :], x03, xsem)
    for copy in sources:
        copy.start()
    up = earlier()
    for k in range(2):
        sources[k].wait()
        for copy in (first, cents[0]) if k == 0 else cents[1:]:
            copy.start()
        rank = ranks(vbuf[k, TOK:EXT, :], blk_ref[:, 0:1], up)
        rank_ref[k] = rank
        x45[:, k * MOST : (k + 1) * MOST, :] = gathered(rank, vbuf[k, 0:TOK, :])
    back = pltpu.make_async_copy(x45, rows_out.at[pl.ds(0, NBLK), pl.ds(384, 192), :], osem)
    back.start()
    first.wait()
    for q in range(3):
        cents[q].wait()
        for i in range(2):
            b = 2 * q + i
            cent = cb[q, i * BS : (i + 1) * BS, :]
            norm = half_norm(cent)
            chunks = (x03[b, 0:256, :], jnp.concatenate([x03[b, 256:384, :], x45[b, 0:128, :]], axis=0))
            for k, rows in enumerate(chunks):
                e, peak, lse = score_chunk(cent, norm, rows)
                eb[b, :, k * 256 : (k + 1) * 256] = e
                peak_ref[b : b + 1, k * 256 : (k + 1) * 256] = peak
                lse_ref[b : b + 1, k * 256 : (k + 1) * 256] = lse
            pltpu.make_async_copy(eb.at[b], e_out.at[b, :, pl.ds(0, 512)], esem.at[b]).start()
    back.wait()
    for b in range(6):
        pltpu.make_async_copy(eb.at[b], e_out.at[b, :, pl.ds(0, 512)], esem.at[b]).wait()


def middle(sources, blk, cents, rows):
    anywhere, hbm = pl.BlockSpec(memory_space=pl.ANY), pl.BlockSpec(memory_space=pltpu.HBM)
    vmem = pl.BlockSpec(memory_space=pltpu.VMEM)
    return pl.pallas_call(
        middle_kernel,
        in_specs=[anywhere] * 2 + [vmem] + [anywhere] * 3 + [hbm],
        out_specs=(hbm, vmem, hbm, vmem, vmem),
        out_shape=(
            jax.ShapeDtypeStruct(ROWS, BF16),
            jax.ShapeDtypeStruct((2, NBLK, TOK), F32),
            jax.ShapeDtypeStruct(SCORES, BF16),
            jax.ShapeDtypeStruct((NBLK, 512), F32),
            jax.ShapeDtypeStruct((NBLK, 512), F32),
        ),
        scratch_shapes=[
            pltpu.VMEM((2, EXT, D), BF16),
            pltpu.VMEM((6, 384, D), BF16),
            pltpu.VMEM((NBLK, 192, D), BF16),
            pltpu.VMEM((3, 1024, D), BF16),
            pltpu.VMEM((6, BS, 512), BF16),
            pltpu.SemaphoreType.DMA((2,)),
            pltpu.SemaphoreType.DMA((3,)),
            pltpu.SemaphoreType.DMA,
            pltpu.SemaphoreType.DMA,
            pltpu.SemaphoreType.DMA((6,)),
        ],
        input_output_aliases={6: 0},
        compiler_params=params(34),
        cost_estimate=cost(4 * NBLK * MOST * TOK * D, 20e6, 6 * BS * 512),
        name="middle",
    )(*sources, blk, *cents, rows)


def late_kernel(
    source, blk_ref, c0, c1, c2, c3, rank0, rank1, rank2, rank3, peak0, lse0, rows_in, e_in,
    rows_out, e_out, rank_ref, peak_ref, stat_ref,
    vbuf, xa, xb, x7, cb, ea, eb, lse_scr, vsem, csem, xsem, osem, esem,
):
    load = pltpu.make_async_copy(source, vbuf, vsem)
    near = pltpu.make_async_copy(rows_in.at[pl.ds(0, 6), pl.ds(512, 160), :], xa, xsem.at[0])
    far_rows = pltpu.make_async_copy(rows_in.at[pl.ds(6, 2), pl.ds(0, 672), :], xb, xsem.at[1])
    cents = [pltpu.make_async_copy(c, cb.at[k], csem.at[k]) for k, c in enumerate((c0, c1, c2, c3))]
    load.start()
    peak_ref[:, 0:512] = peak0[...]
    lse_scr[:, 0:512] = lse0[...]
    up = earlier()
    load.wait()
    for copy in (near, *cents, far_rows):
        copy.start()
    rank = ranks(vbuf[TOK:EXT, :], blk_ref[:, 0:1], up)
    rank_ref[0] = rank
    x7[...] = gathered(rank, vbuf[0:TOK, :])
    back = pltpu.make_async_copy(x7, rows_out.at[pl.ds(0, NBLK), pl.ds(672, MOST), :], osem)
    back.start()
    near.wait()

    @pl.loop(0, 3)
    def _(q):
        pltpu.make_async_copy(c0, cb.at[q], csem.at[q]).wait()
        for i in range(2):
            b = 2 * q + i
            cent = cb[q, i * BS : (i + 1) * BS, :]
            e, peak, lse = score_chunk(cent, half_norm(cent), jnp.concatenate([xa[b], x7[b]], axis=0))
            ea[b] = e
            peak_ref[pl.ds(b, 1), 512:768] = peak
            lse_scr[pl.ds(b, 1), 512:768] = lse
            pltpu.make_async_copy(ea.at[b], e_out.at[b, :, pl.ds(512, 256)], esem.at[b]).start()

    cents[3].wait()
    far_rows.wait()
    for i in range(2):
        b = 6 + i
        cent = cb[3, i * BS : (i + 1) * BS, :]
        norm = half_norm(cent)
        chunks = (xb[i, 0:256, :], xb[i, 256:512, :], jnp.concatenate([xb[i, 512:672, :], x7[b]], axis=0))
        for k, rows in enumerate(chunks):
            e, peak, lse = score_chunk(cent, norm, rows)
            eb[i, :, k * 256 : (k + 1) * 256] = e
            peak_ref[b : b + 1, k * 256 : (k + 1) * 256] = peak
            lse_scr[b : b + 1, k * 256 : (k + 1) * 256] = lse
        pltpu.make_async_copy(eb.at[i], e_out.at[b], esem.at[b]).start()

    sources = [(ref, k) for ref in (rank0, rank1, rank2, rank3, rank_ref) for k in range(ref.shape[0])]
    for s, (ref, k) in enumerate(sources):
        k0, k1 = s * MOST // 128, (s * MOST + MOST - 1) // 128
        for j in range(TOK // 128):
            r = ref[k, :, j * 128 : (j + 1) * 128].astype(jnp.int32)
            at = r + s * MOST
            low = at & 127
            got = jnp.take_along_axis(lse_scr[:, k0 * 128 : (k0 + 1) * 128], low, axis=1, mode="promise_in_bounds")
            if k1 > k0:
                other = jnp.take_along_axis(
                    lse_scr[:, k1 * 128 : (k1 + 1) * 128], low, axis=1, mode="promise_in_bounds"
                )
                got = jnp.where((at >> 7) == k0, got, other)
            got = jnp.where(r >= 0, got, LOW)
            m = jnp.max(got, axis=0, keepdims=True)
            t = jnp.sum(jnp.exp(got - m), axis=0, keepdims=True)
            stat_ref[s : s + 1, j * 128 : (j + 1) * 128] = m + jnp.log(t)

    back.wait()
    for b in range(6):
        pltpu.make_async_copy(ea.at[b], e_out.at[b, :, pl.ds(512, 256)], esem.at[b]).wait()
    for i in range(2):
        pltpu.make_async_copy(eb.at[i], e_out.at[6 + i], esem.at[6 + i]).wait()


def late_scores(source, blk, cents, ranked, peak0, lse0, rows, e):
    anywhere, hbm = pl.BlockSpec(memory_space=pl.ANY), pl.BlockSpec(memory_space=pltpu.HBM)
    vmem = pl.BlockSpec(memory_space=pltpu.VMEM)
    return pl.pallas_call(
        late_kernel,
        in_specs=[anywhere, vmem] + [anywhere] * 4 + [vmem] * 6 + [hbm] * 2,
        out_specs=(hbm, hbm, vmem, vmem, vmem),
        out_shape=(
            jax.ShapeDtypeStruct(ROWS, BF16),
            jax.ShapeDtypeStruct(SCORES, BF16),
            jax.ShapeDtypeStruct((1, NBLK, TOK), F32),
            jax.ShapeDtypeStruct((NBLK, SLOTS), F32),
            jax.ShapeDtypeStruct((NSRC, TOK), F32),
        ),
        scratch_shapes=[
            pltpu.VMEM((EXT, D), BF16),
            pltpu.VMEM((6, 160, D), BF16),
            pltpu.VMEM((2, 672, D), BF16),
            pltpu.VMEM((NBLK, MOST, D), BF16),
            pltpu.VMEM((4, 1024, D), BF16),
            pltpu.VMEM((6, BS, 256), BF16),
            pltpu.VMEM((2, BS, SLOTS), BF16),
            pltpu.VMEM((NBLK, SLOTS), F32),
            pltpu.SemaphoreType.DMA,
            pltpu.SemaphoreType.DMA((4,)),
            pltpu.SemaphoreType.DMA((2,)),
            pltpu.SemaphoreType.DMA,
            pltpu.SemaphoreType.DMA((8,)),
        ],
        input_output_aliases={12: 0, 13: 1},
        compiler_params=params(34),
        cost_estimate=cost(2 * 6 * BS * SLOTS * D, 20e6, 4 * BS * SLOTS),
        name="late_scores",
    )(source, blk, *cents, *ranked, peak0, lse0, rows, e)


def factor_kernel(stat_refs, idx_ref, peak_ref, f_scr):
    own, from_d, from_e, from_f = stat_refs
    tables = []
    for s in range(NSRC):
        parts = [own[s : s + 1, :]]
        for ref, order in ((from_d, FROM_D), (from_e, FROM_E), (from_f, FROM_F)):
            parts.append(ref[order[s] : order[s] + 1, :])
        m = jnp.maximum(jnp.maximum(parts[0], parts[1]), jnp.maximum(parts[2], parts[3]))
        t = jnp.exp(parts[0] - m)
        for k in range(1, 4):
            t = t + jnp.exp(parts[k] - m)
        tables.append(m + jnp.log(t))
    for k in range(SLOTS // 128):
        at = idx_ref[:, k * 128 : (k + 1) * 128]
        low = at & 127
        high = at >> 7
        lse = jnp.zeros((NBLK, 128), F32)
        for s in range(k * 128 // MOST, (k * 128 + 127) // MOST + 1):
            for j in range(TOK // 128):
                table = jnp.broadcast_to(tables[s][:, j * 128 : (j + 1) * 128], (NBLK, 128))
                got = jnp.take_along_axis(table, low, axis=1, mode="promise_in_bounds")
                lse = jnp.where(high == s * (TOK // 128) + j, got, lse)
        f = jnp.exp(peak_ref[:, k * 128 : (k + 1) * 128] - lse)
        f_scr[:, k * 128 : (k + 1) * 128] = jnp.where(at >= 0, f, 0.0)


def load_factors(s0, s1, s2, s3, idx0, idx1, peak_any, factor_out, f_scr, stats, idx_ref, peak_ref, sem):
    loads = [pltpu.make_async_copy(s, stats.at[k], sem.at[k]) for k, s in enumerate((s0, s1, s2, s3))]
    loads.append(pltpu.make_async_copy(idx0, idx_ref.at[:, pl.ds(0, 512)], sem.at[4]))
    loads.append(pltpu.make_async_copy(idx1, idx_ref.at[:, pl.ds(512, 256)], sem.at[5]))
    loads.append(pltpu.make_async_copy(peak_any, peak_ref, sem.at[6]))
    for load in loads:
        load.start()
    for load in loads:
        load.wait()
    factor_kernel([stats.at[k] for k in range(4)], idx_ref, peak_ref, f_scr)
    factor_out[...] = f_scr[...]


def sums_kernel(steps, n_in, *refs):
    ins, refs = refs[:n_in], refs[n_in:]
    e_any, rows_any = ins[-2:]
    n = len(steps)
    first_call = steps[0][1] == 1
    i = pl.program_id(0)
    slot = i % 2

    def at_step(k, column):
        return sum(jnp.where(k == step, entry[column], 0) for step, entry in enumerate(steps))

    def block(k):
        return 2 * at_step(k, 0) + at_step(k, 1)

    if first_call:
        outs, factor_out, f_scr, refs = refs[:5], refs[5], refs[6], refs[7:]
        (e_buf, rows_buf, esem, rsem), refs = refs[:4], refs[4:]
    else:
        outs, refs = refs[:n], refs[n:]
        (f_scr, e_buf, rows_buf, fsem, esem, rsem), refs = refs[:6], refs[6:]

    def load_block(k):
        b = block(k)
        pltpu.make_async_copy(e_any.at[b], e_buf.at[k], esem.at[k]).start()
        pltpu.make_async_copy(rows_any.at[b], rows_buf.at[k], rsem.at[k]).start()

    @pl.when(i == 0)
    def _():
        for k in range(2):
            load_block(k)
        if first_call:
            load_factors(*ins[1:8], factor_out, f_scr, *refs[:4])
        else:
            load = pltpu.make_async_copy(ins[0], f_scr, fsem)
            load.start()
            load.wait()

    @pl.when(i < n - 2)
    def _():
        load_block(i + 2)

    f = f_scr[pl.ds(block(i), 1), :]
    pltpu.make_async_copy(e_any.at[0], e_buf.at[i], esem.at[i]).wait()
    pltpu.make_async_copy(rows_any.at[0], rows_buf.at[i], rsem.at[i]).wait()
    totals, counts = [], []
    for m in range(4):
        w = e_buf[i, m * 128 : (m + 1) * 128, :].astype(F32) * f
        count = jnp.sum(w, axis=1, keepdims=True)
        counts.append(jnp.transpose(jnp.broadcast_to(count, (128, 128)))[0:EXTRA])
        totals.append(jnp.dot(w.astype(BF16), rows_buf[i], preferred_element_type=F32).astype(BF16))
    if first_call:
        part_first(i, at_step(i, 0), slot, ins[0], totals, counts, outs[:4], *refs[4:9])

        @pl.when(i == 4)
        def _():
            owner_first(0, 1, totals, counts, outs[4:], *refs[9:])
    else:
        owner_first(i, n, totals, counts, outs, *refs)


def owner_first(i, n, totals, counts, outs, buf, sem):
    for m in range(4):
        buf[i, m * 128 : (m + 1) * 128, :] = totals[m]
    tile = jnp.concatenate([*counts, jnp.zeros((EXTRA, D - BS), F32)], axis=1)
    buf[i, BS : BS + EXTRA, :] = tile.astype(BF16)
    for k in range(n):
        @pl.when(i == k)
        def _(k=k):
            pltpu.make_async_copy(buf.at[k], outs[k], sem.at[k]).start()

    @pl.when(i == n - 1)
    def _():
        for k in range(n):
            pltpu.make_async_copy(buf.at[k], outs[k], sem.at[k]).wait()


def part_first(i, q, slot, where_ref, totals, counts, outs, buf, gcount, gtile, sem, tsem):
    def send(k, slot=slot):
        start = pl.multiple_of(q * 128, 128)
        return pltpu.make_async_copy(buf.at[slot, k], outs[k].at[pl.ds(start, 128), :], sem.at[slot, k])

    def send_tile(k):
        return pltpu.make_async_copy(gtile.at[k], outs[k].at[pl.ds(BS, EXTRA), :], tsem.at[k])

    @pl.when(i == 0)
    def _():
        gcount[...] = jnp.zeros_like(gcount)

    @pl.when((i == 2) | (i == 3))
    def _():
        for k in range(4):
            send(k).wait()

    @pl.when(i < 4)
    def _():
        for m in range(4):
            at = sum(jnp.where(where_ref[4 + k] == m, k, 0) for k in range(1, 4))
            buf[slot, at] = totals[m]
            gcount[at, pl.ds(q, 1), :] = counts[m][0:1]
        for k in range(4):
            send(k).start()

    @pl.when(i == 3)
    def _():
        for k in range(4):
            tile = jnp.concatenate([gcount[k], jnp.zeros((8, 128), F32)], axis=0)
            tile = jnp.concatenate([tile, jnp.zeros((EXTRA, D - 128), F32)], axis=1)
            gtile[k] = tile.astype(BF16)
            send_tile(k).start()

    @pl.when(i == 4)
    def _():
        for other in range(2):
            for k in range(4):
                send(k, other).wait()
        for k in range(4):
            send_tile(k).wait()


SUMS_SHAPE = (BS + EXTRA, D)


def sums_call(steps, small, big, out_shape, out_specs, own):
    n = len(steps)
    first_call = steps[0][1] == 1

    def kern(*refs):
        sums_kernel(steps, len(small) + len(big), *refs)

    specs = [pl.BlockSpec(memory_space=pl.ANY)] * len(small)
    if first_call:
        specs[0] = pl.BlockSpec(memory_space=pltpu.SMEM)
    factor = [pltpu.VMEM((NBLK, SLOTS), F32)]
    return pl.pallas_call(
        kern,
        grid=(n,),
        in_specs=specs + [pl.BlockSpec(memory_space=pltpu.HBM)] * len(big),
        out_specs=out_specs,
        out_shape=out_shape,
        scratch_shapes=factor
        + [pltpu.VMEM((n, BS, SLOTS), BF16), pltpu.VMEM((n, SLOTS, D), BF16)]
        + ([] if first_call else [pltpu.SemaphoreType.DMA])
        + [pltpu.SemaphoreType.DMA((n,)), pltpu.SemaphoreType.DMA((n,))]
        + own,
        compiler_params=params(54),
        cost_estimate=cost(2 * n * BS * SLOTS * D, n * 3e6),
        name=f"sums{n}",
    )(*small, *big)


def first_sums(where, stats, idx, peak, e, rows):
    anywhere = pl.BlockSpec(memory_space=pl.ANY)
    own = [
        pltpu.VMEM((4, NSRC, TOK), F32),
        pltpu.VMEM((NBLK, SLOTS), jnp.int32),
        pltpu.VMEM((NBLK, SLOTS), F32),
        pltpu.SemaphoreType.DMA((7,)),
        pltpu.VMEM((2, 4, 128, D), BF16),
        pltpu.VMEM((4, 8, 128), F32),
        pltpu.VMEM((4, EXTRA, D), BF16),
        pltpu.SemaphoreType.DMA((2, 4)),
        pltpu.SemaphoreType.DMA((4,)),
        pltpu.VMEM((1, *SUMS_SHAPE), BF16),
        pltpu.SemaphoreType.DMA((1,)),
    ]
    *out, factor = sums_call(
        ((3, 1), (1, 1), (2, 1), (0, 1), (3, 0)),
        (where, *stats, *idx, peak),
        (e, rows),
        (jax.ShapeDtypeStruct(SUMS_SHAPE, BF16),) * 5 + (jax.ShapeDtypeStruct((NBLK, SLOTS), F32),),
        (anywhere,) * 5 + (pl.BlockSpec((NBLK, SLOTS), lambda i: (0, 0)),),
        own,
    )
    return out[:4], out[4], factor


def owner_sums(owners, factor, e, rows):
    n = len(owners)
    own = [pltpu.VMEM((n, *SUMS_SHAPE), BF16), pltpu.SemaphoreType.DMA((n,))]
    return sums_call(
        tuple((q, 0) for q in owners),
        (factor,),
        (e, rows),
        (jax.ShapeDtypeStruct(SUMS_SHAPE, BF16),) * n,
        (pl.BlockSpec(memory_space=pl.ANY),) * n,
        own,
    )


def fetched(refs, buf, sem):
    copies = [pltpu.make_async_copy(ref, buf.at[k], sem.at[k]) for k, ref in enumerate(refs)]
    for copy in copies:
        copy.start()
    for copy in copies:
        copy.wait()
    return [buf.at[k] for k in range(len(refs))]


def count_tile(counts):
    counts = jnp.broadcast_to(counts, (EXTRA, 128))
    return jnp.concatenate([counts, jnp.zeros((EXTRA, D - 128), F32)], axis=1).astype(BF16)


def owner_parts_kernel(where_ref, *refs):
    outs, (acc, buf, sem) = refs[3:7], refs[7:]
    h0, h1, h2 = fetched(refs[:3], buf, sem)
    acc[...] = h0[...].astype(F32) + h1[...].astype(F32) + h2[...].astype(F32)
    counts = acc[BS : BS + 8, 0:BS]
    for k in range(4):
        part = where_ref[4 + k]
        outs[k][0:128, :] = acc[pl.ds(pl.multiple_of(part * 128, 128), 128), :].astype(BF16)
        picked = counts[:, 0:128]
        for m in range(1, 4):
            picked = jnp.where(part == m, counts[:, m * 128 : (m + 1) * 128], picked)
        outs[k][128:, :] = count_tile(picked[0:1])


def part_owners_kernel(where_ref, *refs):
    outs, (_, buf, sem) = refs[3:7], refs[7:]
    g0, g1, g2 = fetched(refs[:3], buf, sem)
    counts = g0[BS:, 0:128].astype(F32) + g1[BS:, 0:128].astype(F32) + g2[BS:, 0:128].astype(F32)
    for k in range(4):
        rows = slice(k * 128, (k + 1) * 128)
        total = g0[rows, :].astype(F32) + g1[rows, :].astype(F32) + g2[rows, :].astype(F32)
        outs[k][0:128, :] = total.astype(BF16)
        outs[k][128:, :] = count_tile(counts[k : k + 1])


def parted(part, where, terms):
    vmem = pl.BlockSpec(memory_space=pltpu.VMEM)
    return pl.pallas_call(
        owner_parts_kernel if part == 0 else part_owners_kernel,
        in_specs=[pl.BlockSpec(memory_space=pltpu.SMEM)] + [pl.BlockSpec(memory_space=pl.ANY)] * 3,
        out_specs=(vmem,) * 4,
        out_shape=(jax.ShapeDtypeStruct((128 + EXTRA, D), BF16),) * 4,
        scratch_shapes=[
            pltpu.VMEM((BS + EXTRA, D), F32),
            pltpu.VMEM((3, BS + EXTRA, D), BF16),
            pltpu.SemaphoreType.DMA((3,)),
        ],
        compiler_params=params(12),
        cost_estimate=cost(1e6, 4e6),
        name=f"parted{part}",
    )(where, *terms)


def final_kernel(*refs):
    mine_ref, out_ref, buf, sem = refs[8:]
    h0, h1, h2, h3, g0, g1, g2, g3 = fetched(refs[:8], buf, sem)
    for i, refs in enumerate(((h0, h1, h2, h3), (g0, g1, g2, g3))):
        total = (refs[0][...].astype(F32) + refs[1][...].astype(F32)) + (refs[2][...].astype(F32) + refs[3][...].astype(F32))
        column = jnp.transpose(jnp.broadcast_to(total[128:129, 0:128], (128, 128)))[:, 0:1]
        out_ref[i] = ((total[0:128] + mine_ref[i].astype(F32)) / (column + 1.0)).astype(BF16)


def final(h, g, mine):
    return pl.pallas_call(
        final_kernel,
        in_specs=[pl.BlockSpec(memory_space=pl.ANY)] * 8 + [pl.BlockSpec(memory_space=pltpu.VMEM)],
        out_specs=pl.BlockSpec(memory_space=pltpu.VMEM),
        out_shape=jax.ShapeDtypeStruct((2, 128, D), BF16),
        scratch_shapes=[pltpu.VMEM((8, 128 + EXTRA, D), BF16), pltpu.SemaphoreType.DMA((8,))],
        compiler_params=params(8),
        cost_estimate=cost(1e6, 2e6),
        name="final",
    )(*h, *g, mine)


def place_kernel(where_ref, *refs):
    parts, (out_ref, buf, in_sem, out_sem) = refs[:8], refs[8:]
    loads = [pltpu.make_async_copy(part, buf.at[k], in_sem.at[k]) for k, part in enumerate(parts)]
    copies = []
    for side in range(2):
        for k in range(4):
            for i in range(2):
                block = where_ref[8 + side] * 2 + i
                quarter = where_ref[4 * side + k]
                copies.append(
                    pltpu.make_async_copy(
                        buf.at[side * 4 + k, i], out_ref.at[block, quarter], out_sem.at[len(copies)]
                    )
                )
    for load in loads:
        load.start()
    for k, load in enumerate(loads):
        load.wait()
        copies[2 * k].start()
        copies[2 * k + 1].start()
    for copy in copies:
        copy.wait()


def place(where, parts):
    return pl.pallas_call(
        place_kernel,
        in_specs=[pl.BlockSpec(memory_space=pltpu.SMEM)] + [pl.BlockSpec(memory_space=pl.ANY)] * 8,
        out_specs=pl.BlockSpec(memory_space=pl.ANY),
        out_shape=jax.ShapeDtypeStruct((4, 4, 128, D), BF16),
        scratch_shapes=[
            pltpu.VMEM((8, 2, 128, D), BF16),
            pltpu.SemaphoreType.DMA((8,)),
            pltpu.SemaphoreType.DMA((16,)),
        ],
        compiler_params=params(8),
        cost_estimate=cost(0, 6e6),
        name="place",
    )(where, *parts)


def tie(a, *after):
    return pl.pallas_call(
        lambda *refs: None,
        in_specs=[pl.BlockSpec(memory_space=pl.ANY)] * (1 + len(after)),
        out_specs=pl.BlockSpec(memory_space=pl.ANY),
        out_shape=jax.ShapeDtypeStruct(a.shape, a.dtype),
        input_output_aliases={0: 0},
        compiler_params=params(8),
        cost_estimate=cost(0, 0),
        name="tie",
    )(a, *after)


def add(*terms):
    total = terms[0].astype(F32)
    for t in terms[1:]:
        total = total + t.astype(F32)
    return total


def ring_terms(own, d, e, f, axis, after=None):
    r1 = turn(f, axis, 1)
    r2 = turn(d if after is None else tie(d, after), axis, -1)
    e = add(e, r1).astype(BF16)
    r3 = turn(e, axis, 1)
    return (own, r2, r3), e


def direct_terms(own, d, e, f, axis):
    return own, turn(d, axis, -1), turn(e, axis, 1), far(f, axis)


def body(vectors, centroids, candidates):
    core, x, y, z = (lax.axis_index(a) for a in ("core", "x", "y", "z"))
    step = 1 - 2 * core

    def around(i):
        return jnp.stack([i, (i - step) % 4, (i + step) % 4, (i + 2) % 4]).astype(jnp.int32)

    xs, zs = around(x), around(z)
    other_zs = jnp.stack([zs[0], zs[2], zs[1], zs[3]])

    where = jnp.concatenate([xs, zs])
    v = pack(vectors, candidates.T)
    a, b = turn(v, "y", 1), turn(v, "y", -1)
    c0 = lax.dynamic_slice_in_dim(centroids, core * 1024, 1024, 0)
    c1, c2 = turn(c0, "x", 1), turn(c0, "x", -1)
    mine = lax.dynamic_slice_in_dim(c0.reshape(2, BS, D), z * 128, 128, 1)
    blk = ((y * 4 + xs) * 4 + 2 * core)[:, None] + jnp.arange(2, dtype=jnp.int32)[None, :]
    blk = jnp.broadcast_to(blk.reshape(NBLK, 1), (NBLK, 128)).astype(F32)

    rank0, rows = dispatch(0, (v, swap(v)), blk, None)
    a = tie(a, rank0, b, c1, c2)
    c = turn(a, "y", 1)
    c3 = turn(c1, "x", 1)
    rank1, rows = dispatch(2, (a, b), blk, rows)
    rows, rank2, e, peak0, lse0 = middle((swap(a), swap(b)), blk, (c0, c1, c2), rows)
    ranked = (rank0, rank1, rank2)
    idx0 = indices(ranked, [(s, s, 0, MOST) for s in range(5)] + [(5, 5, 0, 32)])
    c = tie(c, idx0, c3)
    rank3, rows = dispatch(6, (c,), blk, rows)
    rows, e, rank4, peak, stat = late_scores(
        swap(c), blk, (c0, c1, c2, c3), (*ranked, rank3), peak0, lse0, rows, e
    )
    idx = (idx0, indices((rank2, rank3, rank4), [(5, 1, 32, MOST), (6, 2, 0, MOST), (7, 3, 0, MOST)]))

    theirs = swap(stat)
    theirs = jnp.concatenate([theirs[s : s + 1] for s in SWAPPED])
    m = jnp.maximum(stat, theirs)
    merged = m + jnp.log(jnp.exp(stat - m) + jnp.exp(theirs - m))
    stats = (merged, turn(merged, "y", 1), turn(merged, "y", -1), far(merged, "y"))

    g, h3, factor = first_sums(where, stats, idx, peak, e, rows)
    h1, h2, h0 = owner_sums((1, 2, 0), factor, e, rows)
    h, _ = ring_terms(h0, h1, h2, h3, "x", h2)
    g, _ = ring_terms(*g, "z", h0)
    h = direct_terms(*parted(0, where, h), "z")
    g = direct_terms(*parted(1, where, g), "x")
    fresh = final(h, g, mine)

    others = [turn(fresh, "z", 1), turn(fresh, "z", -1), far(fresh, "z")]
    parts = [fresh, *others] + [swap(p) for p in (fresh, *others)]
    places = jnp.concatenate([zs, other_zs, jnp.stack([core, 1 - core])]).astype(jnp.int32)
    return place(places, parts).reshape(2048, D)


def solution(mesh):
    fine = Mesh(np.asarray(mesh.devices).reshape(4, 2, 4, 4), ("z", "core", "y", "x"))
    return jax.shard_map(
        body,
        mesh=fine,
        in_specs=(P(("z", "core", "y", "x"), None), P(("y", "x"), None), P(("z", "core", "y", "x"), None)),
        out_specs=P(("y", "x"), None),
        check_vma=False,
    )
```

```python
import jax
import jax.numpy as jnp
import numpy as np
from jax import lax
from jax.experimental import pallas as pl
from jax.experimental.pallas import tpu as pltpu
from jax.sharding import Mesh, PartitionSpec as P

BS = 512
MOST = 96
TOK = 1024
D = 768
NSRC = 8
NBLK = 8
SLOTS = NSRC * MOST
EXTRA = 16
EXT = TOK + EXTRA
ROWS = (28, SLOTS, D)
SCORES = (40, BS, SLOTS)
LOW = -1e30
F32 = jnp.float32
BF16 = jnp.bfloat16

NAMES = ("v", "v'", "a", "b", "a'", "b'", "c", "c'")


def order(**came):
    return tuple(NAMES.index(came[n.replace("'", "_")]) for n in NAMES)


SWAPPED = order(v="v'", v_="v", a="a'", a_="a", b="b'", b_="b", c="c'", c_="c")
FROM_D = order(a="v", b_="v'", c="a", v_="a'", v="b", c_="b'", b="c", a_="c'")
FROM_E = order(b="v", a_="v'", v="a", c_="a'", c="b", v_="b'", a="c", b_="c'")
FROM_F = order(c="v", c_="v'", b="a", b_="a'", a="b", a_="b'", v="c", v_="c'")


def turn(a, axis, sign):
    axes = ("z", "core") if axis == "z" else ("core", axis)
    at = (lambda core, i: i * 2 + core) if axis == "z" else (lambda core, i: core * 4 + i)
    pairs = []
    for core in range(2):
        for i in range(4):
            pairs.append((at(core, i), at(core, (i + (sign if core == 0 else -sign)) % 4)))
    return lax.ppermute(a, axes, pairs)


def far(a, axis):
    return lax.ppermute(a, axis, [(i, (i + 2) % 4) for i in range(4)])


def swap(a):
    return lax.ppermute(a, "core", [(0, 1), (1, 0)])


def params(mib):
    return pltpu.CompilerParams(vmem_limit_bytes=mib * 1024 * 1024)


def cost(flops, nbytes, trans=0):
    return pl.CostEstimate(flops=int(flops), bytes_accessed=int(nbytes), transcendentals=int(trans))


def earlier():
    up = lax.broadcasted_iota(jnp.int32, (TOK, TOK), 0) < lax.broadcasted_iota(jnp.int32, (TOK, TOK), 1)
    return jnp.where(up, 1.0, 0.0).astype(BF16)


def pack_kernel(vectors, cand_ref, out, buf, in_sem, out_sem):
    loads, stores = [], []
    for k in range(2):
        rows = pl.ds(k * 512, 512)
        loads.append(pltpu.make_async_copy(vectors.at[rows, :], buf.at[rows, :], in_sem.at[k]))
        stores.append(pltpu.make_async_copy(buf.at[rows, :], out.at[rows, :], out_sem.at[k]))
        loads[k].start()
    cand = cand_ref[...].astype(F32)
    halves = [cand[pick : pick + 1, h * 512 : (h + 1) * 512] for pick in range(4) for h in range(2)]
    tail = jnp.concatenate([*halves, jnp.zeros((EXTRA - 8, 512), F32)], axis=0)
    tail = jnp.concatenate([tail, jnp.zeros((EXTRA, D - 512), F32)], axis=1)
    buf[TOK:EXT, :] = tail.astype(BF16)
    end = pltpu.make_async_copy(buf.at[pl.ds(TOK, EXTRA), :], out.at[pl.ds(TOK, EXTRA), :], out_sem.at[4])
    end.start()
    for load, store in zip(loads, stores):
        load.wait()
        store.start()
    for store in (*stores, end):
        store.wait()


def pack(vectors, cand):
    anywhere = pl.BlockSpec(memory_space=pl.ANY)
    return pl.pallas_call(
        pack_kernel,
        in_specs=[anywhere, pl.BlockSpec(memory_space=pltpu.VMEM)],
        out_specs=anywhere,
        out_shape=jax.ShapeDtypeStruct((EXT, D), BF16),
        scratch_shapes=[
            pltpu.VMEM((EXT, D), BF16),
            pltpu.SemaphoreType.DMA((4,)),
            pltpu.SemaphoreType.DMA((5,)),
        ],
        compiler_params=params(60),
        cost_estimate=cost(0, 3e6),
        name="pack",
    )(vectors, cand)


def ranks(tail, blk, up):
    tail = tail.astype(F32)
    hit = None
    for pick in range(4):
        named = jnp.concatenate([tail[2 * pick : 2 * pick + 1, 0:512], tail[2 * pick + 1 : 2 * pick + 2, 0:512]], axis=1)
        m = named == blk
        hit = m if hit is None else hit | m
    hit = jnp.where(hit, 1.0, 0.0)
    hits = jnp.concatenate([hit, jnp.zeros((8, TOK), F32)], axis=0).astype(BF16)
    before = jnp.dot(hits, up, preferred_element_type=F32)[0:NBLK]
    return jnp.where(hit > 0, before, -1.0)


def gathered(rank, vectors):
    slot = lax.broadcasted_iota(jnp.int32, (MOST, TOK), 0).astype(F32)
    hot = [jnp.where(slot == rank[b : b + 1, :], 1.0, 0.0).astype(BF16) for b in range(NBLK)]
    hot = jnp.concatenate(hot, axis=0)
    rows = jnp.dot(hot, vectors, preferred_element_type=F32).astype(BF16)
    return rows.reshape(NBLK, MOST, D)


def index_kernel(pieces, *refs):
    rank_refs, idx_ref = refs[:-1], refs[-1]
    sources = [(ref, k) for ref in rank_refs for k in range(ref.shape[0])]
    row = lax.broadcasted_iota(jnp.int32, (8, TOK), 0)
    v = lax.broadcasted_iota(jnp.int32, (8, TOK), 1)
    place = jnp.where(row == 0, v >> 3, jnp.where(row == 1, v & 7, jnp.where(row == 2, 1, 0)))
    place = place.astype(F32).astype(BF16)
    lane = lax.broadcasted_iota(jnp.int32, (1, idx_ref.shape[1]), 1)
    base, end = jnp.zeros(lane.shape, F32), 0
    for s, _, lo, hi in pieces:
        base = jnp.where(lane >= end, float(s * TOK), base)
        end += hi - lo
    for b in range(NBLK):
        hot = []
        for _, at, lo, hi in pieces:
            ref, k = sources[at]
            slot = (lax.broadcasted_iota(jnp.int32, (hi - lo, TOK), 0) + lo).astype(F32)
            hot.append(jnp.where(slot == ref[k, b : b + 1, :], 1.0, 0.0).astype(BF16))
        hot = jnp.concatenate(hot, axis=0)
        found = lax.dot_general(place, hot, (((1,), (1,)), ((), ())), preferred_element_type=F32)
        where = found[0:1] * 8.0 + found[1:2] + base
        idx_ref[b : b + 1, :] = jnp.where(found[2:3] > 0, where, -1.0).astype(jnp.int32)


def indices(ranked, pieces):
    def kern(*refs):
        index_kernel(pieces, *refs)

    width = sum(hi - lo for _, _, lo, hi in pieces)
    return pl.pallas_call(
        kern,
        out_shape=jax.ShapeDtypeStruct((NBLK, width), jnp.int32),
        compiler_params=params(12),
        cost_estimate=cost(4e9, 1e6),
        name="indices",
    )(*ranked)


def dispatch_kernel(n, *refs):
    sources, blk_ref, (rank_ref, out_ref, buf, sems, up) = refs[:n], refs[n], refs[-5:]
    i = pl.program_id(0)

    def copy(k):
        return pltpu.make_async_copy(sources[k], buf.at[k % 2], sems.at[k % 2])

    @pl.when(i == 0)
    def _():
        copy(0).start()
        up[...] = earlier()

    for k in range(n):
        @pl.when(i == k)
        def _(k=k):
            if k + 1 < n:
                copy(k + 1).start()
            copy(k).wait()

    rank = ranks(buf[i % 2, TOK:EXT, :], blk_ref[:, 0:1], up[...])
    rank_ref[0] = rank
    out_ref[...] = gathered(rank, buf[i % 2, 0:TOK, :])


def dispatch(first, sources, blk, rows):
    n = len(sources)
    anywhere = pl.BlockSpec(memory_space=pl.ANY)
    in_specs = [anywhere] * n + [pl.BlockSpec((NBLK, 128), lambda i: (0, 0))]
    args = [*sources, blk]
    alias = {}
    if rows is not None:
        in_specs.append(pl.BlockSpec(memory_space=pltpu.HBM))
        args.append(rows)
        alias = {n + 1: 1}

    def kern(*refs):
        dispatch_kernel(n, *refs)

    return pl.pallas_call(
        kern,
        grid=(n,),
        in_specs=in_specs,
        out_specs=(
            pl.BlockSpec((1, NBLK, TOK), lambda i: (i, 0, 0)),
            pl.BlockSpec((NBLK, MOST, D), lambda i: (0, first + i, 0)),
        ),
        out_shape=(
            jax.ShapeDtypeStruct((n, NBLK, TOK), F32),
            jax.ShapeDtypeStruct(ROWS, BF16),
        ),
        scratch_shapes=[
            pltpu.VMEM((2, EXT, D), BF16),
            pltpu.SemaphoreType.DMA((2,)),
            pltpu.VMEM((TOK, TOK), BF16),
        ],
        input_output_aliases=alias,
        compiler_params=params(34),
        cost_estimate=cost(2 * n * NBLK * MOST * TOK * D, n * 3e6),
        name=f"dispatch{first}",
    )(*args)


def half_norm(cent):
    wide = cent.astype(F32)
    return 0.5 * jnp.sum(wide * wide, axis=1, keepdims=True)


def score_chunk(cent, norm, rows):
    raw = lax.dot_general(cent, rows, (((1,), (1,)), ((), ())), preferred_element_type=F32)
    score = raw - norm
    peak = jnp.max(score, axis=0, keepdims=True)
    e = jnp.exp(score - peak)
    return e.astype(BF16), peak, peak + jnp.log(jnp.sum(e, axis=0, keepdims=True))


def middle_kernel(
    s0, s1, blk_ref, c0, c1, c2, rows_in,
    rows_out, rank_ref, e_out, peak_ref, lse_ref,
    vbuf, x03, x45, cb, eb, vsem, csem, xsem, osem, esem,
):
    sources = [pltpu.make_async_copy(s, vbuf.at[k], vsem.at[k]) for k, s in enumerate((s0, s1))]
    cents = [pltpu.make_async_copy(c, cb.at[k], csem.at[k]) for k, c in enumerate((c0, c1, c2))]
    first = pltpu.make_async_copy(rows_in.at[pl.ds(0, 6), pl.ds(0, 384), :], x03, xsem)
    for copy in sources:
        copy.start()
    up = earlier()
    for k in range(2):
        sources[k].wait()
        for copy in (first, cents[0]) if k == 0 else cents[1:]:
            copy.start()
        rank = ranks(vbuf[k, TOK:EXT, :], blk_ref[:, 0:1], up)
        rank_ref[k] = rank
        x45[:, k * MOST : (k + 1) * MOST, :] = gathered(rank, vbuf[k, 0:TOK, :])
    back = pltpu.make_async_copy(x45, rows_out.at[pl.ds(0, NBLK), pl.ds(384, 192), :], osem)
    back.start()
    first.wait()
    for q in range(3):
        cents[q].wait()
        for i in range(2):
            b = 2 * q + i
            cent = cb[q, i * BS : (i + 1) * BS, :]
            norm = half_norm(cent)
            chunks = (x03[b, 0:256, :], jnp.concatenate([x03[b, 256:384, :], x45[b, 0:128, :]], axis=0))
            for k, rows in enumerate(chunks):
                e, peak, lse = score_chunk(cent, norm, rows)
                eb[b, :, k * 256 : (k + 1) * 256] = e
                peak_ref[b : b + 1, k * 256 : (k + 1) * 256] = peak
                lse_ref[b : b + 1, k * 256 : (k + 1) * 256] = lse
            pltpu.make_async_copy(eb.at[b], e_out.at[b, :, pl.ds(0, 512)], esem.at[b]).start()
    back.wait()
    for b in range(6):
        pltpu.make_async_copy(eb.at[b], e_out.at[b, :, pl.ds(0, 512)], esem.at[b]).wait()


def middle(sources, blk, cents, rows):
    anywhere, hbm = pl.BlockSpec(memory_space=pl.ANY), pl.BlockSpec(memory_space=pltpu.HBM)
    vmem = pl.BlockSpec(memory_space=pltpu.VMEM)
    return pl.pallas_call(
        middle_kernel,
        in_specs=[anywhere] * 2 + [vmem] + [anywhere] * 3 + [hbm],
        out_specs=(hbm, vmem, hbm, vmem, vmem),
        out_shape=(
            jax.ShapeDtypeStruct(ROWS, BF16),
            jax.ShapeDtypeStruct((2, NBLK, TOK), F32),
            jax.ShapeDtypeStruct(SCORES, BF16),
            jax.ShapeDtypeStruct((NBLK, 512), F32),
            jax.ShapeDtypeStruct((NBLK, 512), F32),
        ),
        scratch_shapes=[
            pltpu.VMEM((2, EXT, D), BF16),
            pltpu.VMEM((6, 384, D), BF16),
            pltpu.VMEM((NBLK, 192, D), BF16),
            pltpu.VMEM((3, 1024, D), BF16),
            pltpu.VMEM((6, BS, 512), BF16),
            pltpu.SemaphoreType.DMA((2,)),
            pltpu.SemaphoreType.DMA((3,)),
            pltpu.SemaphoreType.DMA,
            pltpu.SemaphoreType.DMA,
            pltpu.SemaphoreType.DMA((6,)),
        ],
        input_output_aliases={6: 0},
        compiler_params=params(34),
        cost_estimate=cost(4 * NBLK * MOST * TOK * D, 20e6, 6 * BS * 512),
        name="middle",
    )(*sources, blk, *cents, rows)


def late_kernel(
    source, blk_ref, c0, c1, c2, c3, rank0, rank1, rank2, rank3, peak0, lse0, rows_in, e_in,
    rows_out, e_out, rank_ref, peak_ref, stat_ref,
    vbuf, xa, xb, x7, cb, ea, eb, lse_scr, vsem, csem, xsem, osem, esem,
):
    load = pltpu.make_async_copy(source, vbuf, vsem)
    near = pltpu.make_async_copy(rows_in.at[pl.ds(0, 6), pl.ds(512, 160), :], xa, xsem.at[0])
    far_rows = pltpu.make_async_copy(rows_in.at[pl.ds(6, 2), pl.ds(0, 672), :], xb, xsem.at[1])
    cents = [pltpu.make_async_copy(c, cb.at[k], csem.at[k]) for k, c in enumerate((c0, c1, c2, c3))]
    load.start()
    peak_ref[:, 0:512] = peak0[...]
    lse_scr[:, 0:512] = lse0[...]
    up = earlier()
    load.wait()
    for copy in (near, *cents, far_rows):
        copy.start()
    rank = ranks(vbuf[TOK:EXT, :], blk_ref[:, 0:1], up)
    rank_ref[0] = rank
    x7[...] = gathered(rank, vbuf[0:TOK, :])
    back = pltpu.make_async_copy(x7, rows_out.at[pl.ds(0, NBLK), pl.ds(672, MOST), :], osem)
    back.start()
    near.wait()

    @pl.loop(0, 3)
    def _(q):
        pltpu.make_async_copy(c0, cb.at[q], csem.at[q]).wait()
        for i in range(2):
            b = 2 * q + i
            cent = cb[q, i * BS : (i + 1) * BS, :]
            e, peak, lse = score_chunk(cent, half_norm(cent), jnp.concatenate([xa[b], x7[b]], axis=0))
            ea[b] = e
            peak_ref[pl.ds(b, 1), 512:768] = peak
            lse_scr[pl.ds(b, 1), 512:768] = lse
            pltpu.make_async_copy(ea.at[b], e_out.at[b, :, pl.ds(512, 256)], esem.at[b]).start()

    cents[3].wait()
    far_rows.wait()
    for i in range(2):
        b = 6 + i
        cent = cb[3, i * BS : (i + 1) * BS, :]
        norm = half_norm(cent)
        chunks = (xb[i, 0:256, :], xb[i, 256:512, :], jnp.concatenate([xb[i, 512:672, :], x7[b]], axis=0))
        for k, rows in enumerate(chunks):
            e, peak, lse = score_chunk(cent, norm, rows)
            eb[i, :, k * 256 : (k + 1) * 256] = e
            peak_ref[b : b + 1, k * 256 : (k + 1) * 256] = peak
            lse_scr[b : b + 1, k * 256 : (k + 1) * 256] = lse
        pltpu.make_async_copy(eb.at[i], e_out.at[b], esem.at[b]).start()

    sources = [(ref, k) for ref in (rank0, rank1, rank2, rank3, rank_ref) for k in range(ref.shape[0])]
    for s, (ref, k) in enumerate(sources):
        k0, k1 = s * MOST // 128, (s * MOST + MOST - 1) // 128
        for j in range(TOK // 128):
            r = ref[k, :, j * 128 : (j + 1) * 128].astype(jnp.int32)
            at = r + s * MOST
            low = at & 127
            got = jnp.take_along_axis(lse_scr[:, k0 * 128 : (k0 + 1) * 128], low, axis=1, mode="promise_in_bounds")
            if k1 > k0:
                other = jnp.take_along_axis(
                    lse_scr[:, k1 * 128 : (k1 + 1) * 128], low, axis=1, mode="promise_in_bounds"
                )
                got = jnp.where((at >> 7) == k0, got, other)
            got = jnp.where(r >= 0, got, LOW)
            m = jnp.max(got, axis=0, keepdims=True)
            t = jnp.sum(jnp.exp(got - m), axis=0, keepdims=True)
            stat_ref[s : s + 1, j * 128 : (j + 1) * 128] = m + jnp.log(t)

    back.wait()
    for b in range(6):
        pltpu.make_async_copy(ea.at[b], e_out.at[b, :, pl.ds(512, 256)], esem.at[b]).wait()
    for i in range(2):
        pltpu.make_async_copy(eb.at[i], e_out.at[6 + i], esem.at[6 + i]).wait()


def late_scores(source, blk, cents, ranked, peak0, lse0, rows, e):
    anywhere, hbm = pl.BlockSpec(memory_space=pl.ANY), pl.BlockSpec(memory_space=pltpu.HBM)
    vmem = pl.BlockSpec(memory_space=pltpu.VMEM)
    return pl.pallas_call(
        late_kernel,
        in_specs=[anywhere, vmem] + [anywhere] * 4 + [vmem] * 6 + [hbm] * 2,
        out_specs=(hbm, hbm, vmem, vmem, vmem),
        out_shape=(
            jax.ShapeDtypeStruct(ROWS, BF16),
            jax.ShapeDtypeStruct(SCORES, BF16),
            jax.ShapeDtypeStruct((1, NBLK, TOK), F32),
            jax.ShapeDtypeStruct((NBLK, SLOTS), F32),
            jax.ShapeDtypeStruct((NSRC, TOK), F32),
        ),
        scratch_shapes=[
            pltpu.VMEM((EXT, D), BF16),
            pltpu.VMEM((6, 160, D), BF16),
            pltpu.VMEM((2, 672, D), BF16),
            pltpu.VMEM((NBLK, MOST, D), BF16),
            pltpu.VMEM((4, 1024, D), BF16),
            pltpu.VMEM((6, BS, 256), BF16),
            pltpu.VMEM((2, BS, SLOTS), BF16),
            pltpu.VMEM((NBLK, SLOTS), F32),
            pltpu.SemaphoreType.DMA,
            pltpu.SemaphoreType.DMA((4,)),
            pltpu.SemaphoreType.DMA((2,)),
            pltpu.SemaphoreType.DMA,
            pltpu.SemaphoreType.DMA((8,)),
        ],
        input_output_aliases={12: 0, 13: 1},
        compiler_params=params(34),
        cost_estimate=cost(2 * 6 * BS * SLOTS * D, 20e6, 4 * BS * SLOTS),
        name="late_scores",
    )(source, blk, *cents, *ranked, peak0, lse0, rows, e)


def factor_kernel(stat_refs, idx_ref, peak_ref, f_scr):
    own, from_d, from_e, from_f = stat_refs
    tables = []
    for s in range(NSRC):
        parts = [own[s : s + 1, :]]
        for ref, order in ((from_d, FROM_D), (from_e, FROM_E), (from_f, FROM_F)):
            parts.append(ref[order[s] : order[s] + 1, :])
        m = jnp.maximum(jnp.maximum(parts[0], parts[1]), jnp.maximum(parts[2], parts[3]))
        t = jnp.exp(parts[0] - m)
        for k in range(1, 4):
            t = t + jnp.exp(parts[k] - m)
        tables.append(m + jnp.log(t))
    for k in range(SLOTS // 128):
        at = idx_ref[:, k * 128 : (k + 1) * 128]
        low = at & 127
        high = at >> 7
        lse = jnp.zeros((NBLK, 128), F32)
        for s in range(k * 128 // MOST, (k * 128 + 127) // MOST + 1):
            for j in range(TOK // 128):
                table = jnp.broadcast_to(tables[s][:, j * 128 : (j + 1) * 128], (NBLK, 128))
                got = jnp.take_along_axis(table, low, axis=1, mode="promise_in_bounds")
                lse = jnp.where(high == s * (TOK // 128) + j, got, lse)
        f = jnp.exp(peak_ref[:, k * 128 : (k + 1) * 128] - lse)
        f_scr[:, k * 128 : (k + 1) * 128] = jnp.where(at >= 0, f, 0.0)


def load_factors(s0, s1, s2, s3, idx0, idx1, peak_any, factor_out, f_scr, stats, idx_ref, peak_ref, sem, load_block):
    loads = [pltpu.make_async_copy(s, stats.at[k], sem.at[k]) for k, s in enumerate((s0, s1, s2, s3))]
    loads.append(pltpu.make_async_copy(idx0, idx_ref.at[:, pl.ds(0, 512)], sem.at[4]))
    loads.append(pltpu.make_async_copy(idx1, idx_ref.at[:, pl.ds(512, 256)], sem.at[5]))
    loads.append(pltpu.make_async_copy(peak_any, peak_ref, sem.at[6]))
    for load in loads:
        load.start()
    load_block(0)
    for load in loads:
        load.wait()
    load_block(1)
    factor_kernel([stats.at[k] for k in range(4)], idx_ref, peak_ref, f_scr)
    factor_out[...] = f_scr[...]


def sums_kernel(steps, n_in, *refs):
    ins, refs = refs[:n_in], refs[n_in:]
    e_any, rows_any = ins[-2:]
    n = len(steps)
    first_call = steps[0][1] == 1
    i = pl.program_id(0)
    slot = i % 2

    def at_step(k, column):
        return sum(jnp.where(k == step, entry[column], 0) for step, entry in enumerate(steps))

    def block(k):
        return 2 * at_step(k, 0) + at_step(k, 1)

    if first_call:
        outs, factor_out, f_scr, refs = refs[:5], refs[5], refs[6], refs[7:]
        (e_buf, rows_buf, esem, rsem), refs = refs[:4], refs[4:]
    else:
        outs, refs = refs[:n], refs[n:]
        (f_scr, e_buf, rows_buf, fsem, esem, rsem), refs = refs[:6], refs[6:]

    def load_block(k):
        b = block(k)
        pltpu.make_async_copy(e_any.at[b], e_buf.at[k], esem.at[k]).start()
        pltpu.make_async_copy(rows_any.at[b], rows_buf.at[k], rsem.at[k]).start()

    @pl.when(i == 0)
    def _():
        if first_call:
            load_factors(*ins[1:8], factor_out, f_scr, *refs[:4], load_block)
        else:
            for k in range(2):
                load_block(k)
            load = pltpu.make_async_copy(ins[0], f_scr, fsem)
            load.start()
            load.wait()

    @pl.when(i < n - 2)
    def _():
        load_block(i + 2)

    f = f_scr[pl.ds(block(i), 1), :]
    pltpu.make_async_copy(e_any.at[0], e_buf.at[i], esem.at[i]).wait()
    pltpu.make_async_copy(rows_any.at[0], rows_buf.at[i], rsem.at[i]).wait()
    totals, counts = [], []
    for m in range(4):
        w = e_buf[i, m * 128 : (m + 1) * 128, :].astype(F32) * f
        count = jnp.sum(w, axis=1, keepdims=True)
        counts.append(jnp.transpose(jnp.broadcast_to(count, (128, 128)))[0:EXTRA])
        totals.append(jnp.dot(w.astype(BF16), rows_buf[i], preferred_element_type=F32).astype(BF16))
    if first_call:
        part_first(i, at_step(i, 0), slot, ins[0], totals, counts, outs[:4], *refs[4:9])

        @pl.when(i == 4)
        def _():
            owner_first(0, 1, totals, counts, outs[4:], *refs[9:])
    else:
        owner_first(i, n, totals, counts, outs, *refs)


def owner_first(i, n, totals, counts, outs, buf, sem):
    for m in range(4):
        buf[i, m * 128 : (m + 1) * 128, :] = totals[m]
    tile = jnp.concatenate([*counts, jnp.zeros((EXTRA, D - BS), F32)], axis=1)
    buf[i, BS : BS + EXTRA, :] = tile.astype(BF16)
    for k in range(n):
        @pl.when(i == k)
        def _(k=k):
            pltpu.make_async_copy(buf.at[k], outs[k], sem.at[k]).start()

    @pl.when(i == n - 1)
    def _():
        for k in range(n):
            pltpu.make_async_copy(buf.at[k], outs[k], sem.at[k]).wait()


def part_first(i, q, slot, where_ref, totals, counts, outs, buf, gcount, gtile, sem, tsem):
    def send(k, slot=slot):
        start = pl.multiple_of(q * 128, 128)
        return pltpu.make_async_copy(buf.at[slot, k], outs[k].at[pl.ds(start, 128), :], sem.at[slot, k])

    def send_tile(k):
        return pltpu.make_async_copy(gtile.at[k], outs[k].at[pl.ds(BS, EXTRA), :], tsem.at[k])

    @pl.when(i == 0)
    def _():
        gcount[...] = jnp.zeros_like(gcount)

    @pl.when((i == 2) | (i == 3))
    def _():
        for k in range(4):
            send(k).wait()

    @pl.when(i < 4)
    def _():
        for m in range(4):
            at = sum(jnp.where(where_ref[4 + k] == m, k, 0) for k in range(1, 4))
            buf[slot, at] = totals[m]
            gcount[at, pl.ds(q, 1), :] = counts[m][0:1]
        for k in range(4):
            send(k).start()

    @pl.when(i == 3)
    def _():
        for k in range(4):
            tile = jnp.concatenate([gcount[k], jnp.zeros((8, 128), F32)], axis=0)
            tile = jnp.concatenate([tile, jnp.zeros((EXTRA, D - 128), F32)], axis=1)
            gtile[k] = tile.astype(BF16)
            send_tile(k).start()

    @pl.when(i == 4)
    def _():
        for other in range(2):
            for k in range(4):
                send(k, other).wait()
        for k in range(4):
            send_tile(k).wait()


SUMS_SHAPE = (BS + EXTRA, D)


def sums_call(steps, small, big, out_shape, out_specs, own):
    n = len(steps)
    first_call = steps[0][1] == 1

    def kern(*refs):
        sums_kernel(steps, len(small) + len(big), *refs)

    specs = [pl.BlockSpec(memory_space=pl.ANY)] * len(small)
    if first_call:
        specs[0] = pl.BlockSpec(memory_space=pltpu.SMEM)
    factor = [pltpu.VMEM((NBLK, SLOTS), F32)]
    return pl.pallas_call(
        kern,
        grid=(n,),
        in_specs=specs + [pl.BlockSpec(memory_space=pltpu.HBM)] * len(big),
        out_specs=out_specs,
        out_shape=out_shape,
        scratch_shapes=factor
        + [pltpu.VMEM((n, BS, SLOTS), BF16), pltpu.VMEM((n, SLOTS, D), BF16)]
        + ([] if first_call else [pltpu.SemaphoreType.DMA])
        + [pltpu.SemaphoreType.DMA((n,)), pltpu.SemaphoreType.DMA((n,))]
        + own,
        compiler_params=params(54),
        cost_estimate=cost(2 * n * BS * SLOTS * D, n * 3e6),
        name=f"sums{n}",
    )(*small, *big)


def first_sums(where, stats, idx, peak, e, rows):
    anywhere = pl.BlockSpec(memory_space=pl.ANY)
    own = [
        pltpu.VMEM((4, NSRC, TOK), F32),
        pltpu.VMEM((NBLK, SLOTS), jnp.int32),
        pltpu.VMEM((NBLK, SLOTS), F32),
        pltpu.SemaphoreType.DMA((7,)),
        pltpu.VMEM((2, 4, 128, D), BF16),
        pltpu.VMEM((4, 8, 128), F32),
        pltpu.VMEM((4, EXTRA, D), BF16),
        pltpu.SemaphoreType.DMA((2, 4)),
        pltpu.SemaphoreType.DMA((4,)),
        pltpu.VMEM((1, *SUMS_SHAPE), BF16),
        pltpu.SemaphoreType.DMA((1,)),
    ]
    *out, factor = sums_call(
        ((3, 1), (1, 1), (2, 1), (0, 1), (3, 0)),
        (where, *stats, *idx, peak),
        (e, rows),
        (jax.ShapeDtypeStruct(SUMS_SHAPE, BF16),) * 5 + (jax.ShapeDtypeStruct((NBLK, SLOTS), F32),),
        (anywhere,) * 5 + (pl.BlockSpec((NBLK, SLOTS), lambda i: (0, 0)),),
        own,
    )
    return out[:4], out[4], factor


def owner_sums(owners, factor, e, rows):
    n = len(owners)
    own = [pltpu.VMEM((n, *SUMS_SHAPE), BF16), pltpu.SemaphoreType.DMA((n,))]
    return sums_call(
        tuple((q, 0) for q in owners),
        (factor,),
        (e, rows),
        (jax.ShapeDtypeStruct(SUMS_SHAPE, BF16),) * n,
        (pl.BlockSpec(memory_space=pl.ANY),) * n,
        own,
    )


def fetched(refs, buf, sem):
    copies = [pltpu.make_async_copy(ref, buf.at[k], sem.at[k]) for k, ref in enumerate(refs)]
    for copy in copies:
        copy.start()
    for copy in copies:
        copy.wait()
    return [buf.at[k] for k in range(len(refs))]


def count_tile(counts):
    counts = jnp.broadcast_to(counts, (EXTRA, 128))
    return jnp.concatenate([counts, jnp.zeros((EXTRA, D - 128), F32)], axis=1).astype(BF16)


def owner_parts_kernel(where_ref, *refs):
    outs, (acc, buf, sem) = refs[3:7], refs[7:]
    h0, h1, h2 = fetched(refs[:3], buf, sem)
    acc[...] = h0[...].astype(F32) + h1[...].astype(F32) + h2[...].astype(F32)
    counts = acc[BS : BS + 8, 0:BS]
    for k in range(4):
        part = where_ref[4 + k]
        outs[k][0:128, :] = acc[pl.ds(pl.multiple_of(part * 128, 128), 128), :].astype(BF16)
        picked = counts[:, 0:128]
        for m in range(1, 4):
            picked = jnp.where(part == m, counts[:, m * 128 : (m + 1) * 128], picked)
        outs[k][128:, :] = count_tile(picked[0:1])


def part_owners_kernel(where_ref, *refs):
    outs, (_, buf, sem) = refs[3:7], refs[7:]
    g0, g1, g2 = fetched(refs[:3], buf, sem)
    counts = g0[BS:, 0:128].astype(F32) + g1[BS:, 0:128].astype(F32) + g2[BS:, 0:128].astype(F32)
    for k in range(4):
        rows = slice(k * 128, (k + 1) * 128)
        total = g0[rows, :].astype(F32) + g1[rows, :].astype(F32) + g2[rows, :].astype(F32)
        outs[k][0:128, :] = total.astype(BF16)
        outs[k][128:, :] = count_tile(counts[k : k + 1])


def parted(part, where, terms):
    vmem = pl.BlockSpec(memory_space=pltpu.VMEM)
    return pl.pallas_call(
        owner_parts_kernel if part == 0 else part_owners_kernel,
        in_specs=[pl.BlockSpec(memory_space=pltpu.SMEM)] + [pl.BlockSpec(memory_space=pl.ANY)] * 3,
        out_specs=(vmem,) * 4,
        out_shape=(jax.ShapeDtypeStruct((128 + EXTRA, D), BF16),) * 4,
        scratch_shapes=[
            pltpu.VMEM((BS + EXTRA, D), F32),
            pltpu.VMEM((3, BS + EXTRA, D), BF16),
            pltpu.SemaphoreType.DMA((3,)),
        ],
        compiler_params=params(12),
        cost_estimate=cost(1e6, 4e6),
        name=f"parted{part}",
    )(where, *terms)


def final_kernel(*refs):
    mine_ref, out_ref, buf, sem = refs[8:]
    h0, h1, h2, h3, g0, g1, g2, g3 = fetched(refs[:8], buf, sem)
    for i, refs in enumerate(((h0, h1, h2, h3), (g0, g1, g2, g3))):
        total = (refs[0][...].astype(F32) + refs[1][...].astype(F32)) + (refs[2][...].astype(F32) + refs[3][...].astype(F32))
        column = jnp.transpose(jnp.broadcast_to(total[128:129, 0:128], (128, 128)))[:, 0:1]
        out_ref[i] = ((total[0:128] + mine_ref[i].astype(F32)) / (column + 1.0)).astype(BF16)


def final(h, g, mine):
    return pl.pallas_call(
        final_kernel,
        in_specs=[pl.BlockSpec(memory_space=pl.ANY)] * 8 + [pl.BlockSpec(memory_space=pltpu.VMEM)],
        out_specs=pl.BlockSpec(memory_space=pltpu.VMEM),
        out_shape=jax.ShapeDtypeStruct((2, 128, D), BF16),
        scratch_shapes=[pltpu.VMEM((8, 128 + EXTRA, D), BF16), pltpu.SemaphoreType.DMA((8,))],
        compiler_params=params(8),
        cost_estimate=cost(1e6, 2e6),
        name="final",
    )(*h, *g, mine)


def place_kernel(where_ref, *refs):
    parts, (out_ref, buf, in_sem, out_sem) = refs[:8], refs[8:]
    loads = [pltpu.make_async_copy(part, buf.at[k], in_sem.at[k]) for k, part in enumerate(parts)]
    copies = []
    for side in range(2):
        for k in range(4):
            for i in range(2):
                block = where_ref[8 + side] * 2 + i
                quarter = where_ref[4 * side + k]
                copies.append(
                    pltpu.make_async_copy(
                        buf.at[side * 4 + k, i], out_ref.at[block, quarter], out_sem.at[len(copies)]
                    )
                )
    for load in loads:
        load.start()
    for k, load in enumerate(loads):
        load.wait()
        copies[2 * k].start()
        copies[2 * k + 1].start()
    for copy in copies:
        copy.wait()


def place(where, parts):
    return pl.pallas_call(
        place_kernel,
        in_specs=[pl.BlockSpec(memory_space=pltpu.SMEM)] + [pl.BlockSpec(memory_space=pl.ANY)] * 8,
        out_specs=pl.BlockSpec(memory_space=pl.ANY),
        out_shape=jax.ShapeDtypeStruct((4, 4, 128, D), BF16),
        scratch_shapes=[
            pltpu.VMEM((8, 2, 128, D), BF16),
            pltpu.SemaphoreType.DMA((8,)),
            pltpu.SemaphoreType.DMA((16,)),
        ],
        compiler_params=params(8),
        cost_estimate=cost(0, 6e6),
        name="place",
    )(where, *parts)


def tie(a, *after):
    return pl.pallas_call(
        lambda *refs: None,
        in_specs=[pl.BlockSpec(memory_space=pl.ANY)] * (1 + len(after)),
        out_specs=pl.BlockSpec(memory_space=pl.ANY),
        out_shape=jax.ShapeDtypeStruct(a.shape, a.dtype),
        input_output_aliases={0: 0},
        compiler_params=params(8),
        cost_estimate=cost(0, 0),
        name="tie",
    )(a, *after)


def add(*terms):
    total = terms[0].astype(F32)
    for t in terms[1:]:
        total = total + t.astype(F32)
    return total


def ring_terms(own, d, e, f, axis, after=None):
    r1 = turn(f, axis, 1)
    r2 = turn(d if after is None else tie(d, after), axis, -1)
    e = add(e, r1).astype(BF16)
    r3 = turn(e, axis, 1)
    return (own, r2, r3), e


def direct_terms(own, d, e, f, axis):
    return own, turn(d, axis, -1), turn(e, axis, 1), far(f, axis)


def body(vectors, centroids, candidates):
    core, x, y, z = (lax.axis_index(a) for a in ("core", "x", "y", "z"))
    step = 1 - 2 * core

    def around(i):
        return jnp.stack([i, (i - step) % 4, (i + step) % 4, (i + 2) % 4]).astype(jnp.int32)

    xs, zs = around(x), around(z)
    other_zs = jnp.stack([zs[0], zs[2], zs[1], zs[3]])

    where = jnp.concatenate([xs, zs])
    v = pack(vectors, candidates.T)
    a, b = turn(v, "y", 1), turn(v, "y", -1)
    c0 = lax.dynamic_slice_in_dim(centroids, core * 1024, 1024, 0)
    c1, c2 = turn(c0, "x", 1), turn(c0, "x", -1)
    mine = lax.dynamic_slice_in_dim(c0.reshape(2, BS, D), z * 128, 128, 1)
    blk = ((y * 4 + xs) * 4 + 2 * core)[:, None] + jnp.arange(2, dtype=jnp.int32)[None, :]
    blk = jnp.broadcast_to(blk.reshape(NBLK, 1), (NBLK, 128)).astype(F32)

    rank0, rows = dispatch(0, (v, swap(v)), blk, None)
    a = tie(a, rank0, b, c1, c2)
    c = turn(a, "y", 1)
    c3 = turn(c1, "x", 1)
    rank1, rows = dispatch(2, (a, b), blk, rows)
    rows, rank2, e, peak0, lse0 = middle((swap(a), swap(b)), blk, (c0, c1, c2), rows)
    ranked = (rank0, rank1, rank2)
    idx0 = indices(ranked, [(s, s, 0, MOST) for s in range(5)] + [(5, 5, 0, 32)])
    c = tie(c, idx0, c3)
    rank3, rows = dispatch(6, (c,), blk, rows)
    rows, e, rank4, peak, stat = late_scores(
        swap(c), blk, (c0, c1, c2, c3), (*ranked, rank3), peak0, lse0, rows, e
    )
    idx = (idx0, indices((rank2, rank3, rank4), [(5, 1, 32, MOST), (6, 2, 0, MOST), (7, 3, 0, MOST)]))

    theirs = swap(stat)
    theirs = jnp.concatenate([theirs[s : s + 1] for s in SWAPPED])
    m = jnp.maximum(stat, theirs)
    merged = m + jnp.log(jnp.exp(stat - m) + jnp.exp(theirs - m))
    stats = (merged, turn(merged, "y", 1), turn(merged, "y", -1), far(merged, "y"))

    g, h3, factor = first_sums(where, stats, idx, peak, e, rows)
    h1, h2, h0 = owner_sums((1, 2, 0), factor, e, rows)
    h, _ = ring_terms(h0, h1, h2, h3, "x", h2)
    g, _ = ring_terms(*g, "z", h0)
    h = direct_terms(*parted(0, where, h), "z")
    g = direct_terms(*parted(1, where, g), "x")
    fresh = final(h, g, mine)

    others = [turn(fresh, "z", 1), turn(fresh, "z", -1), far(fresh, "z")]
    parts = [fresh, *others] + [swap(p) for p in (fresh, *others)]
    places = jnp.concatenate([zs, other_zs, jnp.stack([core, 1 - core])]).astype(jnp.int32)
    return place(places, parts).reshape(2048, D)


def solution(mesh):
    fine = Mesh(np.asarray(mesh.devices).reshape(4, 2, 4, 4), ("z", "core", "y", "x"))
    return jax.shard_map(
        body,
        mesh=fine,
        in_specs=(P(("z", "core", "y", "x"), None), P(("y", "x"), None), P(("z", "core", "y", "x"), None)),
        out_specs=P(("y", "x"), None),
        check_vma=False,
    )
```
